32 devices in a mesh: clip: 8 (over z, y), chan: 4 (over x, core).
Axes of the slice: x: 2, y: 2, z: 4, core: 2. Of those that a mesh axis runs over, the one named last changes fastest.
Arguments:
- frames_in: bfloat16 [16, 16, 49, 2048], P('clip', None, None, 'chan'), may hold values from -15 to 15
- seg_counts: int32 [16], replicated, may hold values from 8 to 16, as said below
- w_reduce: bfloat16 [2048, 512], P(None, 'chan'), may hold values from -0.125 to 0.125
- gain_one: float32 [512], P('chan'), may hold values from 0.5 to 1.5
- shift_one: float32 [512], P('chan'), may hold values from -3 to 3
- w_spatial: bfloat16 [9, 512, 512], P(None, None, 'chan'), may hold values from -0.09375 to 0.09375
- gain_two: float32 [512], P('chan'), may hold values from 0.5 to 1.5
- shift_two: float32 [512], P('chan'), may hold values from -3 to 3
- near_kern: float32 [9, 512], P(None, 'chan'), may hold values from -2 to 2
- far_kern: float32 [9, 512], P(None, 'chan'), may hold values from -2 to 2
- w_expand: bfloat16 [512, 2048], P(None, 'chan'), may hold values from -0.25 to 0.25
- gain_three: float32 [2048], P('chan'), may hold values from 0.5 to 1.5
- shift_three: float32 [2048], P('chan'), may hold values from -3 to 3
- w_classes: bfloat16 [2048, 174], P('chan'), may hold values from -0.125 to 0.125
- class_bias: float32 [174], replicated, may hold values from -3 to 3
- out_grad: bfloat16 [16, 16, 49, 2048], P('clip', None, None, 'chan'), may hold values from -6 to 6
- logit_grad: bfloat16 [16, 174], P('clip'), may hold values from -6 to 6
Outputs:
- output: bfloat16 [16, 16, 49, 2048], P('clip', None, None, 'chan')
- logits: float32 [16, 174], P('clip')
- grad_frames: float32 [16, 16, 49, 2048], P('clip', None, None, 'chan')
- grad_w_reduce: float32 [2048, 512], P(None, 'chan')
- grad_gain_one: float32 [512], P('chan')
- grad_shift_one: float32 [512], P('chan')
- grad_w_spatial: float32 [9, 512, 512], P(None, None, 'chan')
- grad_gain_two: float32 [512], P('chan')
- grad_shift_two: float32 [512], P('chan')
- grad_near: float32 [9, 512], P(None, 'chan')
- grad_far: float32 [9, 512], P(None, 'chan')
- grad_w_expand: float32 [512, 2048], P(None, 'chan')
- grad_gain_three: float32 [2048], P('chan')
- grad_shift_three: float32 [2048], P('chan')
- grad_w_classes: float32 [2048, 174], P('chan')
- grad_class_bias: float32 [174], replicated
The draws below stay inside these ranges and needn't reach their ends.
Inputs may be any that keep to these rules, and one draw needn't show every extreme that they name: Each clip's valid segments are the first seg_counts of its 16 slots, either 8 or 16; clip 0 has 16 and clip 1 has 8.
All inputs are finite; a program needn't handle non-finite values.
Results may differ from the reference program's by a relative error of at most 0.024.
Values may be sent and summed in bfloat16 or wider, within the bound.
No kernel may reach another device: no remote copies, remote signals or barrier semaphores. Data moves between devices by JAX's collectives and lax.ppermute only.
A program may use at most 192 MiB of HBM per device.

```python
import jax
import jax.numpy as jnp
from jax import lax

C = 2048
M = 512
K = 174
S = 16
SIDE = 7
P_SIZE = 49
B = 16


def draw_frames_in(key, part):
    key = jax.random.fold_in(key, 11)
    key_base, key_clip, key_chan = jax.random.split(key, 3)
    clip_scale = jnp.exp(jax.random.uniform(key_clip, (B, 1, 1, 1), jnp.float32, -0.8, 0.8))
    chan_scale = jnp.exp(jax.random.uniform(key_chan, (1, 1, 1, C), jnp.float32, -0.5, 0.5))
    base_draw = jnp.clip(jax.random.normal(key_base, (B, S, P_SIZE, C), jnp.float32), -4.0, 4.0)
    return (base_draw * clip_scale * chan_scale).astype(jnp.bfloat16)


def draw_seg_counts(key, part):
    key = jax.random.fold_in(key, 23)
    coin_flips = jax.random.randint(key, (B,), 0, 2) * 8 + 8
    position = jnp.arange(B)
    return jnp.where(position == 0, 16, jnp.where(position == 1, 8, coin_flips)).astype(jnp.int32)


def shard_levels(key, shape, cuts, smallest, largest):
    loudness = 1.0
    for dim, parts in cuts:
        steps = jax.random.uniform(jax.random.fold_in(jax.random.fold_in(key, 6), dim), (parts,), jnp.float32, smallest / len(cuts), largest / len(cuts))
        loudness = loudness * jnp.repeat(jnp.exp(steps), shape[dim] // parts).reshape((-1,) + (1,) * (len(shape) - 1 - dim))
    return loudness


def noise(rng, extent, deviation, limit, cuts=(), kind=jnp.bfloat16):
    entries = jax.random.normal(rng, extent, jnp.float32) * deviation
    if len(cuts) > 0:
        entries = shard_levels(rng, extent, cuts, -0.22, 0.18) * entries
    return jnp.clip(entries, min=-limit, max=limit).astype(kind)


def setup_inputs(seed: int = 0) -> dict:
    seeds = jax.random.split(jax.random.key(seed), 18)
    return {
        "frames_in": draw_frames_in(jax.random.fold_in(seeds[17], 71), 0),
        "seg_counts": draw_seg_counts(jax.random.fold_in(seeds[17], 71), 0),
        "w_reduce": noise(seeds[2], (C, M), C ** -0.5, 0.125, ((1, 4),)),
        "gain_one": jnp.clip(1.0 + 0.1 * jax.random.normal(seeds[3], (M,), jnp.float32), 0.5, 1.5),
        "shift_one": noise(seeds[4], (M,), 0.5, 3.0, ((0, 4),), jnp.float32),
        "w_spatial": noise(seeds[5], (9, M, M), (9 * M) ** -0.5, 0.09375, ((2, 4),)),
        "gain_two": jnp.clip(1.0 + 0.1 * jax.random.normal(seeds[6], (M,), jnp.float32), 0.5, 1.5),
        "shift_two": noise(seeds[7], (M,), 0.5, 3.0, ((0, 4),), jnp.float32),
        "near_kern": noise(seeds[8], (9, M), 9 ** -0.5, 2.0, ((1, 4),), jnp.float32),
        "far_kern": noise(seeds[9], (9, M), 9 ** -0.5, 2.0, ((1, 4),), jnp.float32),
        "w_expand": noise(seeds[10], (M, C), M ** -0.5, 0.25, ((1, 4),)),
        "gain_three": jnp.clip(1.0 + 0.1 * jax.random.normal(seeds[11], (C,), jnp.float32), 0.5, 1.5),
        "shift_three": noise(seeds[12], (C,), 0.5, 3.0, ((0, 4),), jnp.float32),
        "w_classes": noise(seeds[13], (C, K), C ** -0.5, 0.125, ((0, 4),)),
        "class_bias": noise(seeds[14], (K,), 0.5, 3.0, (), jnp.float32),
        "out_grad": noise(seeds[15], (B, S, P_SIZE, C), 1.0, 6.0, ((0, 8), (3, 4))),
        "logit_grad": noise(seeds[16], (B, K), 1.0, 6.0, ((0, 8),)),
    }


EPSILON = 1e-05

@jax.custom_vjp
def low(v):
    return lax.optimization_barrier(v.astype(jnp.bfloat16)).astype(jnp.float32)

@jax.custom_vjp
def low_back(v):
    return v

def low_keep(v):
    return (low(v), None)

def low_pass(kept, grad):
    return (grad,)

def back_keep(v):
    return (v, None)

def back_low(kept, grad):
    return (low(grad),)
low.defvjp(low_keep, low_pass)
low_back.defvjp(back_keep, back_low)

def matmul_hi(left, right):
    return jnp.dot(left, right, precision=lax.Precision.HIGHEST, preferred_element_type=jnp.float32)

def shifted_columns(frames, dilate, frame_side):
    padded = jnp.pad(frames, ((0, 0), (dilate, dilate), (dilate, dilate), (0, 0)))
    pieces = [padded[:, row_off * dilate:row_off * dilate + frame_side, col_off * dilate:col_off * dilate + frame_side, :] for row_off in range(3) for col_off in range(3)]
    return jnp.stack(pieces, axis=3)

def temporal_gate(features, seg_mask, near_kern, far_kern):
    clip_count, seg_count, pixel_count, chan_count = features.shape
    following = jnp.concatenate([features[:, 1:], jnp.zeros_like(features[:, :1])], axis=1)
    next_valid = jnp.concatenate([seg_mask[:, 1:], jnp.zeros_like(seg_mask[:, :1])], axis=1)
    differ = next_valid[:, :, None, None] * (following - features)
    frames = differ.reshape(clip_count * seg_count, SIDE, SIDE, chan_count)
    near_sum = lax.optimization_barrier(jnp.sum(shifted_columns(frames, 1, SIDE) * near_kern[None, None, None], axis=3))
    far_sum = lax.optimization_barrier(jnp.sum(shifted_columns(frames, 2, SIDE) * far_kern[None, None, None], axis=3))
    gate_value = jax.nn.sigmoid(near_sum + far_sum).reshape(features.shape)
    return features * (1.0 + gate_value)

def batch_norm(activation, mask_rows, gain_vec, shift_vec, valid_total):
    average = lax.optimization_barrier(jnp.sum(activation * mask_rows, axis=0)) / valid_total
    spread = lax.optimization_barrier(jnp.sum(activation * activation * mask_rows, axis=0)) / valid_total - average * average
    return gain_vec * (activation - average) * lax.rsqrt(spread + EPSILON) + shift_vec

def forward(frames_f, w_reduce, gain_one, shift_one, w_spatial, gain_two, shift_two, near_kern, far_kern, w_expand, gain_three, shift_three, w_classes, class_bias, seg_mask, count_scale):
    clip_count, seg_count, pixel_count, chan_count = frames_f.shape
    row_count = clip_count * seg_count * pixel_count
    mid_width = w_reduce.shape[1]
    mask_rows = jnp.broadcast_to(seg_mask[:, :, None], (clip_count, seg_count, pixel_count)).reshape(row_count, 1)
    valid_total = jnp.sum(seg_mask) * pixel_count
    x_rows = frames_f.reshape(row_count, chan_count)
    act_one = low_back(matmul_hi(x_rows, w_reduce))
    hid_one = low(jax.nn.silu(batch_norm(act_one, mask_rows, gain_one, shift_one, valid_total)))
    columns = shifted_columns(hid_one.reshape(clip_count * seg_count, SIDE, SIDE, mid_width), 1, SIDE).reshape(row_count, 9 * mid_width)
    act_two = low_back(matmul_hi(columns, w_spatial.reshape(9 * mid_width, mid_width)))
    hid_two = jax.nn.silu(batch_norm(act_two, mask_rows, gain_two, shift_two, valid_total))
    gated = temporal_gate(hid_two.reshape(clip_count, seg_count, pixel_count, mid_width), seg_mask, near_kern, far_kern).reshape(row_count, mid_width)
    act_three = low_back(matmul_hi(low(gated), w_expand))
    output = mask_rows * jax.nn.silu(x_rows + batch_norm(act_three, mask_rows, gain_three, shift_three, valid_total))
    pooled = low(lax.optimization_barrier(jnp.sum(output.reshape(clip_count, seg_count * pixel_count, chan_count), axis=1)) * count_scale)
    logits = matmul_hi(pooled, w_classes) + class_bias
    return (output.reshape(frames_f.shape), logits)

def reference(frames_in, seg_counts, w_reduce, gain_one, shift_one, w_spatial, gain_two, shift_two, near_kern, far_kern, w_expand, gain_three, shift_three, w_classes, class_bias, out_grad, logit_grad):
    seg_mask = (jnp.arange(S)[None, :] < seg_counts[:, None]).astype(jnp.float32)
    count_scale = (1.0 / (seg_counts.astype(jnp.float32) * P_SIZE))[:, None]
    params = (frames_in.astype(jnp.float32), w_reduce.astype(jnp.float32), gain_one, shift_one, w_spatial.astype(jnp.float32), gain_two, shift_two, near_kern, far_kern, w_expand.astype(jnp.float32), gain_three, shift_three, w_classes.astype(jnp.float32), class_bias)

    def closed(*inputs):
        return forward(*inputs, seg_mask, count_scale)
    (output, logits), pullback = jax.vjp(closed, *params)
    gradients = pullback((out_grad.astype(jnp.float32), logit_grad.astype(jnp.float32)))
    return (output.astype(jnp.bfloat16), logits, gradients[0], gradients[1], gradients[2], gradients[3], gradients[4], gradients[5], gradients[6], gradients[7], gradients[8], gradients[9], gradients[10], gradients[11], gradients[12], gradients[13])
```

```python
import functools

import jax
import jax.numpy as jnp
from jax import lax
from jax.experimental import pallas as pl
from jax.experimental.pallas import tpu as pltpu
from jax.sharding import PartitionSpec as P

SIDE = 7
WIDE = SIDE + 1
EDGE = SIDE + 4
EPSILON = 1e-05
LANES = 128
F32 = jnp.float32
BF16 = jnp.bfloat16
VMEM_BYTES = 20 * 1024 * 1024


def silu_slope(pre_act):
    logistic = jax.nn.sigmoid(pre_act)
    return logistic * (1.0 + pre_act * (1.0 - logistic))


def seg_index(row_count, seg_count):
    return lax.broadcasted_iota(jnp.int32, (row_count, 1), 0) % seg_count


def dot32(left, right, dims=((1,), (0,))):
    return lax.dot_general(left, right, (dims, ((), ())), preferred_element_type=F32)


class Pick:
    def __init__(self, array, index):
        self.array = array
        self.index = index


class Free:
    def __init__(self, array):
        self.array = array


class Near:
    def __init__(self, array):
        self.array = array


class Arriving:
    def __init__(self, copy, ref):
        self.copy = copy
        self.ref = ref
        self.shape = ref.shape

    def __getitem__(self, index):
        if self.copy is not None:
            self.copy.wait()
            self.copy = None
        return self.ref[index]


def near(shape, kind):
    return pltpu.VMEM(shape, kind)


def call(body, out_shape, scratch=(), deps=(), ints=None, floats=None):
    single = not isinstance(out_shape, (tuple, list))
    shapes = (out_shape,) if single else tuple(out_shape)
    away = [isinstance(out, jax.ShapeDtypeStruct) for out in shapes]
    outs = tuple(pltpu.HBM(out.shape, out.dtype) if far else out for out, far in zip(shapes, away))
    scalars = [array for array in (ints, floats) if array is not None]

    def bare(arg):
        while isinstance(arg, (Pick, Free, Near)):
            arg = arg.array
        return arg

    def placed(arg):
        inner = arg.array if isinstance(arg, Pick) else arg
        if isinstance(inner, Free):
            return inner.array
        if isinstance(inner, Near):
            return pltpu.with_memory_space_constraint(inner.array, pltpu.VMEM)
        return pltpu.with_memory_space_constraint(inner, pltpu.HBM)

    def run(*args):
        fetched = [isinstance(arg, Pick) and not isinstance(arg.array, Near) for arg in args]
        buffers = [pltpu.VMEM(arg.array.shape[1:], arg.array.dtype) for arg, own in zip(args, fetched) if own]
        if buffers:
            buffers.append(pltpu.SemaphoreType.DMA((len(buffers),)))

        def kernel(*refs):
            first = refs[: len(scalars)]
            inputs = refs[len(scalars) : len(scalars) + len(args)]
            rest = refs[len(scalars) + len(args) + len(deps) :]
            results, local = rest[: len(outs)], rest[len(outs) : len(outs) + len(buffers)]
            rest = rest[len(outs) + len(buffers) :]
            passed = []
            for arg, ref, own in zip(args, inputs, fetched):
                if isinstance(arg, Pick):
                    ref = ref.at[arg.index if isinstance(arg.index, int) else arg.index(first[0])]
                if own:
                    place = sum(isinstance(each, Arriving) for each in passed)
                    copy = pltpu.make_async_copy(ref, local[place], local[-1].at[place])
                    copy.start()
                    ref = Arriving(copy, local[place])
                passed.append(ref)
            body(*first, *passed, *results, *rest)

        kernel.__name__ = getattr(body, "func", body).__name__
        anywhere = pl.BlockSpec(memory_space=pl.ANY)
        results = pl.pallas_call(
            kernel,
            out_shape=outs,
            in_specs=[SMEM] * len(scalars)
            + [anywhere if own else VMEM for own in fetched]
            + [anywhere] * len(deps),
            out_specs=[VMEM] * len(outs),
            scratch_shapes=buffers + list(scratch),
            compiler_params=pltpu.CompilerParams(vmem_limit_bytes=VMEM_BYTES),
        )(*scalars, *[placed(arg) for arg in args], *[bare(dep) for dep in deps])
        results = tuple(result if far else Near(result) for result, far in zip(results, away))
        return results[0] if single else results

    return run


SMEM = pl.BlockSpec(memory_space=pltpu.SMEM)
VMEM = pl.BlockSpec(memory_space=pltpu.VMEM)


def store_taps(cat_ref, line, values, line_rows, seg_count):
    depth = values.shape[1]
    for tap in range(3):
        start = ((line + 1) * WIDE + 1 - tap) * seg_count
        cat_ref[start : start + line_rows, tap * depth : (tap + 1) * depth] = values


def line_sums(values, row_of):
    return jnp.sum(values.reshape(-1, 8, values.shape[1]), axis=0) + row_of


def send_sums(sent_ref, total, cross):
    sums = jnp.concatenate([jnp.sum(total, axis=0, keepdims=True), jnp.sum(cross, axis=0, keepdims=True)], axis=0)
    if len(sent_ref.shape) == 2:
        sent_ref[0:2, :] = sums
        return
    for peer in range(sent_ref.shape[0]):
        sent_ref[peer, 0:2, :] = sums


def side_sums(got_ref, side):
    total = jnp.zeros((2, got_ref.shape[3]), F32)
    for clip in range(got_ref.shape[0]):
        for core in range(2):
            total += got_ref[clip, side * 2 + core, 0:2, :]
    return total


def norm_rows(sums, gain_vec, shift_vec, count):
    average = sums[0:1, :] / count
    inv_std = lax.rsqrt(sums[1:2, :] / count - average * average + EPSILON)
    return average, gain_vec * inv_std, shift_vec, inv_std


def line_mask(line_rows, seg_count, count):
    return (seg_index(line_rows, seg_count) < count).astype(F32)


def split_blocks(ints_ref, w_ref, *refs):
    size = refs[0].shape[0]
    for bits, ref in enumerate(refs):
        start = (ints_ref[0] ^ bits) * size
        ref[...] = w_ref[pl.ds(pl.multiple_of(start, size), size), :]


def reduce_other(ints_ref, own_ref, near_ref, far_ref, cross_ref, x_ref, part_ref, w_ref):
    core = ints_ref[3]
    size = own_ref.shape[1]
    for place, (first, second) in enumerate(((own_ref, near_ref), (far_ref, cross_ref))):
        for index, ref in ((core, first), (1 - core, second)):
            start = pl.multiple_of((2 * place + index) * size, size)
            w_ref[:, pl.ds(start, size)] = ref[...]
    part_ref[...] = dot32(x_ref[...], w_ref[...]).astype(BF16)


def add_low(near_ref, far_ref, out_ref):
    half = out_ref.shape[1]
    out_ref[...] = (far_ref[...] + near_ref[:, half:].astype(F32)).astype(BF16)


def pack_small(gain_one_ref, shift_one_ref, gain_two_ref, shift_two_ref, near_ref, far_ref, out_ref):
    out_ref[...] = jnp.zeros_like(out_ref)
    for row, ref in enumerate((gain_one_ref, shift_one_ref, gain_two_ref, shift_two_ref)):
        out_ref[row : row + 1, :] = ref[...]
    out_ref[4:13, :] = near_ref[...]
    out_ref[13:22, :] = far_ref[...]


def join_small(ints_ref, own_ref, near_ref, far_ref, cross_ref, out_ref):
    chan = 2 * ints_ref[1] + ints_ref[3]
    for bits, ref in enumerate((own_ref, near_ref, far_ref, cross_ref)):
        out_ref[chan ^ bits] = ref[...]


def small_row(small_ref, side, row):
    return jnp.concatenate([small_ref[2 * side + core, row : row + 1, :] for core in range(2)], axis=1)


def reduce_own(ints_ref, near_ref, w_ref, x_ref, part_ref, send_ref):
    half = w_ref.shape[1] // 2
    send = dot32(x_ref[...], w_ref[:, half:]) + near_ref[:, half:].astype(F32)
    send_ref[...] = send.astype(BF16)
    part_ref[...] = dot32(x_ref[...], w_ref[:, :half]) + near_ref[:, :half].astype(F32)


def first_sums(seg_count, ints_ref, part_ref, far_ref, act_ref, low_ref, sent_ref):
    line_rows = SIDE * seg_count
    mask = line_mask(line_rows, seg_count, ints_ref[0])
    total = cross = jnp.zeros((8, act_ref.shape[1]), F32)
    for line in range(SIDE):
        rows = slice(line * line_rows, (line + 1) * line_rows)
        act = part_ref[rows, :] + far_ref[rows, :].astype(F32)
        act_ref[rows, :] = act
        low_ref[rows, :] = act.astype(BF16)
        kept = act * mask
        total = line_sums(kept, total)
        cross = line_sums(kept * act, cross)
    send_sums(sent_ref, total, cross)


def conv_forward(
    seg_count, ints_ref, floats_ref, own_ref, oth_ref, got_ref, small_ref, w_ref,
    act_ref, low_ref, sent_ref, hid_ref, cat_ref, acc_ref,
):
    line_rows = SIDE * seg_count
    half = own_ref.shape[1]
    side = ints_ref[1]
    cat_ref[...] = jnp.zeros_like(cat_ref)
    own, oth = [
        norm_rows(side_sums(got_ref, index), small_row(small_ref, index, 0), small_row(small_ref, index, 1), floats_ref[0])
        for index in (side, 1 - side)
    ]
    average, scale, shift, _ = [jnp.concatenate(pieces, axis=1) for pieces in zip(own, oth)]
    for line in range(SIDE):
        rows = slice(line * line_rows, (line + 1) * line_rows)
        act = jnp.concatenate([own_ref[rows, :], oth_ref[rows, :].astype(F32)], axis=1)
        pre = (act - average) * scale + shift
        hid = (pre * jax.nn.sigmoid(pre)).astype(BF16)
        hid_ref[rows, :] = hid
        store_taps(cat_ref, line, hid, line_rows, seg_count)
    span = SIDE * WIDE * seg_count
    step = WIDE * seg_count
    for row_off in range(3):
        part = dot32(cat_ref[row_off * step : row_off * step + span, :], w_ref[row_off])
        if row_off == 0:
            acc_ref[...] = part
        else:
            acc_ref[...] += part
    mask = line_mask(line_rows, seg_count, ints_ref[0])
    total = cross = jnp.zeros((8, half), F32)
    for line in range(SIDE):
        rows = slice(line * line_rows, (line + 1) * line_rows)
        act = acc_ref[line * step : line * step + line_rows, :]
        act_ref[rows, :] = act
        low_ref[rows, :] = act.astype(BF16)
        kept = act * mask
        total = line_sums(kept, total)
        cross = line_sums(kept * act, cross)
    send_sums(sent_ref, total, cross)


def store_frames(pad_ref, line, values, line_rows, seg_count):
    start = ((line + 2) * EDGE + 2) * seg_count
    pad_ref[start : start + line_rows, :] = values


def load_frames(pad_ref, line, row_off, col_off, line_rows, seg_count):
    start = ((line + 2 + row_off) * EDGE + 2 + col_off) * seg_count
    return pad_ref[start : start + line_rows, :]


def tap_offsets():
    for index in range(9):
        yield index, index // 3 - 1, index % 3 - 1
    for index in range(9):
        yield 9 + index, 2 * (index // 3 - 1), 2 * (index % 3 - 1)


def next_mask(line_rows, seg_count, count):
    seg = seg_index(line_rows, seg_count)
    return (seg + 1 < jnp.minimum(count, seg_count)).astype(F32)


def gate_forward(
    seg_count, other, ints_ref, floats_ref, act_ref, got_ref, small_ref, gated_ref, *rest,
):
    hid_ref, gate_ref = (None, None) if other else rest[:2]
    roll_ref, pad_ref = rest[-2:]
    line_rows = SIDE * seg_count
    pad_ref[...] = jnp.zeros_like(pad_ref)
    roll_ref[...] = jnp.zeros_like(roll_ref)
    side = 1 - ints_ref[1] if other else ints_ref[1]
    sums = side_sums(got_ref, side)
    follows = next_mask(line_rows, seg_count, ints_ref[0])
    for core in range(act_ref.shape[1] // LANES):
        lanes = slice(core * LANES, (core + 1) * LANES)
        rows_for = small_ref.at[2 * side + core]
        average, scale, shift, _ = norm_rows(sums[:, lanes], rows_for[2:3, :], rows_for[3:4, :], floats_ref[0])
        for line in range(SIDE):
            rows = slice(line * line_rows, (line + 1) * line_rows)
            act = act_ref[rows, lanes].astype(F32)
            pre = (act - average) * scale + shift
            roll_ref[rows, :] = pre * jax.nn.sigmoid(pre)
        for line in range(SIDE):
            first = line * line_rows
            here = roll_ref[first : first + line_rows, :]
            after = roll_ref[first + 1 : first + 1 + line_rows, :]
            store_frames(pad_ref, line, follows * (after - here), line_rows, seg_count)
        for line in range(SIDE):
            rows = slice(line * line_rows, (line + 1) * line_rows)
            total = jnp.zeros((line_rows, LANES), F32)
            for index, row_off, col_off in tap_offsets():
                kern = rows_for[4 + index : 5 + index, :]
                total += load_frames(pad_ref, line, row_off, col_off, line_rows, seg_count) * kern
            gate = jax.nn.sigmoid(total)
            hid = roll_ref[rows, :]
            gated_ref[rows, lanes] = (hid * (1.0 + gate)).astype(BF16)
            if not other:
                hid_ref[rows, lanes] = hid
                gate_ref[rows, lanes] = gate


def expand(
    seg_count, ints_ref, own_ref, oth_ref, near_own_ref, near_oth_ref, w_ref, bias_ref, act_ref, sent_ref,
):
    half = own_ref.shape[1]
    row_count = own_ref.shape[0]
    line_rows = SIDE * seg_count
    side = ints_ref[1]
    w_own = w_ref[pl.ds(pl.multiple_of(side * half, half), half), :]
    w_oth = w_ref[pl.ds(pl.multiple_of((1 - side) * half, half), half), :]
    total = cross = jnp.zeros((8, w_ref.shape[1]), F32)
    for clip, (left, right) in enumerate(((own_ref, oth_ref), (near_own_ref, near_oth_ref))):
        act_ref[clip] = dot32(left[...], w_own) + dot32(right[...], w_oth)
        mask = line_mask(line_rows, seg_count, ints_ref[2 * clip])
        for line in range(SIDE):
            act = act_ref[clip, line * line_rows : (line + 1) * line_rows, :]
            kept = act * mask
            total = line_sums(kept, total)
            cross = line_sums(kept * act, cross)
    send_sums(sent_ref, total, cross)
    sent_ref[2:3, :] = bias_ref[...]


def finish(
    seg_count, ints_ref, floats_ref, got_ref, gain_ref, shift_ref, flat_ref, act_own_ref, x_own_ref, grad_own_ref,
    act_oth_ref, x_oth_ref, grad_oth_ref, out_ref, resid_ref, pooled_ref, sent_ref,
):
    line_rows = SIDE * seg_count
    width = act_own_ref.shape[1]
    average, _, shift, inv_std = norm_rows(got_ref, gain_ref[...], shift_ref[...], floats_ref[0])
    gain = gain_ref[...]
    total = cross = jnp.zeros((8, width), F32)
    own, oth = (act_own_ref, x_own_ref, grad_own_ref), (act_oth_ref, x_oth_ref, grad_oth_ref)
    for clip, (act_ref, x_ref, grad_ref) in enumerate((own, oth)):
        place = ints_ref[3] if clip == 0 else 1 - ints_ref[3]
        mask = line_mask(line_rows, seg_count, ints_ref[2 * clip])
        flat = flat_ref[clip : clip + 1, :]
        pool = jnp.zeros((8, width), F32)
        for line in range(SIDE):
            rows = slice(line * line_rows, (line + 1) * line_rows)
            normed = (act_ref[rows, :] - average) * inv_std
            resid = x_ref[rows, :].astype(F32) + gain * normed + shift
            logistic = jax.nn.sigmoid(resid)
            output = mask * resid * logistic
            out_ref[place, rows, :] = output.astype(BF16)
            pool = line_sums(output, pool)
            grad = (grad_ref[rows, :].astype(F32) + flat) * mask
            grad = grad * (logistic * (1.0 + resid * (1.0 - logistic)))
            resid_ref[clip, rows, :] = grad
            total = line_sums(grad, total)
            cross = line_sums(grad * normed, cross)
        pooled_ref[clip : clip + 1, :] = jnp.sum(pool, axis=0, keepdims=True) * floats_ref[1 + clip]
    send_sums(sent_ref, total, cross)


def expand_backward(
    seg_count, clip, ints_ref, floats_ref, got_ref, back_ref, gain_ref, resid_ref, act_ref, w_ref,
    low_ref, *part_refs,
):
    line_rows = SIDE * seg_count
    half = w_ref.shape[0] // 2
    side = ints_ref[1]
    average, scale, _, inv_std = norm_rows(got_ref, gain_ref[...], gain_ref[...], floats_ref[0])
    back = back_ref[0:2, :] / floats_ref[0]
    mask = line_mask(line_rows, seg_count, ints_ref[2 * clip])
    for line in range(SIDE):
        rows = slice(line * line_rows, (line + 1) * line_rows)
        normed = (act_ref[rows, :] - average) * inv_std
        grad = scale * (resid_ref[rows, :] - mask * (back[0:1, :] + normed * back[1:2, :]))
        low_ref[rows, :] = grad.astype(BF16)
    for place, index in enumerate((side, 1 - side)):
        w_side = w_ref[pl.ds(pl.multiple_of(index * half, half), half), :]
        part = dot32(low_ref[...], w_side, ((1,), (1,)))
        if clip == 0:
            part_refs[place][...] = part
        else:
            part_refs[0][:, place * half : (place + 1) * half] = part.astype(BF16)


def gate_backward(
    seg_count, ints_ref, floats_ref, grad_ref, near_ref, far_ref, hid_ref, gate_ref, act_ref, got_ref, small_ref,
    logit_ref, slope_ref, low_ref, sent_ref, kern_grad_ref, field_ref, pad_ref, back_ref,
):
    line_rows = SIDE * seg_count
    pad_ref[...] = jnp.zeros_like(pad_ref)
    field_ref[...] = jnp.zeros_like(field_ref)
    back_ref[...] = jnp.zeros_like(back_ref)
    kern_grad_ref[...] = jnp.zeros_like(kern_grad_ref)
    side = ints_ref[1]
    sums = side_sums(got_ref, side)
    follows = next_mask(line_rows, seg_count, ints_ref[0])
    totals_all, cross_all = [], []
    for core in range(act_ref.shape[1] // LANES):
        lanes = slice(core * LANES, (core + 1) * LANES)
        rows_for = small_ref.at[2 * side + core]
        average, scale, shift, inv_std = norm_rows(sums[:, lanes], rows_for[2:3, :], rows_for[3:4, :], floats_ref[0])

        def whole_grad(rows):
            return grad_ref[rows, lanes] + near_ref[rows, lanes].astype(F32) + far_ref[rows, lanes].astype(F32)

        for line in range(SIDE):
            first = line * line_rows
            rows = slice(first, first + line_rows)
            here = hid_ref[rows, lanes]
            if line < SIDE - 1:
                after = hid_ref[first + 1 : first + 1 + line_rows, lanes]
            else:
                after = jnp.concatenate([hid_ref[first + 1 : first + line_rows, lanes], here[:1, :]], axis=0)
            store_frames(pad_ref, line, follows * (after - here), line_rows, seg_count)
            gate = gate_ref[rows, lanes]
            store_frames(field_ref, line, whole_grad(rows) * here * gate * (1.0 - gate), line_rows, seg_count)
        totals = [jnp.zeros((8, LANES), F32) for _ in range(18)]
        for line in range(SIDE):
            field = load_frames(field_ref, line, 0, 0, line_rows, seg_count)
            back = jnp.zeros((line_rows, LANES), F32)
            for index, row_off, col_off in tap_offsets():
                shifted = load_frames(pad_ref, line, row_off, col_off, line_rows, seg_count)
                totals[index] = line_sums(field * shifted, totals[index])
                kern = rows_for[4 + index : 5 + index, :]
                back += load_frames(field_ref, line, -row_off, -col_off, line_rows, seg_count) * kern
            start = 8 + line * line_rows
            back_ref[start : start + line_rows, :] = follows * back
        kern_grad_ref[0:18, lanes] = jnp.concatenate(
            [jnp.sum(each, axis=0, keepdims=True) for each in totals], axis=0
        )
        total = cross = jnp.zeros((8, LANES), F32)
        for line in range(SIDE):
            first = line * line_rows
            rows = slice(first, first + line_rows)
            before = back_ref[first + 7 : first + 7 + line_rows, :]
            here = back_ref[first + 8 : first + 8 + line_rows, :]
            grad = whole_grad(rows) * (1.0 + gate_ref[rows, lanes]) + before - here
            centred = act_ref[rows, lanes] - average
            grad = grad * silu_slope(centred * scale + shift)
            slope_ref[rows, lanes] = grad
            low_ref[rows, lanes] = grad.astype(BF16)
            total = line_sums(grad, total)
            cross = line_sums(grad * (centred * inv_std), cross)
        totals_all.append(total)
        cross_all.append(cross)
    send_sums(sent_ref, jnp.concatenate(totals_all, axis=1), jnp.concatenate(cross_all, axis=1))
    for peer in range(sent_ref.shape[0]):
        sent_ref[peer, 2:4, :] = logit_ref[...]


def back_rows(got_ref, back_ref, small_ref, row, side, count):
    average, scale, shift, inv_std = norm_rows(
        side_sums(got_ref, side), small_row(small_ref, side, row), small_row(small_ref, side, row + 1), count
    )
    back = side_sums(back_ref, side) / count
    return average, inv_std, scale, back[0:1, :], back[1:2, :], shift


def conv_backward(
    seg_count, ints_ref, floats_ref, grad_ref, more_ref, act_ref, oth_ref, got_ref, back_ref, first_ref, got_one_ref,
    small_ref, w_ref, from_ref, pair_ref, slope_ref, low_ref, sent_ref, field_ref, cat_ref, acc_ref, w_all_ref,
):
    line_rows = SIDE * seg_count
    half = grad_ref.shape[1]
    step = WIDE * seg_count
    span = SIDE * step
    side = ints_ref[1]
    count = floats_ref[0]
    mask = line_mask(line_rows, seg_count, ints_ref[0])
    cat_ref[...] = jnp.zeros_like(cat_ref)
    field_ref[...] = jnp.zeros_like(field_ref)
    own = back_rows(got_ref, back_ref, small_ref, 2, side, count)
    oth = back_rows(got_ref, back_ref, small_ref, 2, 1 - side, count)
    average, inv_std, scale, mean, mix, _ = [jnp.concatenate(pieces, axis=1) for pieces in zip(own, oth)]
    for line in range(SIDE):
        rows = slice(line * line_rows, (line + 1) * line_rows)
        act = jnp.concatenate([act_ref[rows, :], oth_ref[rows, :].astype(F32)], axis=1)
        grad = jnp.concatenate([grad_ref[rows, :], more_ref[rows, :].astype(F32)], axis=1)
        normed = (act - average) * inv_std
        low = (scale * (grad - mask * (mean + normed * mix))).astype(BF16)
        store_taps(cat_ref, line, low, line_rows, seg_count)
        field_ref[line * step : line * step + line_rows, :] = low[:, :half]
    core = ints_ref[3]
    size = half // 2
    depth = 2 * half
    for tap in range(9):
        w_all_ref[tap, :, :half] = w_ref[tap // 3, (tap % 3) * depth : (tap % 3) * depth + half, :]
        for index, ref in ((core, from_ref), (1 - core, pair_ref)):
            w_all_ref[tap, :, pl.ds(pl.multiple_of(half + index * size, size), size)] = ref[tap]
    for row_off in range(3):
        rows = slice(row_off * step, row_off * step + span)
        part = sum(
            dot32(cat_ref[rows, tap * depth : (tap + 1) * depth], w_all_ref[8 - 3 * row_off - tap], ((1,), (1,)))
            for tap in range(3)
        )
        if row_off == 0:
            acc_ref[...] = part
        else:
            acc_ref[...] += part
    average, scale, shift, inv_std = norm_rows(
        side_sums(got_one_ref, side), small_row(small_ref, side, 0), small_row(small_ref, side, 1), count
    )
    total = cross = jnp.zeros((8, half), F32)
    for line in range(SIDE):
        rows = slice(line * line_rows, (line + 1) * line_rows)
        centred = first_ref[rows, :] - average
        grad = acc_ref[line * step : line * step + line_rows, :]
        grad = grad * silu_slope(centred * scale + shift)
        slope_ref[rows, :] = grad
        low_ref[rows, :] = grad.astype(BF16)
        total = line_sums(grad, total)
        cross = line_sums(grad * (centred * inv_std), cross)
    send_sums(sent_ref, total, cross)


def split_rows(rows_ref, index, keep_ref, send_ref):
    size = keep_ref.shape[0]
    keep_ref[...] = rows_ref[pl.ds(pl.multiple_of(index * size, 16), size), :]
    send_ref[...] = rows_ref[pl.ds(pl.multiple_of((1 - index) * size, 16), size), :]


def taps_gradient(seg_count, ints_ref, hid_ref, field_ref, kern_grad_ref, keep_ref, send_ref, taps_ref):
    line_rows = SIDE * seg_count
    taps_ref[...] = jnp.zeros_like(taps_ref)
    for line in range(SIDE):
        rows = slice(line * line_rows, (line + 1) * line_rows)
        store_taps(taps_ref, line, hid_ref[rows, :], line_rows, seg_count)
    step = WIDE * seg_count
    span = SIDE * step
    depth = taps_ref.shape[1] // 3
    lanes_of = [pl.ds(pl.multiple_of(index * LANES, LANES), LANES) for index in (ints_ref[3], 1 - ints_ref[3])]
    fields = jnp.concatenate([field_ref[:, lanes] for lanes in lanes_of], axis=1)
    for tap in range(9):
        start = (tap // 3) * step
        left = taps_ref[start : start + span, (tap % 3) * depth : (tap % 3 + 1) * depth]
        part = dot32(left, fields, ((0,), (0,))).astype(BF16)
        for place, ref in enumerate((keep_ref, send_ref)):
            ref[tap * depth : (tap + 1) * depth, :] = part[:, place * LANES : (place + 1) * LANES]
    rest = keep_ref.shape[0] - 9 * depth
    count = kern_grad_ref.shape[0]
    for lanes, ref in zip(lanes_of, (keep_ref, send_ref)):
        ref[9 * depth : 9 * depth + count, :] = kern_grad_ref[:, lanes].astype(BF16)
        ref[9 * depth + count :, :] = jnp.zeros((rest - count, LANES), BF16)


def sum_into(sum_ref, *refs):
    total = refs[0][...].astype(F32)
    for ref in refs[1:]:
        total += ref[...].astype(F32)
    sum_ref[...] = total.astype(sum_ref.dtype)


def store_blocks(ints_ref, rows_ref, refs):
    size = refs[0].shape[0]
    for bits, ref in enumerate(refs):
        start = pl.multiple_of((ints_ref[5] ^ bits) * size, 8)
        ref[...] = rows_ref[pl.ds(start, size), :].astype(ref.dtype)


def join_blocks(ints_ref, refs, out_ref):
    size = refs[0].shape[0]
    for bits, ref in enumerate(refs):
        start = pl.multiple_of((ints_ref[5] ^ bits) * size, 8)
        out_ref[pl.ds(start, size), :] = ref[...]


def sum_split(ints_ref, own_ref, got_ref, keep_ref, send_ref, sum_ref):
    sum_into(sum_ref, own_ref, got_ref)
    split_rows(sum_ref, ints_ref[4], keep_ref, send_ref)


def sum_blocks(ints_ref, own_ref, got_ref, *refs):
    sum_into(refs[-1], own_ref, got_ref)
    store_blocks(ints_ref, refs[-1], refs[:-1])


def sum_parts(*refs):
    sum_into(refs[-1], *refs[:-1])


def join_pair(ints_ref, own_ref, got_ref, out_ref):
    size = own_ref.shape[0]
    for index, ref in ((ints_ref[4], own_ref), (1 - ints_ref[4], got_ref)):
        out_ref[pl.ds(pl.multiple_of(index * size, 16), size), :] = ref[...]


def stage_one(places, ints_ref, pack_ref, pack_got_ref, reduce_ref, *refs):
    wide, refs = refs[:places], refs[places:]
    blocks, (keep_ref, send_ref, join_ref, sum_ref) = refs[:places], refs[places:]
    sum_into(sum_ref, pack_ref, pack_got_ref)
    store_blocks(ints_ref, sum_ref, blocks)
    split_rows(reduce_ref, ints_ref[4], keep_ref, send_ref)
    join_blocks(ints_ref, wide, join_ref)


def stage_two(places, ints_ref, keep_ref, got_ref, *refs):
    pack, (part_ref, *blocks, sum_ref) = refs[:places], refs[places:]
    sum_into(part_ref, *pack)
    sum_into(sum_ref, keep_ref, got_ref)
    store_blocks(ints_ref, sum_ref, blocks)


def stage_three(places, ints_ref, *refs):
    pack, reduce, (join_ref, columns_ref) = refs[:places], refs[places : 2 * places], refs[2 * places :]
    join_blocks(ints_ref, pack, join_ref)
    total = reduce[0][...].astype(F32)
    for ref in reduce[1:]:
        total += ref[...].astype(F32)
    total = total.astype(BF16)
    size = columns_ref.shape[2]
    for place, side in enumerate((ints_ref[1], 1 - ints_ref[1])):
        for core in range(2):
            start = (2 * place + core) * size
            for clip in range(columns_ref.shape[0] // 4):
                columns_ref[clip * 4 + 2 * side + core] = total[:, start : start + size]


def unpack_spatial(ints_ref, own_ref, got_ref, out_ref, near_ref, far_ref, rows_ref):
    join_pair(ints_ref, own_ref, got_ref, rows_ref)
    depth = out_ref.shape[1]
    half = depth // 2
    side = ints_ref[1]
    for tap in range(9):
        for place, index in enumerate((side, 1 - side)):
            start = tap * depth + place * half
            target = pl.ds(pl.multiple_of(index * half, half), half)
            out_ref[tap, target, :] = rows_ref[start : start + half, :].astype(F32)
    rest = rows_ref[9 * depth : 9 * depth + 32, :].astype(F32)
    near_ref[...] = rest[0:9, :]
    far_ref[...] = rest[9:18, :]


def unpack_wide(ints_ref, own_ref, got_ref, out_ref, classes_ref, rows_ref):
    join_pair(ints_ref, own_ref, got_ref, rows_ref)
    half = out_ref.shape[0] // 2
    for place, index in enumerate((ints_ref[1], 1 - ints_ref[1])):
        target = pl.ds(pl.multiple_of(index * half, half), half)
        out_ref[target, :] = rows_ref[place * half : (place + 1) * half, :].astype(F32)
    classes_ref[...] = rows_ref[2 * half :, :].astype(F32)


def last_norm(
    seg_count, ints_ref, floats_ref, grad_ref, more_ref, act_ref, oth_ref, got_ref, back_ref, small_ref, low_ref,
):
    line_rows = SIDE * seg_count
    side = ints_ref[1]
    mask = line_mask(line_rows, seg_count, ints_ref[0])
    half = grad_ref.shape[1]
    for place, (grads, acts) in enumerate(((grad_ref, act_ref), (more_ref, oth_ref))):
        index = side if place == 0 else 1 - side
        average, inv_std, scale, mean, mix, _ = back_rows(
            got_ref, back_ref, small_ref, 0, index, floats_ref[0]
        )
        for line in range(SIDE):
            rows = slice(line * line_rows, (line + 1) * line_rows)
            normed = (acts[rows, :].astype(F32) - average) * inv_std
            grad = scale * (grads[rows, :].astype(F32) - mask * (mean + normed * mix))
            low_ref[rows, place * half : (place + 1) * half] = grad.astype(BF16)


def pick_rows(ints_ref, w_ref, out_ref):
    size = out_ref.shape[1]
    out_ref[...] = w_ref[:, pl.ds(pl.multiple_of((1 - ints_ref[1]) * size, size), size), :]


def expand_gradient(
    ints_ref, own_ref, oth_ref, near_own_ref, near_oth_ref, low_ref, near_low_ref, classes_ref,
    keep_ref, send_ref, out_ref,
):
    half = own_ref.shape[1]
    for place, (first, second) in enumerate(((own_ref, near_own_ref), (oth_ref, near_oth_ref))):
        part = dot32(first[...], low_ref[...], ((0,), (0,))) + dot32(second[...], near_low_ref[...], ((0,), (0,)))
        out_ref[place * half : (place + 1) * half, :] = part.astype(BF16)
    rest = out_ref.shape[0] - 2 * half
    out_ref[2 * half :, :] = jnp.zeros((rest, out_ref.shape[1]), BF16)
    count = classes_ref.shape[0]
    out_ref[2 * half : 2 * half + count, :] = classes_ref[...].astype(BF16)
    split_rows(out_ref, ints_ref[4], keep_ref, send_ref)


def reduce_gradient(ints_ref, x_own_ref, low_ref, x_oth_ref, near_ref, out_ref):
    part = dot32(x_own_ref[...], low_ref[...], ((0,), (0,)))
    out_ref[...] = (part + dot32(x_oth_ref[...], near_ref[...], ((0,), (0,)))).astype(BF16)


def input_gradient(ints_ref, low_ref, w_ref, resid_ref, near_ref, out_ref):
    core = ints_ref[3]
    out_ref[core] = resid_ref[0] + dot32(low_ref[...], w_ref[...], ((1,), (1,)))
    out_ref[1 - core] = resid_ref[1] + dot32(near_ref[...], w_ref[...], ((1,), (1,)))


def per_device(
    clip_size,
    chan_size,
    frames_in,
    seg_counts,
    w_reduce,
    gain_one,
    shift_one,
    w_spatial,
    gain_two,
    shift_two,
    near_kern,
    far_kern,
    w_expand,
    gain_three,
    shift_three,
    w_classes,
    class_bias,
    out_grad,
    logit_grad,
):
    clip_count, seg_count, pixel_count, chan_local = frames_in.shape
    mid_local = w_reduce.shape[1]
    mid_width = w_spatial.shape[1]
    half = mid_width // 2
    row_count = seg_count * pixel_count
    class_count = w_classes.shape[1]
    chan_index = lax.axis_index("chan")
    clip_index = lax.axis_index("clip")
    side_index = chan_index // 2
    core_index = chan_index % 2
    everyone = clip_size * chan_size
    sds = jax.ShapeDtypeStruct

    def swap(array, bits):
        array = array.array if isinstance(array, Near) else array
        return lax.ppermute(array, "chan", [(i, i ^ bits) for i in range(chan_size)])

    def own_first(array, index, size, axis):
        own = lax.dynamic_slice_in_dim(array, index * size, size, axis)
        oth = lax.dynamic_slice_in_dim(array, (1 - index) * size, size, axis)
        return own, oth

    def pair(own, oth):
        flip = core_index == 1
        return jnp.where(flip, oth, own), jnp.where(flip, own, oth)

    def swap_clip(array, bits):
        array = array.array if isinstance(array, Near) else array
        return lax.ppermute(array, "clip", [(i, i ^ bits) for i in range(clip_size)])

    parity, place = clip_index % 2, clip_index // 2
    places = clip_size // 2
    groups = [list(range(first, clip_size, 2)) for first in range(2)]

    def sum_places(values):
        if places > 4:
            return lax.psum(values, "clip", axis_index_groups=groups)
        return sum([values] + [swap_clip(values, 2 * bits) for bits in range(1, places)])

    def share_all(sent):
        got = lax.all_to_all(sent, ("clip", "chan"), 0, 0)
        return got.reshape((clip_size, chan_size) + sent.shape[1:])

    def share_clip(sent):
        sent = sent.array
        return sum_places(sent + swap_clip(sent, 1))

    own_counts = lax.dynamic_slice_in_dim(seg_counts, clip_index * clip_count, clip_count)
    count_pair = jnp.concatenate(own_first(own_counts, core_index, 1, 0))
    valid_total = jnp.sum(seg_counts).astype(F32) * pixel_count
    count_scale = 1.0 / (count_pair.astype(F32) * pixel_count)
    ints = jnp.stack([count_pair[0], side_index, count_pair[1], core_index, parity, place])
    floats = jnp.concatenate([valid_total[None], count_scale])

    x_all = frames_in.transpose(0, 2, 1, 3).reshape(clip_count, row_count, chan_local)
    grad_all = out_grad.transpose(0, 2, 1, 3).reshape(clip_count, row_count, chan_local)
    x_own, x_oth = Pick(x_all, lambda ints: ints[3]), Pick(x_all, lambda ints: 1 - ints[3])
    grad_own, grad_oth = Pick(grad_all, lambda ints: ints[3]), Pick(grad_all, lambda ints: 1 - ints[3])
    half_f32, near_f32 = sds((row_count, half), F32), near((row_count, half), F32)
    half_low, near_low_half = sds((row_count, half), BF16), near((row_count, half), BF16)
    sums_shape = sds((everyone, 2, half), F32)
    pad_rows = 9 * WIDE * seg_count
    span = SIDE * WIDE * seg_count
    edge_rows = EDGE * EDGE * seg_count

    block_shape = sds((chan_local, mid_local), BF16)
    chan = chan_index.astype(jnp.int32)[None]
    sent_blocks = call(split_blocks, (block_shape,) * chan_size, ints=chan)(w_reduce)
    got_blocks = {bits: swap(sent_blocks[bits], bits) for bits in (2, 3, 1)}

    small_own = call(pack_small, sds((24, mid_local), F32))(
        gain_one[None], shift_one[None], gain_two[None], shift_two[None], near_kern, far_kern
    )
    small = call(join_small, sds((chan_size, 24, mid_local), F32), ints=ints)(
        small_own, *[swap(small_own, bits) for bits in (1, 2, 3)]
    )

    part_oth, w_rows = call(
        reduce_other,
        (near((row_count, mid_width), BF16), sds((chan_local, mid_width), BF16)),
        deps=(small,),
        ints=ints,
    )(sent_blocks[0], got_blocks[1], got_blocks[2], got_blocks[3], x_oth)
    near_one = swap(part_oth, 1)
    part_own, far_send = call(
        reduce_own,
        (near((row_count, half), F32), near((row_count, half), BF16)),
        ints=ints,
    )(near_one, w_rows, x_own)
    far_one = swap(far_send, 2)

    w_pair = jnp.concatenate(pair(w_spatial, swap(w_spatial, 1)), axis=2)
    w_fwd_own, w_fwd_oth = own_first(w_pair, side_index, half, 1)
    w_fwd = jnp.concatenate([w_fwd_own, w_fwd_oth], axis=1).reshape(3, 3 * mid_width, half)

    act_one, act_one_low, sent_one = call(
        functools.partial(first_sums, seg_count), (half_f32, half_low, sums_shape), deps=(w_fwd,), ints=ints,
    )(part_own, far_one)
    act_one_oth = swap(act_one_low, 2)
    got_one = share_all(sent_one)

    act_two, act_two_low, sent_two, hid_one = call(
        functools.partial(conv_forward, seg_count),
        (half_f32, half_low, sums_shape, sds((row_count, mid_width), BF16)),
        [pltpu.VMEM((pad_rows, 3 * mid_width), BF16), pltpu.VMEM((span, half), F32)],
        ints=ints,
        floats=floats,
    )(act_one, act_one_oth, got_one, small, w_fwd)
    act_two_oth = swap(act_two_low, 2)
    got_two = share_all(sent_two)

    def gate_call(act, other):
        return call(
            functools.partial(gate_forward, seg_count, other),
            (near_low_half,) if other else (near_low_half, near_f32, near_f32),
            [pltpu.VMEM((row_count + 8, LANES), F32), pltpu.VMEM((edge_rows, LANES), F32)],
            ints=ints,
            floats=floats,
        )(act, got_two, small)

    gated_own, hid_two, gate = gate_call(act_two, False)
    near_own = swap(gated_own, 1)
    gated_oth = gate_call(act_two_oth, True)[0]
    near_oth = swap(gated_oth, 1)

    bias_row = jnp.sum(logit_grad.astype(F32), axis=0)
    bias_row = jnp.pad(bias_row, (0, chan_local - class_count))[None]
    act_three, sent_three = call(
        functools.partial(expand, seg_count),
        (near((2, row_count, chan_local), F32), near((3, chan_local), F32)),
        ints=ints,
    )(gated_own, gated_oth, near_own, near_oth, w_expand, bias_row)
    got_three = share_clip(sent_three)

    to_side = call(pick_rows, sds((9, half, mid_local), BF16), deps=(sent_three,), ints=ints)(Free(w_spatial))
    from_side = swap(to_side, 2)
    from_pair = swap(from_side, 1)


    logit_pair = jnp.concatenate(own_first(logit_grad, core_index, 1, 0))
    grad_pooled = dot32(logit_pair, w_classes, ((1,), (1,))) * count_scale[:, None]
    output, grad_resid, pooled, sent_back = call(
        functools.partial(finish, seg_count),
        (
            sds((2, row_count, chan_local), BF16),
            near((2, row_count, chan_local), F32),
            near((2, chan_local), F32),
            near((2, chan_local), F32),
        ),
        ints=ints,
        floats=floats,
    )(
        got_three, gain_three[None], shift_three[None], grad_pooled,
        Pick(act_three, 0), x_own, grad_own, Pick(act_three, 1), x_oth, grad_oth,
    )
    got_back = share_clip(sent_back)
    pooled = pooled.array.astype(BF16)

    def back_call(clip):
        outs = [near((row_count, chan_local), BF16)]
        if clip == 0:
            outs += [near((row_count, half), F32)] * 2
        else:
            outs += [near((row_count, mid_width), BF16)]
        return call(
            functools.partial(expand_backward, seg_count, clip), tuple(outs), deps=(from_side,), ints=ints, floats=floats,
        )(got_three, got_back, gain_three[None], Pick(grad_resid, clip), Pick(act_three, clip), w_expand)

    low_three_oth, back_oth = back_call(1)
    near_back = swap(back_oth, 1)
    low_three_own, back_own, back_far = back_call(0)

    unit = 16 * clip_size
    def halves(rows, width):
        return (sds((rows // 2, width), BF16),) * 2

    def to_places(blocks):
        if places > 4:
            order = place ^ jnp.arange(places)
            sent = jnp.stack(blocks)[order]
            return list(lax.all_to_all(sent, "clip", 0, 0, axis_index_groups=groups)[order])
        return [blocks[0]] + [swap_clip(blocks[bits], 2 * bits) for bits in range(1, places)]

    def blocks_of(rows, width):
        return (sds((rows // places, width), BF16),) * places

    grad_classes = dot32(logit_pair, pooled, ((0,), (0,)))
    wide_rows = -(-(mid_width + class_count) // unit) * unit
    wide_keep, wide_send = call(
        expand_gradient, halves(wide_rows, chan_local), [pltpu.VMEM((wide_rows, chan_local), BF16)], ints=ints,
    )(gated_own, gated_oth, near_own, near_oth, low_three_own, low_three_oth, grad_classes)

    far_back = swap(call(add_low, near_low_half, deps=())(near_back, back_far), 2)
    wide_blocks = call(
        sum_blocks,
        blocks_of(wide_rows // 2, chan_local),
        [pltpu.VMEM((wide_rows // 2, chan_local), BF16)],
        ints=ints,
    )(wide_keep, swap_clip(wide_send, 1))
    wide_got = to_places(wide_blocks)

    logits_part = jnp.concatenate(own_first(dot32(pooled, w_classes), core_index, 1, 0))
    logits_wide = jnp.pad(logits_part, ((0, 0), (0, half - class_count)))
    slope_two, slope_two_low, sent_back_two, kern_grad = call(
        functools.partial(gate_backward, seg_count),
        (half_f32, half_low, sds((everyone, 4, half), F32), sds((32, half), F32)),
        [
            pltpu.VMEM((edge_rows, LANES), F32),
            pltpu.VMEM((edge_rows, LANES), F32),
            pltpu.VMEM((row_count + 8, LANES), F32),
        ],
        deps=(wide_send,),
        ints=ints,
        floats=floats,
    )(back_own, near_back, far_back, hid_two, gate, act_two, got_two, small, logits_wide)
    slope_two_oth = swap(slope_two_low, 2)
    got_back_two = share_all(sent_back_two)
    slope_one, slope_one_low, sent_back_one, field_two = call(
        functools.partial(conv_backward, seg_count),
        (half_f32, half_low, sums_shape, sds((span, half), BF16)),
        [
            pltpu.VMEM((pad_rows, 3 * mid_width), BF16),
            pltpu.VMEM((span, half), F32),
            pltpu.VMEM((9, half, mid_width), BF16),
        ],
        deps=(wide_blocks[0],),
        ints=ints,
        floats=floats,
    )(
        slope_two, slope_two_oth, act_two, act_two_oth, got_two, got_back_two, act_one, got_one, small, w_fwd,
        from_side, from_pair,
    )
    slope_one_oth = swap(slope_one_low, 2)
    got_back_one = share_all(sent_back_one)

    pack_rows = -(-(9 * mid_width + 32) // unit) * unit
    pack_own, pack_send = call(
        functools.partial(taps_gradient, seg_count),
        (sds((pack_rows, mid_local), BF16),) * 2,
        [pltpu.VMEM((pad_rows, 3 * mid_width), BF16)],
        ints=ints,
    )(hid_one, field_two, kern_grad)
    pack_keep, pack_pair = call(
        sum_split, halves(pack_rows, mid_local), [pltpu.VMEM((pack_rows, mid_local), BF16)], ints=ints,
    )(pack_own, swap(pack_send, 1))
    wide_part = call(sum_parts, sds((wide_rows // clip_size, chan_local), BF16))(*wide_got)

    low_one = call(
        functools.partial(last_norm, seg_count),
        sds((row_count, mid_width), BF16),
        deps=(pack_pair, wide_part),
        ints=ints,
        floats=floats,
    )(slope_one, slope_one_oth, act_one, act_one_oth, got_one, got_back_one, small)
    near_low = swap(low_one, 1)
    reduce_all = call(reduce_gradient, sds((chan_local, mid_width), BF16), ints=ints)(
        x_own, low_one, x_oth, near_low
    )

    share = chan_local // clip_size
    stage = call(
        functools.partial(stage_one, places),
        blocks_of(pack_rows // 2, mid_local) + halves(chan_local, mid_width) + (sds((wide_rows // 2, chan_local), BF16),),
        [pltpu.VMEM((pack_rows // 2, mid_local), BF16)],
        ints=ints,
    )(pack_keep, swap_clip(pack_pair, 1), reduce_all, *to_places([wide_part] * places))
    pack_blocks, (reduce_keep, reduce_send, wide_join) = stage[:places], stage[places:]
    grad_frames = call(
        input_gradient, sds((2, row_count, chan_local), F32), deps=(pack_blocks[0],), ints=ints,
    )(low_one, w_rows, grad_resid, near_low)
    wide_other = swap_clip(wide_join, 1)
    pack_part, *reduce_blocks = call(
        functools.partial(stage_two, places),
        (sds((pack_rows // clip_size, mid_local), BF16),) + blocks_of(chan_local // 2, mid_width),
        [pltpu.VMEM((chan_local // 2, mid_width), F32)],
        deps=(grad_frames, wide_other),
        ints=ints,
    )(reduce_keep, swap_clip(reduce_send, 1), *to_places(pack_blocks))
    grad_w_expand, classes_got = call(
        unpack_wide,
        (sds((mid_width, chan_local), F32), sds((wide_rows - mid_width, chan_local), F32)),
        [pltpu.VMEM((wide_rows, chan_local), BF16)],
        deps=(pack_part,),
        ints=ints,
    )(wide_join, wide_other)
    grad_w_classes = classes_got[:class_count].T
    pack_join, columns = call(
        functools.partial(stage_three, places),
        (sds((pack_rows // 2, mid_local), BF16), sds((everyone, share, mid_local), BF16)),
        deps=(grad_w_expand,),
        ints=ints,
    )(*to_places([pack_part] * places), *to_places(reduce_blocks))
    reduce_got = lax.all_to_all(columns, ("clip", "chan"), 0, 0)
    reduce_got = reduce_got.reshape(places, 2, chan_size, share, mid_local).transpose(2, 1, 0, 3, 4)
    grad_w_reduce = reduce_got.reshape(chan_size * chan_local, mid_local).astype(F32)
    grad_spatial, grad_near, grad_far = call(
        unpack_spatial,
        (sds((9, mid_width, mid_local), F32),) + (sds((9, mid_local), F32),) * 2,
        [pltpu.VMEM((pack_rows, mid_local), BF16)],
        ints=ints,
    )(pack_join, swap_clip(pack_join, 1))

    mine = lax.dynamic_index_in_dim(got_back_two, clip_index, 0, keepdims=False)
    logits = jnp.sum(mine, axis=0)[2:, :class_count] + class_bias

    def own_sums(got):
        sums = jnp.sum(got.reshape((clip_size, 2, 2) + got.shape[2:]), axis=(0, 2))
        sums = lax.dynamic_index_in_dim(sums, side_index, 0, keepdims=False)
        return lax.dynamic_slice_in_dim(sums[:2], core_index * mid_local, mid_local, 1)

    grads_one = own_sums(got_back_one)
    grads_two = own_sums(got_back_two)
    grads_three = got_back
    grad_bias = got_three[2, :class_count]

    def whole(array):
        return array.reshape(2, pixel_count, seg_count, chan_local).transpose(0, 2, 1, 3)

    return (
        whole(output),
        logits,
        whole(grad_frames),
        grad_w_reduce,
        grads_one[1],
        grads_one[0],
        grad_spatial,
        grads_two[1],
        grads_two[0],
        grad_near,
        grad_far,
        grad_w_expand,
        grads_three[1],
        grads_three[0],
        grad_w_classes,
        grad_bias,
    )


def solution(mesh):
    in_specs = (
        P("clip", None, None, "chan"),
        P(),
        P(None, "chan"),
        P("chan"),
        P("chan"),
        P(None, None, "chan"),
        P("chan"),
        P("chan"),
        P(None, "chan"),
        P(None, "chan"),
        P(None, "chan"),
        P("chan"),
        P("chan"),
        P("chan", None),
        P(),
        P("clip", None, None, "chan"),
        P("clip", None),
    )
    out_specs = (
        P("clip", None, None, "chan"),
        P("clip", None),
        P("clip", None, None, "chan"),
        P(None, "chan"),
        P("chan"),
        P("chan"),
        P(None, None, "chan"),
        P("chan"),
        P("chan"),
        P(None, "chan"),
        P(None, "chan"),
        P(None, "chan"),
        P("chan"),
        P("chan"),
        P("chan", None),
        P(),
    )
    body = functools.partial(per_device, mesh.shape["clip"], mesh.shape["chan"])
    return jax.shard_map(
        body, mesh=mesh, in_specs=in_specs, out_specs=out_specs, check_vma=False
    )
```

```python
import functools

import jax
import jax.numpy as jnp
from jax import lax
from jax.experimental import pallas as pl
from jax.experimental.pallas import tpu as pltpu
from jax.sharding import PartitionSpec as P

SIDE = 7
WIDE = SIDE + 1
EDGE = SIDE + 4
EPSILON = 1e-05
LANES = 128
F32 = jnp.float32
BF16 = jnp.bfloat16
VMEM_BYTES = 20 * 1024 * 1024


def silu_slope(pre_act):
    logistic = jax.nn.sigmoid(pre_act)
    return logistic * (1.0 + pre_act * (1.0 - logistic))


def seg_index(row_count, seg_count):
    return lax.broadcasted_iota(jnp.int32, (row_count, 1), 0) % seg_count


def dot32(left, right, dims=((1,), (0,))):
    return lax.dot_general(left, right, (dims, ((), ())), preferred_element_type=F32)


class Pick:
    def __init__(self, array, index):
        self.array = array
        self.index = index


class Free:
    def __init__(self, array):
        self.array = array


class Late:
    def __init__(self, array):
        self.array = array


class Early:
    def __init__(self, shape, dtype, parts):
        self.shape = shape
        self.dtype = dtype
        self.parts = parts


class Leaving:
    def __init__(self, target, ref, sems):
        self.target = target
        self.ref = ref
        self.sems = sems
        self.copies = []
        self.shape = ref.shape
        self.dtype = ref.dtype

    def __getitem__(self, index):
        return self.ref[index]

    def __setitem__(self, index, value):
        self.ref[index] = value

    def leave(self, source, target):
        copy = pltpu.make_async_copy(self.ref.at[source], self.target.at[target], self.sems.at[len(self.copies)])
        copy.start()
        self.copies.append(copy)


class Near:
    def __init__(self, array):
        self.array = array


class Loose:
    def __init__(self, shape, dtype):
        self.shape = shape
        self.dtype = dtype


class Arriving:
    def __init__(self, copy, ref):
        self.copy = copy
        self.ref = ref
        self.shape = ref.shape

    def __getitem__(self, index):
        if self.copy is not None:
            self.copy.wait()
            self.copy = None
        return self.ref[index]


def near(shape, kind):
    return pltpu.VMEM(shape, kind)


def call(body, out_shape, scratch=(), deps=(), ints=None, floats=None, work=0, room=VMEM_BYTES):
    single = not isinstance(out_shape, (tuple, list))
    shapes = (out_shape,) if single else tuple(out_shape)
    early = [isinstance(out, Early) for out in shapes]
    away = [isinstance(out, (jax.ShapeDtypeStruct, Early)) for out in shapes]
    loose = [isinstance(out, Loose) for out in shapes]
    outs = tuple(
        pltpu.HBM(out.shape, out.dtype) if far else jax.ShapeDtypeStruct(out.shape, out.dtype) if free else out
        for out, far, free in zip(shapes, away, loose)
    )
    scalars = [array for array in (ints, floats) if array is not None]

    def bare(arg):
        while isinstance(arg, (Pick, Free, Near, Late)):
            arg = arg.array
        return arg

    def placed(arg):
        inner = arg.array if isinstance(arg, (Pick, Late)) else arg
        if isinstance(inner, Free):
            return inner.array
        if isinstance(inner, Near):
            return pltpu.with_memory_space_constraint(inner.array, pltpu.VMEM)
        return pltpu.with_memory_space_constraint(inner, pltpu.HBM)

    def run(*args):
        fetched = [
            isinstance(arg, Late) or isinstance(arg, Pick) and not isinstance(arg.array, Near) for arg in args
        ]
        buffers = [
            pltpu.VMEM(arg.array.shape[1 if isinstance(arg, Pick) else 0 :], arg.array.dtype)
            for arg, own in zip(args, fetched)
            if own
        ]
        count = len(buffers)
        for out, parts in zip(shapes, early):
            if parts:
                buffers += [pltpu.VMEM(out.shape, out.dtype), pltpu.SemaphoreType.DMA((out.parts,))]
        if count:
            buffers.append(pltpu.SemaphoreType.DMA((count,)))

        def kernel(*refs):
            first = refs[: len(scalars)]
            inputs = refs[len(scalars) : len(scalars) + len(args)]
            rest = refs[len(scalars) + len(args) + len(deps) :]
            results, local = rest[: len(outs)], rest[len(outs) : len(outs) + len(buffers)]
            rest = rest[len(outs) + len(buffers) :]
            passed = []
            for arg, ref, own in zip(args, inputs, fetched):
                if isinstance(arg, Pick):
                    ref = ref.at[arg.index if isinstance(arg.index, int) else arg.index(first[0])]
                if own:
                    place = sum(isinstance(each, Arriving) for each in passed)
                    copy = pltpu.make_async_copy(ref, local[place], local[-1].at[place])
                    copy.start()
                    ref = Arriving(copy, local[place])
                passed.append(ref)
            leaving, done = [], count
            for result, parts in zip(results, early):
                if parts:
                    result = Leaving(result, local[done], local[done + 1])
                    done += 2
                leaving.append(result)
            body(*first, *passed, *leaving, *rest)
            for result in leaving:
                if isinstance(result, Leaving):
                    for copy in result.copies:
                        copy.wait()

        kernel.__name__ = getattr(body, "func", body).__name__
        anywhere = pl.BlockSpec(memory_space=pl.ANY)
        results = pl.pallas_call(
            kernel,
            out_shape=outs,
            in_specs=[SMEM] * len(scalars)
            + [anywhere if own else VMEM for own in fetched]
            + [anywhere] * len(deps),
            out_specs=[anywhere if parts else VMEM for parts in early],
            scratch_shapes=buffers + list(scratch),
            compiler_params=pltpu.CompilerParams(vmem_limit_bytes=room),
            cost_estimate=pl.CostEstimate(flops=work, bytes_accessed=0, transcendentals=0) if work else None,
        )(*scalars, *[placed(arg) for arg in args], *[placed(dep) for dep in deps])
        results = tuple(
            result if far else Free(result) if free else Near(result)
            for result, far, free in zip(results, away, loose)
        )
        return results[0] if single else results

    return run


SMEM = pl.BlockSpec(memory_space=pltpu.SMEM)
VMEM = pl.BlockSpec(memory_space=pltpu.VMEM)


def store_taps(cat_ref, line, values, line_rows, seg_count):
    depth = values.shape[1]
    for tap in range(3):
        start = ((line + 1) * WIDE + 1 - tap) * seg_count
        cat_ref[start : start + line_rows, tap * depth : (tap + 1) * depth] = values


def line_sums(values, row_of):
    return jnp.sum(values.reshape(-1, 8, values.shape[1]), axis=0) + row_of


def send_sums(sent_ref, total, cross):
    sums = jnp.concatenate([jnp.sum(total, axis=0, keepdims=True), jnp.sum(cross, axis=0, keepdims=True)], axis=0)
    if len(sent_ref.shape) == 2:
        sent_ref[0:2, :] = sums
        return
    for peer in range(sent_ref.shape[0]):
        sent_ref[peer, 0:2, :] = sums


def side_sums(got_ref, side):
    total = jnp.zeros((2, got_ref.shape[3]), F32)
    for clip in range(got_ref.shape[0]):
        for core in range(2):
            total += got_ref[clip, side * 2 + core, 0:2, :]
    return total


def norm_rows(sums, gain_vec, shift_vec, count):
    average = sums[0:1, :] / count
    inv_std = lax.rsqrt(sums[1:2, :] / count - average * average + EPSILON)
    return average, gain_vec * inv_std, shift_vec, inv_std


def line_mask(line_rows, seg_count, count):
    return (seg_index(line_rows, seg_count) < count).astype(F32)


def split_blocks(
    ints_ref, w_ref, gain_one_ref, shift_one_ref, gain_two_ref, shift_two_ref, near_ref, far_ref, *refs
):
    size = refs[0].shape[0] - 96
    small = jnp.concatenate(
        [ref[...] for ref in (gain_one_ref, shift_one_ref, gain_two_ref, shift_two_ref, near_ref, far_ref)]
        + [jnp.zeros((10, refs[0].shape[1]), F32)],
        axis=0,
    )
    pieces = []
    for _ in range(3):
        piece = small.astype(BF16)
        pieces.append(piece)
        small = small - piece.astype(F32)
    for bits, ref in enumerate(refs):
        start = (ints_ref[0] ^ bits) * size
        ref[:size, :] = w_ref[pl.ds(pl.multiple_of(start, size), size), :]
        for index, piece in enumerate(pieces):
            ref[size + 32 * index : size + 32 * (index + 1), :] = piece


def reduce_other(ints_ref, own_ref, near_ref, far_ref, cross_ref, x_ref, part_ref, w_ref, small_ref):
    core = ints_ref[3]
    rows, size = w_ref.shape[0], own_ref.shape[1]
    blocks = (own_ref, near_ref, far_ref, cross_ref)
    for bits, ref in enumerate(blocks):
        start = pl.multiple_of((2 * (bits // 2) + (core ^ (bits % 2))) * size, size)
        w_ref[:, pl.ds(start, size)] = ref[:rows, :]
    for bits, ref in enumerate(blocks):
        pieces = [ref[rows + 32 * index : rows + 32 * (index + 1), :].astype(F32) for index in range(3)]
        small_ref[(2 * ints_ref[1] + core) ^ bits] = (pieces[0] + (pieces[1] + pieces[2]))[:24]
    part_ref[...] = dot32(x_ref[...], w_ref[...]).astype(BF16)


def add_low(near_ref, far_ref, out_ref):
    half = out_ref.shape[1]
    out_ref[...] = (far_ref[...] + near_ref[:, half:].astype(F32)).astype(BF16)


def small_row(small_ref, side, row):
    return jnp.concatenate([small_ref[2 * side + core, row : row + 1, :] for core in range(2)], axis=1)


def reduce_own(ints_ref, near_ref, w_ref, x_ref, part_ref, send_ref):
    half = w_ref.shape[1] // 2
    send = dot32(x_ref[...], w_ref[:, half:]) + near_ref[:, half:].astype(F32)
    send_ref[...] = send.astype(BF16)
    part_ref[...] = dot32(x_ref[...], w_ref[:, :half]) + near_ref[:, :half].astype(F32)


def first_sums(seg_count, ints_ref, part_ref, far_ref, act_ref, low_ref, sent_ref):
    line_rows = SIDE * seg_count
    mask = line_mask(line_rows, seg_count, ints_ref[0])
    total = cross = jnp.zeros((8, act_ref.shape[1]), F32)
    for line in range(SIDE):
        rows = slice(line * line_rows, (line + 1) * line_rows)
        act = part_ref[rows, :] + far_ref[rows, :].astype(F32)
        act_ref[rows, :] = act
        low_ref[rows, :] = act.astype(BF16)
        kept = act * mask
        total = line_sums(kept, total)
        cross = line_sums(kept * act, cross)
    send_sums(sent_ref, total, cross)


def conv_forward(
    seg_count, ints_ref, floats_ref, own_ref, oth_ref, got_ref, small_ref, w_ref,
    act_ref, low_ref, sent_ref, hid_ref, cat_ref, acc_ref,
):
    line_rows = SIDE * seg_count
    half = own_ref.shape[1]
    side = ints_ref[1]
    cat_ref[...] = jnp.zeros_like(cat_ref)
    own, oth = [
        norm_rows(side_sums(got_ref, index), small_row(small_ref, index, 0), small_row(small_ref, index, 1), floats_ref[0])
        for index in (side, 1 - side)
    ]
    average, scale, shift, _ = [jnp.concatenate(pieces, axis=1) for pieces in zip(own, oth)]
    for line in range(SIDE):
        rows = slice(line * line_rows, (line + 1) * line_rows)
        act = jnp.concatenate([own_ref[rows, :], oth_ref[rows, :].astype(F32)], axis=1)
        pre = (act - average) * scale + shift
        hid = (pre * jax.nn.sigmoid(pre)).astype(BF16)
        hid_ref[rows, :] = hid
        store_taps(cat_ref, line, hid, line_rows, seg_count)
    span = SIDE * WIDE * seg_count
    step = WIDE * seg_count
    for row_off in range(3):
        part = dot32(cat_ref[row_off * step : row_off * step + span, :], w_ref[row_off])
        if row_off == 0:
            acc_ref[...] = part
        else:
            acc_ref[...] += part
    mask = line_mask(line_rows, seg_count, ints_ref[0])
    total = cross = jnp.zeros((8, half), F32)
    for line in range(SIDE):
        rows = slice(line * line_rows, (line + 1) * line_rows)
        act = acc_ref[line * step : line * step + line_rows, :]
        act_ref[rows, :] = act
        low_ref[rows, :] = act.astype(BF16)
        kept = act * mask
        total = line_sums(kept, total)
        cross = line_sums(kept * act, cross)
    send_sums(sent_ref, total, cross)


def store_frames(pad_ref, line, values, line_rows, seg_count):
    start = ((line + 2) * EDGE + 2) * seg_count
    pad_ref[start : start + line_rows, :] = values


def load_frames(pad_ref, line, row_off, col_off, line_rows, seg_count):
    start = ((line + 2 + row_off) * EDGE + 2 + col_off) * seg_count
    return pad_ref[start : start + line_rows, :]


def tap_offsets():
    for index in range(9):
        yield index, index // 3 - 1, index % 3 - 1
    for index in range(9):
        yield 9 + index, 2 * (index // 3 - 1), 2 * (index % 3 - 1)


def next_mask(line_rows, seg_count, count):
    seg = seg_index(line_rows, seg_count)
    return (seg + 1 < jnp.minimum(count, seg_count)).astype(F32)


def gate_forward(
    seg_count, other, ints_ref, floats_ref, act_ref, got_ref, small_ref, gated_ref, *rest,
):
    hid_ref, gate_ref = (None, None) if other else rest[:2]
    roll_ref, pad_ref = rest[-2:]
    line_rows = SIDE * seg_count
    pad_ref[...] = jnp.zeros_like(pad_ref)
    roll_ref[...] = jnp.zeros_like(roll_ref)
    side = 1 - ints_ref[1] if other else ints_ref[1]
    sums = side_sums(got_ref, side)
    follows = next_mask(line_rows, seg_count, ints_ref[0])
    for core in range(act_ref.shape[1] // LANES):
        lanes = slice(core * LANES, (core + 1) * LANES)
        rows_for = small_ref.at[2 * side + core]
        average, scale, shift, _ = norm_rows(sums[:, lanes], rows_for[2:3, :], rows_for[3:4, :], floats_ref[0])
        for line in range(SIDE):
            rows = slice(line * line_rows, (line + 1) * line_rows)
            act = act_ref[rows, lanes].astype(F32)
            pre = (act - average) * scale + shift
            roll_ref[rows, :] = pre * jax.nn.sigmoid(pre)
        for line in range(SIDE):
            first = line * line_rows
            here = roll_ref[first : first + line_rows, :]
            after = roll_ref[first + 1 : first + 1 + line_rows, :]
            store_frames(pad_ref, line, follows * (after - here), line_rows, seg_count)
        for line in range(SIDE):
            rows = slice(line * line_rows, (line + 1) * line_rows)
            total = jnp.zeros((line_rows, LANES), F32)
            for index, row_off, col_off in tap_offsets():
                kern = rows_for[4 + index : 5 + index, :]
                total += load_frames(pad_ref, line, row_off, col_off, line_rows, seg_count) * kern
            gate = jax.nn.sigmoid(total)
            hid = roll_ref[rows, :]
            gated_ref[rows, lanes] = (hid * (1.0 + gate)).astype(BF16)
            if not other:
                hid_ref[rows, lanes] = hid
                gate_ref[rows, lanes] = gate


def expand(
    seg_count, ints_ref, own_ref, oth_ref, near_own_ref, near_oth_ref, w_ref, bias_ref, act_ref, sent_ref,
):
    half = own_ref.shape[1]
    row_count = own_ref.shape[0]
    line_rows = SIDE * seg_count
    side = ints_ref[1]
    w_own = w_ref[pl.ds(pl.multiple_of(side * half, half), half), :]
    w_oth = w_ref[pl.ds(pl.multiple_of((1 - side) * half, half), half), :]
    total = cross = jnp.zeros((8, w_ref.shape[1]), F32)
    for clip, (left, right) in enumerate(((own_ref, oth_ref), (near_own_ref, near_oth_ref))):
        act_ref[clip] = dot32(left[...], w_own) + dot32(right[...], w_oth)
        mask = line_mask(line_rows, seg_count, ints_ref[2 * clip])
        for line in range(SIDE):
            act = act_ref[clip, line * line_rows : (line + 1) * line_rows, :]
            kept = act * mask
            total = line_sums(kept, total)
            cross = line_sums(kept * act, cross)
    send_sums(sent_ref, total, cross)
    sent_ref[2:3, :] = bias_ref[...]


def finish(
    seg_count, ints_ref, floats_ref, got_ref, gain_ref, shift_ref, flat_ref, act_own_ref, x_own_ref, grad_own_ref,
    act_oth_ref, x_oth_ref, grad_oth_ref, out_ref, resid_ref, pooled_ref, sent_ref,
):
    line_rows = SIDE * seg_count
    width = act_own_ref.shape[1]
    average, _, shift, inv_std = norm_rows(got_ref, gain_ref[...], shift_ref[...], floats_ref[0])
    gain = gain_ref[...]
    total = cross = jnp.zeros((8, width), F32)
    own, oth = (act_own_ref, x_own_ref, grad_own_ref), (act_oth_ref, x_oth_ref, grad_oth_ref)
    for clip, (act_ref, x_ref, grad_ref) in enumerate((own, oth)):
        place = ints_ref[3] if clip == 0 else 1 - ints_ref[3]
        mask = line_mask(line_rows, seg_count, ints_ref[2 * clip])
        flat = flat_ref[clip : clip + 1, :]
        pool = jnp.zeros((8, width), F32)
        for line in range(SIDE):
            rows = slice(line * line_rows, (line + 1) * line_rows)
            normed = (act_ref[rows, :] - average) * inv_std
            resid = x_ref[rows, :].astype(F32) + gain * normed + shift
            logistic = jax.nn.sigmoid(resid)
            output = mask * resid * logistic
            out_ref[place, rows, :] = output.astype(BF16)
            pool = line_sums(output, pool)
            grad = (grad_ref[rows, :].astype(F32) + flat) * mask
            grad = grad * (logistic * (1.0 + resid * (1.0 - logistic)))
            resid_ref[clip, rows, :] = grad
            total = line_sums(grad, total)
            cross = line_sums(grad * normed, cross)
        pooled_ref[clip : clip + 1, :] = jnp.sum(pool, axis=0, keepdims=True) * floats_ref[1 + clip]
    send_sums(sent_ref, total, cross)


def expand_backward(
    seg_count, clip, ints_ref, floats_ref, got_ref, back_ref, gain_ref, resid_ref, act_ref, w_ref,
    low_ref, *part_refs,
):
    line_rows = SIDE * seg_count
    half = w_ref.shape[0] // 2
    side = ints_ref[1]
    average, scale, _, inv_std = norm_rows(got_ref, gain_ref[...], gain_ref[...], floats_ref[0])
    back = back_ref[0:2, :] / floats_ref[0]
    mask = line_mask(line_rows, seg_count, ints_ref[2 * clip])
    for line in range(SIDE):
        rows = slice(line * line_rows, (line + 1) * line_rows)
        normed = (act_ref[rows, :] - average) * inv_std
        grad = scale * (resid_ref[rows, :] - mask * (back[0:1, :] + normed * back[1:2, :]))
        low_ref[rows, :] = grad.astype(BF16)
    for place, index in enumerate((side, 1 - side)):
        w_side = w_ref[pl.ds(pl.multiple_of(index * half, half), half), :]
        part = dot32(low_ref[...], w_side, ((1,), (1,)))
        if clip == 0:
            part_refs[place][...] = part
        else:
            part_refs[0][:, place * half : (place + 1) * half] = part.astype(BF16)


def gate_backward(
    seg_count, ints_ref, floats_ref, grad_ref, near_ref, far_ref, hid_ref, gate_ref, act_ref, got_ref, small_ref,
    logit_ref, slope_ref, low_ref, sent_ref, kern_grad_ref, field_ref, pad_ref, back_ref,
):
    line_rows = SIDE * seg_count
    pad_ref[...] = jnp.zeros_like(pad_ref)
    field_ref[...] = jnp.zeros_like(field_ref)
    back_ref[...] = jnp.zeros_like(back_ref)
    kern_grad_ref[...] = jnp.zeros_like(kern_grad_ref)
    side = ints_ref[1]
    sums = side_sums(got_ref, side)
    follows = next_mask(line_rows, seg_count, ints_ref[0])
    totals_all, cross_all = [], []
    for core in range(act_ref.shape[1] // LANES):
        lanes = slice(core * LANES, (core + 1) * LANES)
        rows_for = small_ref.at[2 * side + core]
        average, scale, shift, inv_std = norm_rows(sums[:, lanes], rows_for[2:3, :], rows_for[3:4, :], floats_ref[0])

        def whole_grad(rows):
            return grad_ref[rows, lanes] + near_ref[rows, lanes].astype(F32) + far_ref[rows, lanes].astype(F32)

        for line in range(SIDE):
            first = line * line_rows
            rows = slice(first, first + line_rows)
            here = hid_ref[rows, lanes]
            if line < SIDE - 1:
                after = hid_ref[first + 1 : first + 1 + line_rows, lanes]
            else:
                after = jnp.concatenate([hid_ref[first + 1 : first + line_rows, lanes], here[:1, :]], axis=0)
            store_frames(pad_ref, line, follows * (after - here), line_rows, seg_count)
            gate = gate_ref[rows, lanes]
            store_frames(field_ref, line, whole_grad(rows) * here * gate * (1.0 - gate), line_rows, seg_count)
        totals = [jnp.zeros((8, LANES), F32) for _ in range(18)]
        for line in range(SIDE):
            field = load_frames(field_ref, line, 0, 0, line_rows, seg_count)
            back = jnp.zeros((line_rows, LANES), F32)
            for index, row_off, col_off in tap_offsets():
                shifted = load_frames(pad_ref, line, row_off, col_off, line_rows, seg_count)
                totals[index] = line_sums(field * shifted, totals[index])
                kern = rows_for[4 + index : 5 + index, :]
                back += load_frames(field_ref, line, -row_off, -col_off, line_rows, seg_count) * kern
            start = 8 + line * line_rows
            back_ref[start : start + line_rows, :] = follows * back
        kern_grad_ref[0:18, lanes] = jnp.concatenate(
            [jnp.sum(each, axis=0, keepdims=True) for each in totals], axis=0
        )
        total = cross = jnp.zeros((8, LANES), F32)
        for line in range(SIDE):
            first = line * line_rows
            rows = slice(first, first + line_rows)
            before = back_ref[first + 7 : first + 7 + line_rows, :]
            here = back_ref[first + 8 : first + 8 + line_rows, :]
            grad = whole_grad(rows) * (1.0 + gate_ref[rows, lanes]) + before - here
            centred = act_ref[rows, lanes] - average
            grad = grad * silu_slope(centred * scale + shift)
            slope_ref[rows, lanes] = grad
            low_ref[rows, lanes] = grad.astype(BF16)
            total = line_sums(grad, total)
            cross = line_sums(grad * (centred * inv_std), cross)
        totals_all.append(total)
        cross_all.append(cross)
    send_sums(sent_ref, jnp.concatenate(totals_all, axis=1), jnp.concatenate(cross_all, axis=1))
    for peer in range(sent_ref.shape[0]):
        sent_ref[peer, 2:4, :] = logit_ref[...]


def back_rows(got_ref, back_ref, small_ref, row, side, count):
    average, scale, shift, inv_std = norm_rows(
        side_sums(got_ref, side), small_row(small_ref, side, row), small_row(small_ref, side, row + 1), count
    )
    back = side_sums(back_ref, side) / count
    return average, inv_std, scale, back[0:1, :], back[1:2, :], shift


def conv_backward(
    seg_count, ints_ref, floats_ref, grad_ref, more_ref, act_ref, oth_ref, got_ref, back_ref, first_ref, got_one_ref,
    small_ref, w_ref, from_ref, pair_ref, kern_grad_ref, slope_ref, low_ref, sent_ref, keep_ref, send_ref,
    field_ref, cat_ref, acc_ref, w_all_ref,
):
    line_rows = SIDE * seg_count
    half = grad_ref.shape[1]
    step = WIDE * seg_count
    span = SIDE * step
    side = ints_ref[1]
    count = floats_ref[0]
    mask = line_mask(line_rows, seg_count, ints_ref[0])
    cat_ref[...] = jnp.zeros_like(cat_ref)
    field_ref[...] = jnp.zeros_like(field_ref)
    own = back_rows(got_ref, back_ref, small_ref, 2, side, count)
    oth = back_rows(got_ref, back_ref, small_ref, 2, 1 - side, count)
    average, inv_std, scale, mean, mix, _ = [jnp.concatenate(pieces, axis=1) for pieces in zip(own, oth)]
    for line in range(SIDE):
        rows = slice(line * line_rows, (line + 1) * line_rows)
        act = jnp.concatenate([act_ref[rows, :], oth_ref[rows, :].astype(F32)], axis=1)
        grad = jnp.concatenate([grad_ref[rows, :], more_ref[rows, :].astype(F32)], axis=1)
        normed = (act - average) * inv_std
        low = (scale * (grad - mask * (mean + normed * mix))).astype(BF16)
        store_taps(cat_ref, line, low, line_rows, seg_count)
        field_ref[line * step : line * step + line_rows, :] = low[:, :half]
    core = ints_ref[3]
    size = half // 2
    depth = 2 * half
    for index, ref in ((core, keep_ref), (1 - core, send_ref)):
        lanes = pl.ds(pl.multiple_of(index * size, size), size)
        ref[:span, :] = field_ref[:, lanes]
        ref[span:, :] = kern_grad_ref[:, lanes].astype(BF16)
    for tap in range(9):
        w_all_ref[tap, :, :half] = w_ref[tap // 3, (tap % 3) * depth : (tap % 3) * depth + half, :]
        for index, ref in ((core, from_ref), (1 - core, pair_ref)):
            w_all_ref[tap, :, pl.ds(pl.multiple_of(half + index * size, size), size)] = ref[tap]
    for row_off in range(3):
        rows = slice(row_off * step, row_off * step + span)
        part = sum(
            dot32(cat_ref[rows, tap * depth : (tap + 1) * depth], w_all_ref[8 - 3 * row_off - tap], ((1,), (1,)))
            for tap in range(3)
        )
        if row_off == 0:
            acc_ref[...] = part
        else:
            acc_ref[...] += part
    average, scale, shift, inv_std = norm_rows(
        side_sums(got_one_ref, side), small_row(small_ref, side, 0), small_row(small_ref, side, 1), count
    )
    total = cross = jnp.zeros((8, half), F32)
    for line in range(SIDE):
        rows = slice(line * line_rows, (line + 1) * line_rows)
        centred = first_ref[rows, :] - average
        grad = acc_ref[line * step : line * step + line_rows, :]
        grad = grad * silu_slope(centred * scale + shift)
        slope_ref[rows, :] = grad
        low_ref[rows, :] = grad.astype(BF16)
        total = line_sums(grad, total)
        cross = line_sums(grad * (centred * inv_std), cross)
    send_sums(sent_ref, total, cross)


def split_rows(rows_ref, index, keep_ref, send_ref):
    size = keep_ref.shape[0]
    keep_ref[...] = rows_ref[pl.ds(pl.multiple_of(index * size, 16), size), :]
    send_ref[...] = rows_ref[pl.ds(pl.multiple_of((1 - index) * size, 16), size), :]


def taps_gradient(
    seg_count, ints_ref, hid_ref, field_ref, near_hid_ref, near_field_ref, keep_ref, send_ref, taps_ref, own_ref, near_ref,
    sum_ref,
):
    line_rows = SIDE * seg_count
    step = WIDE * seg_count
    span = SIDE * step
    taps_ref[...] = jnp.zeros_like(taps_ref)
    for source, turned in ((hid_ref, own_ref), (near_hid_ref, near_ref)):
        for line in range(SIDE):
            rows = slice(line * line_rows, (line + 1) * line_rows)
            store_taps(taps_ref, line, source[rows, :], line_rows, seg_count)
        for start in range(0, taps_ref.shape[1], LANES):
            turned[start : start + LANES, :] = taps_ref[:, start : start + LANES].T
    depth = taps_ref.shape[1]
    own, near = field_ref[:span, :], near_field_ref[:span, :]
    for row_off in range(3):
        rows = slice(row_off * step, row_off * step + span)
        part = dot32(own_ref[:, rows], own) + dot32(near_ref[:, rows], near)
        sum_ref[row_off * depth : (row_off + 1) * depth, :] = part.astype(BF16)
    rest = sum_ref.shape[0] - 3 * depth
    count = field_ref.shape[0] - span
    sum_ref[3 * depth :, :] = jnp.zeros((rest, LANES), BF16)
    kern_grad = field_ref[span:, :].astype(F32) + near_field_ref[span:, :].astype(F32)
    sum_ref[3 * depth : 3 * depth + count, :] = kern_grad.astype(BF16)
    split_rows(sum_ref, ints_ref[4], keep_ref, send_ref)


def sum_into(sum_ref, *refs):
    total = refs[0][...].astype(F32)
    for ref in refs[1:]:
        total += ref[...].astype(F32)
    sum_ref[...] = total.astype(sum_ref.dtype)


def store_blocks(ints_ref, rows_ref, refs):
    size = refs[0].shape[0]
    for bits, ref in enumerate(refs):
        start = pl.multiple_of((ints_ref[5] ^ bits) * size, 8)
        ref[...] = rows_ref[pl.ds(start, size), :].astype(ref.dtype)


def join_blocks(ints_ref, refs, out_ref):
    size = refs[0].shape[0]
    for bits, ref in enumerate(refs):
        start = pl.multiple_of((ints_ref[5] ^ bits) * size, 8)
        out_ref[pl.ds(start, size), :] = ref[...]


def sum_split(ints_ref, own_ref, got_ref, keep_ref, send_ref, sum_ref):
    sum_into(sum_ref, own_ref, got_ref)
    split_rows(sum_ref, ints_ref[4], keep_ref, send_ref)


def sum_blocks(ints_ref, own_ref, got_ref, *refs):
    sum_into(refs[-1], own_ref, got_ref)
    store_blocks(ints_ref, refs[-1], refs[:-1])


def sum_parts(*refs):
    sum_into(refs[-1], *refs[:-1])


def join_pair(ints_ref, own_ref, got_ref, out_ref):
    size = own_ref.shape[0]
    for index, ref in ((ints_ref[4], own_ref), (1 - ints_ref[4], got_ref)):
        out_ref[pl.ds(pl.multiple_of(index * size, 16), size), :] = ref[...]


def stage_one(places, ints_ref, pack_ref, pack_got_ref, reduce_ref, *refs):
    blocks, (keep_ref, send_ref, sum_ref) = refs[:places], refs[places:]
    sum_into(sum_ref, pack_ref, pack_got_ref)
    store_blocks(ints_ref, sum_ref, blocks)
    split_rows(reduce_ref, ints_ref[4], keep_ref, send_ref)


def stage_two(places, ints_ref, keep_ref, got_ref, *refs):
    pack, refs = refs[:places], refs[places:]
    outs, sum_ref = refs[:places], refs[places]
    total = pack[0][...].astype(F32)
    for ref in pack[1:]:
        total += ref[...].astype(F32)
    total = total.astype(BF16)
    sum_into(sum_ref, keep_ref, got_ref)
    rows, lanes = total.shape
    size = sum_ref.shape[0] // places
    for bits, ref in enumerate(outs):
        ref[:rows, :] = total
        start = pl.multiple_of((ints_ref[5] ^ bits) * size, 8)
        block = sum_ref[pl.ds(start, size), :].astype(BF16)
        for index in range(sum_ref.shape[1] // lanes):
            ref[rows + index * size : rows + (index + 1) * size, :] = block[:, index * lanes : (index + 1) * lanes]


def stage_three(places, rows, ints_ref, *refs):
    parts, (join_ref, columns_ref) = refs[:places], refs[places:]
    size = columns_ref.shape[1]
    for bits, ref in enumerate(parts):
        start = pl.multiple_of((ints_ref[5] ^ bits) * rows, 8)
        join_ref[pl.ds(start, rows), :] = ref[:rows, :]
    total = parts[0][rows:, :].astype(F32)
    for ref in parts[1:]:
        total += ref[rows:, :].astype(F32)
    total = total.astype(BF16)
    for place, side in enumerate((ints_ref[1], 1 - ints_ref[1])):
        for core in range(2):
            start = (2 * place + core) * size
            for clip in range(columns_ref.shape[0] // 4):
                columns_ref[clip * 4 + 2 * side + core] = total[start : start + size, :]


def join_places(ints_ref, *refs):
    join_blocks(ints_ref, refs[:-1], refs[-1])


def unpack_spatial(ints_ref, own_ref, got_ref, out_ref, near_ref, far_ref, rows_ref):
    join_pair(ints_ref, own_ref, got_ref, rows_ref)
    depth = out_ref.shape[1]
    half = depth // 2
    side = ints_ref[1]
    for tap in range(9):
        for place, index in enumerate((side, 1 - side)):
            start = tap * depth + place * half
            target = pl.ds(pl.multiple_of(index * half, half), half)
            out_ref[tap, target, :] = rows_ref[start : start + half, :].astype(F32)
    rest = rows_ref[9 * depth : 9 * depth + 32, :].astype(F32)
    near_ref[...] = rest[0:9, :]
    far_ref[...] = rest[9:18, :]


def unpack_wide(ints_ref, own_ref, got_ref, out_ref, classes_ref, rows_ref):
    join_pair(ints_ref, own_ref, got_ref, rows_ref)
    half = out_ref.shape[0] // 2
    for place, index in enumerate((ints_ref[1], 1 - ints_ref[1])):
        target = pl.ds(pl.multiple_of(index * half, half), half)
        out_ref[target, :] = rows_ref[place * half : (place + 1) * half, :].astype(F32)
    classes_ref[...] = rows_ref[2 * half :, :].astype(F32)


def last_norm(
    seg_count, ints_ref, floats_ref, grad_ref, more_ref, act_ref, oth_ref, got_ref, back_ref, small_ref, low_own_ref, low_oth_ref,
):
    line_rows = SIDE * seg_count
    side = ints_ref[1]
    mask = line_mask(line_rows, seg_count, ints_ref[0])
    half = grad_ref.shape[1]
    for place, (grads, acts) in enumerate(((grad_ref, act_ref), (more_ref, oth_ref))):
        index = side if place == 0 else 1 - side
        average, inv_std, scale, mean, mix, _ = back_rows(
            got_ref, back_ref, small_ref, 0, index, floats_ref[0]
        )
        for line in range(SIDE):
            rows = slice(line * line_rows, (line + 1) * line_rows)
            normed = (acts[rows, :].astype(F32) - average) * inv_std
            grad = scale * (grads[rows, :].astype(F32) - mask * (mean + normed * mix))
            (low_own_ref, low_oth_ref)[place][rows, :] = grad.astype(BF16)


def pick_rows(ints_ref, w_ref, out_ref):
    size = out_ref.shape[1]
    out_ref[...] = w_ref[:, pl.ds(pl.multiple_of((1 - ints_ref[1]) * size, size), size), :]


def expand_gradient(
    ints_ref, own_ref, oth_ref, near_own_ref, near_oth_ref, low_ref, near_low_ref, classes_ref,
    keep_ref, send_ref, out_ref,
):
    half = own_ref.shape[1]
    for place, (first, second) in enumerate(((own_ref, near_own_ref), (oth_ref, near_oth_ref))):
        part = dot32(first[...], low_ref[...], ((0,), (0,))) + dot32(second[...], near_low_ref[...], ((0,), (0,)))
        out_ref[place * half : (place + 1) * half, :] = part.astype(BF16)
    rest = out_ref.shape[0] - 2 * half
    out_ref[2 * half :, :] = jnp.zeros((rest, out_ref.shape[1]), BF16)
    count = classes_ref.shape[0]
    out_ref[2 * half : 2 * half + count, :] = classes_ref[...].astype(BF16)
    split_rows(out_ref, ints_ref[4], keep_ref, send_ref)


def reduce_gradient(
    ints_ref, x_own_ref, own_ref, oth_ref, x_oth_ref, near_own_ref, near_oth_ref, keep_ref, send_ref, out_ref
):
    half = own_ref.shape[1]
    for place, (low, near) in enumerate(((own_ref, near_own_ref), (oth_ref, near_oth_ref))):
        part = dot32(x_own_ref[...], low[...], ((0,), (0,))) + dot32(x_oth_ref[...], near[...], ((0,), (0,)))
        out_ref[:, place * half : (place + 1) * half] = part.astype(BF16)
    split_rows(out_ref, ints_ref[4], keep_ref, send_ref)


def input_gradient(
    ints_ref, own_ref, oth_ref, w_ref, resid_ref, near_own_ref, near_oth_ref, out_ref
):
    core = ints_ref[3]
    half = own_ref.shape[1]
    w_own, w_oth = w_ref[:, :half], w_ref[:, half:]
    for clip, (own, oth) in enumerate(((own_ref, oth_ref), (near_own_ref, near_oth_ref))):
        grad = dot32(own[...], w_own, ((1,), (1,))) + dot32(oth[...], w_oth, ((1,), (1,)))
        out_ref[core if clip == 0 else 1 - core] = resid_ref[clip] + grad


def per_device(
    clip_size,
    chan_size,
    frames_in,
    seg_counts,
    w_reduce,
    gain_one,
    shift_one,
    w_spatial,
    gain_two,
    shift_two,
    near_kern,
    far_kern,
    w_expand,
    gain_three,
    shift_three,
    w_classes,
    class_bias,
    out_grad,
    logit_grad,
):
    clip_count, seg_count, pixel_count, chan_local = frames_in.shape
    mid_local = w_reduce.shape[1]
    mid_width = w_spatial.shape[1]
    half = mid_width // 2
    row_count = seg_count * pixel_count
    class_count = w_classes.shape[1]
    chan_index = lax.axis_index("chan")
    clip_index = lax.axis_index("clip")
    side_index = chan_index // 2
    core_index = chan_index % 2
    everyone = clip_size * chan_size
    sds = jax.ShapeDtypeStruct

    def swap(array, bits):
        array = array.array if isinstance(array, (Near, Free)) else array
        return Free(lax.ppermute(array, "chan", [(i, i ^ bits) for i in range(chan_size)]))

    def own_first(array, index, size, axis):
        own = lax.dynamic_slice_in_dim(array, index * size, size, axis)
        oth = lax.dynamic_slice_in_dim(array, (1 - index) * size, size, axis)
        return own, oth

    def pair(own, oth):
        flip = core_index == 1
        return jnp.where(flip, oth, own), jnp.where(flip, own, oth)

    def swap_clip(array, bits):
        array = array.array if isinstance(array, (Near, Free)) else array
        return lax.ppermute(array, "clip", [(i, i ^ bits) for i in range(clip_size)])

    parity, place = clip_index % 2, clip_index // 2
    places = clip_size // 2
    groups = [list(range(first, clip_size, 2)) for first in range(2)]

    def sum_places(values):
        if places > 4:
            return lax.psum(values, "clip", axis_index_groups=groups)
        return sum([values] + [swap_clip(values, 2 * bits) for bits in range(1, places)])

    def share_all(sent):
        got = lax.all_to_all(sent, ("clip", "chan"), 0, 0)
        return got.reshape((clip_size, chan_size) + sent.shape[1:])

    def share_clip(sent):
        sent = sent.array
        return sum_places(sent + swap_clip(sent, 1))

    own_counts = lax.dynamic_slice_in_dim(seg_counts, clip_index * clip_count, clip_count)
    count_pair = jnp.concatenate(own_first(own_counts, core_index, 1, 0))
    valid_total = jnp.sum(seg_counts).astype(F32) * pixel_count
    count_scale = 1.0 / (count_pair.astype(F32) * pixel_count)
    ints = jnp.stack([count_pair[0], side_index, count_pair[1], core_index, parity, place])
    floats = jnp.concatenate([valid_total[None], count_scale])

    x_all = frames_in.transpose(0, 2, 1, 3).reshape(clip_count, row_count, chan_local)
    grad_all = out_grad.transpose(0, 2, 1, 3).reshape(clip_count, row_count, chan_local)
    x_own, x_oth = Pick(x_all, lambda ints: ints[3]), Pick(x_all, lambda ints: 1 - ints[3])
    grad_own, grad_oth = Pick(grad_all, lambda ints: ints[3]), Pick(grad_all, lambda ints: 1 - ints[3])
    half_f32, near_f32 = sds((row_count, half), F32), near((row_count, half), F32)
    half_low, near_low_half = sds((row_count, half), BF16), near((row_count, half), BF16)
    sums_shape = sds((everyone, 2, half), F32)
    pad_rows = 9 * WIDE * seg_count
    span = SIDE * WIDE * seg_count
    edge_rows = EDGE * EDGE * seg_count

    block_shape = sds((chan_local + 96, mid_local), BF16)
    chan = chan_index.astype(jnp.int32)[None]
    sent_blocks = call(split_blocks, (block_shape,) * chan_size, ints=chan)(
        w_reduce, gain_one[None], shift_one[None], gain_two[None], shift_two[None], near_kern, far_kern
    )
    got_blocks = {bits: swap(sent_blocks[bits], bits) for bits in (2, 3, 1)}

    part_oth, w_rows, small = call(
        reduce_other,
        (
            near((row_count, mid_width), BF16),
            sds((chan_local, mid_width), BF16),
            sds((chan_size, 24, mid_local), F32),
        ),
        ints=ints,
    )(sent_blocks[0], got_blocks[1], got_blocks[2], got_blocks[3], x_oth)
    near_one = swap(part_oth, 1)
    part_own, far_send = call(
        reduce_own,
        (near((row_count, half), F32), near((row_count, half), BF16)),
        ints=ints,
    )(near_one, w_rows, x_own)
    far_one = swap(far_send, 2)

    w_pair = jnp.concatenate(pair(w_spatial, swap(w_spatial, 1).array), axis=2)
    w_fwd_own, w_fwd_oth = own_first(w_pair, side_index, half, 1)
    w_fwd = jnp.concatenate([w_fwd_own, w_fwd_oth], axis=1).reshape(3, 3 * mid_width, half)

    act_one, act_one_low, sent_one = call(
        functools.partial(first_sums, seg_count), (half_f32, half_low, sums_shape), deps=(w_fwd,), ints=ints,
    )(part_own, far_one)
    act_one_oth = swap(act_one_low, 2)
    got_one = share_all(sent_one)

    act_two, act_two_low, sent_two, hid_one = call(
        functools.partial(conv_forward, seg_count),
        (half_f32, half_low, sums_shape, sds((row_count, mid_width), BF16)),
        [pltpu.VMEM((pad_rows, 3 * mid_width), BF16), pltpu.VMEM((span, half), F32)],
        ints=ints,
        floats=floats,
    )(act_one, act_one_oth, got_one, small, w_fwd)
    act_two_oth = swap(act_two_low, 2)
    got_two = share_all(sent_two)

    def gate_call(act, other):
        return call(
            functools.partial(gate_forward, seg_count, other),
            (near_low_half,) if other else (near_low_half, near_f32, near_f32),
            [pltpu.VMEM((row_count + 8, LANES), F32), pltpu.VMEM((edge_rows, LANES), F32)],
            ints=ints,
            floats=floats,
        )(act, got_two, small)

    gated_own, hid_two, gate = gate_call(act_two, False)
    near_own = swap(gated_own, 1)
    gated_oth = gate_call(act_two_oth, True)[0]
    near_oth = swap(gated_oth, 1)

    near_hid = swap(hid_one, 1)

    bias_row = jnp.sum(logit_grad.astype(F32), axis=0)
    bias_row = jnp.pad(bias_row, (0, chan_local - class_count))[None]
    act_three, sent_three = call(
        functools.partial(expand, seg_count),
        (near((2, row_count, chan_local), F32), near((3, chan_local), F32)),
        ints=ints,
    )(gated_own, gated_oth, near_own, near_oth, w_expand, bias_row)
    got_three = share_clip(sent_three)

    to_side = call(pick_rows, sds((9, half, mid_local), BF16), deps=(sent_two,), ints=ints)(w_spatial)
    from_side = swap(to_side, 2)
    from_pair = swap(from_side, 1)


    logit_pair = jnp.concatenate(own_first(logit_grad, core_index, 1, 0))
    grad_pooled = dot32(logit_pair, w_classes, ((1,), (1,))) * count_scale[:, None]
    output, grad_resid, pooled, sent_back = call(
        functools.partial(finish, seg_count),
        (
            sds((2, row_count, chan_local), BF16),
            near((2, row_count, chan_local), F32),
            near((2, chan_local), F32),
            near((2, chan_local), F32),
        ),
        ints=ints,
        floats=floats,
    )(
        got_three, gain_three[None], shift_three[None], grad_pooled,
        Pick(act_three, 0), x_own, grad_own, Pick(act_three, 1), x_oth, grad_oth,
    )
    got_back = share_clip(sent_back)
    pooled = pooled.array.astype(BF16)

    def back_call(clip):
        outs = [near((row_count, chan_local), BF16)]
        if clip == 0:
            outs += [near((row_count, half), F32)] * 2
        else:
            outs += [near((row_count, mid_width), BF16)]
        return call(
            functools.partial(expand_backward, seg_count, clip), tuple(outs), deps=(from_side,), ints=ints, floats=floats,
        )(got_three, got_back, gain_three[None], Pick(grad_resid, clip), Pick(act_three, clip), w_expand)

    low_three_oth, back_oth = back_call(1)
    near_back = swap(back_oth, 1)
    low_three_own, back_own, back_far = back_call(0)

    unit = 16 * clip_size
    def halves(rows, width):
        return (sds((rows // 2, width), BF16),) * 2

    def to_places(blocks):
        if places > 4:
            order = place ^ jnp.arange(places)
            sent = jnp.stack([block.array if isinstance(block, Free) else block for block in blocks])[order]
            return list(lax.all_to_all(sent, "clip", 0, 0, axis_index_groups=groups)[order])
        return [blocks[0]] + [swap_clip(blocks[bits], 2 * bits) for bits in range(1, places)]

    def blocks_of(rows, width):
        return (sds((rows // places, width), BF16),) * places

    grad_classes = dot32(logit_pair, pooled, ((0,), (0,)))
    wide_rows = (-(-(mid_width + class_count) // unit) + 1) * unit
    wide_keep, wide_send = call(
        expand_gradient, halves(wide_rows, chan_local), [pltpu.VMEM((wide_rows, chan_local), BF16)], ints=ints,
    )(gated_own, gated_oth, near_own, near_oth, low_three_own, low_three_oth, grad_classes)

    far_back = swap(call(add_low, near_low_half, deps=())(near_back, back_far), 2)
    wide_blocks = call(
        sum_blocks,
        blocks_of(wide_rows // 2, chan_local),
        [pltpu.VMEM((wide_rows // 2, chan_local), BF16)],
        ints=ints,
    )(wide_keep, swap_clip(wide_send, 1))
    wide_got = to_places(wide_blocks)

    logits_part = jnp.concatenate(own_first(dot32(pooled, w_classes), core_index, 1, 0))
    logits_wide = jnp.pad(logits_part, ((0, 0), (0, half - class_count)))
    slope_two, slope_two_low, sent_back_two, kern_grad = call(
        functools.partial(gate_backward, seg_count),
        (half_f32, half_low, sds((everyone, 4, half), F32), sds((32, half), F32)),
        [
            pltpu.VMEM((edge_rows, LANES), F32),
            pltpu.VMEM((edge_rows, LANES), F32),
            pltpu.VMEM((row_count + 8, LANES), F32),
        ],
        deps=(wide_send,),
        ints=ints,
        floats=floats,
    )(back_own, near_back, far_back, hid_two, gate, act_two, got_two, small, logits_wide)
    slope_two_oth = swap(slope_two_low, 2)
    got_back_two = share_all(sent_back_two)
    slope_one, slope_one_low, sent_back_one, field_keep, field_send = call(
        functools.partial(conv_backward, seg_count),
        (half_f32, half_low, sums_shape) + (sds((span + 32, mid_local), BF16),) * 2,
        [
            pltpu.VMEM((span, half), BF16),
            pltpu.VMEM((pad_rows, 3 * mid_width), BF16),
            pltpu.VMEM((span, half), F32),
            pltpu.VMEM((9, half, mid_width), BF16),
        ],
        deps=(wide_blocks[0], near_hid),
        ints=ints,
        floats=floats,
    )(
        slope_two, slope_two_oth, act_two, act_two_oth, got_two, got_back_two, act_one, got_one, small, w_fwd,
        from_side, from_pair, kern_grad,
    )
    slope_one_oth = swap(slope_one_low, 2)
    got_back_one = share_all(sent_back_one)

    pack_rows = -(-(9 * mid_width + 32) // unit) * unit
    pack_keep, pack_pair = call(
        functools.partial(taps_gradient, seg_count),
        halves(pack_rows, mid_local),
        [pltpu.VMEM((pad_rows, 3 * mid_width), BF16)]
        + [pltpu.VMEM((3 * mid_width, pad_rows), BF16)] * 2
        + [pltpu.VMEM((pack_rows, mid_local), BF16)],
        ints=ints,
        work=20_000_000_000,
        room=40 * 1024 * 1024,
    )(hid_one, field_keep, near_hid, swap(field_send, 1))

    wide_part = call(sum_parts, sds((wide_rows // clip_size, chan_local), BF16), deps=(pack_pair,))(*wide_got)

    low_pair = call(
        functools.partial(last_norm, seg_count),
        (half_low,) * 2,
        deps=(pack_pair, wide_part),
        ints=ints,
        floats=floats,
        work=50_000_000_000,
    )(slope_one, slope_one_oth, act_one, act_one_oth, got_one, got_back_one, small)
    near_pair = [swap(low, 1) for low in low_pair]
    pack_other = swap_clip(pack_pair, 1)
    reduce_keep, reduce_send = call(
        reduce_gradient,
        (Loose((chan_local // 2, mid_width), BF16),) * 2,
        [pltpu.VMEM((chan_local, mid_width), BF16)],
        ints=ints,
    )(x_own, *low_pair, x_oth, *near_pair)

    share = chan_local // clip_size
    loose_blocks = (Loose((pack_rows // clip_size, mid_local), BF16),) * places
    pack_blocks = call(
        sum_blocks,
        loose_blocks,
        [pltpu.VMEM((pack_rows // 2, mid_local), BF16)],
        deps=(reduce_send,),
        ints=ints,
    )(pack_keep, Free(pack_other))
    pack_got = to_places(pack_blocks)
    wide_join = call(
        join_places, Loose((wide_rows // 2, chan_local), BF16), deps=(pack_blocks[0],), ints=ints,
    )(*[Free(each) for each in to_places([wide_part] * places)])
    wide_other = swap_clip(wide_join, 1)
    reduce_got = swap_clip(reduce_send, 1)
    part_rows = pack_rows // clip_size
    parts = call(
        functools.partial(stage_two, places),
        (Loose((part_rows + chan_size * share, mid_local), BF16),) * places,
        [pltpu.VMEM((chan_local // 2, mid_width), F32)],
        deps=(wide_join,),
        ints=ints,
    )(reduce_keep, Free(reduce_got), *[Free(each) if index else each for index, each in enumerate(pack_got)])
    parts_got = to_places(parts)
    grad_frames = call(
        input_gradient, sds((2, row_count, chan_local), F32), deps=(parts[0],), ints=ints,
    )(*low_pair, w_rows, grad_resid, *near_pair)
    pack_join, columns = call(
        functools.partial(stage_three, places, part_rows),
        (Loose((pack_rows // 2, mid_local), BF16), sds((everyone, share, mid_local), BF16)),
        deps=(wide_other, grad_frames),
        ints=ints,
    )(*[Free(each) if index else each for index, each in enumerate(parts_got)])
    pack_other = swap_clip(pack_join, 1)
    reduce_got = lax.all_to_all(columns, ("clip", "chan"), 0, 0)
    reduce_got = reduce_got.reshape(places, 2, chan_size, share, mid_local).transpose(2, 1, 0, 3, 4)
    grad_w_reduce = reduce_got.reshape(chan_size * chan_local, mid_local).astype(F32)
    grad_w_expand, classes_got = call(
        unpack_wide,
        (sds((mid_width, chan_local), F32), sds((wide_rows - mid_width, chan_local), F32)),
        [pltpu.VMEM((wide_rows, chan_local), BF16)],
        deps=(pack_join,),
        ints=ints,
    )(wide_join, Free(wide_other))
    grad_w_classes = classes_got[:class_count].T
    grad_spatial, grad_near, grad_far = call(
        unpack_spatial,
        (sds((9, mid_width, mid_local), F32),) + (sds((9, mid_local), F32),) * 2,
        [pltpu.VMEM((pack_rows, mid_local), BF16)],
        ints=ints,
        work=20_000_000_000,
    )(pack_join, Free(pack_other))

    mine = lax.dynamic_index_in_dim(got_back_two, clip_index, 0, keepdims=False)
    logits = jnp.sum(mine, axis=0)[2:, :class_count] + class_bias

    def own_sums(got):
        sums = jnp.sum(got.reshape((clip_size, 2, 2) + got.shape[2:]), axis=(0, 2))
        sums = lax.dynamic_index_in_dim(sums, side_index, 0, keepdims=False)
        return lax.dynamic_slice_in_dim(sums[:2], core_index * mid_local, mid_local, 1)

    grads_one = own_sums(got_back_one)
    grads_two = own_sums(got_back_two)
    grads_three = got_back
    grad_bias = got_three[2, :class_count]

    def whole(array):
        return array.reshape(2, pixel_count, seg_count, chan_local).transpose(0, 2, 1, 3)

    return (
        whole(output),
        logits,
        whole(grad_frames),
        grad_w_reduce,
        grads_one[1],
        grads_one[0],
        grad_spatial,
        grads_two[1],
        grads_two[0],
        grad_near,
        grad_far,
        grad_w_expand,
        grads_three[1],
        grads_three[0],
        grad_w_classes,
        grad_bias,
    )


def solution(mesh):
    in_specs = (
        P("clip", None, None, "chan"),
        P(),
        P(None, "chan"),
        P("chan"),
        P("chan"),
        P(None, None, "chan"),
        P("chan"),
        P("chan"),
        P(None, "chan"),
        P(None, "chan"),
        P(None, "chan"),
        P("chan"),
        P("chan"),
        P("chan", None),
        P(),
        P("clip", None, None, "chan"),
        P("clip", None),
    )
    out_specs = (
        P("clip", None, None, "chan"),
        P("clip", None),
        P("clip", None, None, "chan"),
        P(None, "chan"),
        P("chan"),
        P("chan"),
        P(None, None, "chan"),
        P("chan"),
        P("chan"),
        P(None, "chan"),
        P(None, "chan"),
        P(None, "chan"),
        P("chan"),
        P("chan"),
        P("chan", None),
        P(),
    )
    body = functools.partial(per_device, mesh.shape["clip"], mesh.shape["chan"])
    return jax.shard_map(
        body, mesh=mesh, in_specs=in_specs, out_specs=out_specs, check_vma=False
    )
```

```python
import functools

import jax
import jax.numpy as jnp
from jax import lax
from jax.experimental import pallas as pl
from jax.experimental.pallas import tpu as pltpu
from jax.sharding import PartitionSpec as P

SIDE = 7
WIDE = SIDE + 1
EDGE = SIDE + 4
EPSILON = 1e-05
LANES = 128
F32 = jnp.float32
WORK = {"taps_gradient": 20, "unpack_spatial": 20, "last_norm": 1, "stage_two": 50}
BF16 = jnp.bfloat16
VMEM_BYTES = 20 * 1024 * 1024


def silu_slope(pre_act):
    logistic = jax.nn.sigmoid(pre_act)
    return logistic * (1.0 + pre_act * (1.0 - logistic))


def seg_index(row_count, seg_count):
    return lax.broadcasted_iota(jnp.int32, (row_count, 1), 0) % seg_count


def dot32(left, right, dims=((1,), (0,))):
    return lax.dot_general(left, right, (dims, ((), ())), preferred_element_type=F32)


class Pick:
    def __init__(self, array, index):
        self.array = array
        self.index = index


class Free:
    def __init__(self, array):
        self.array = array


class Late:
    def __init__(self, array):
        self.array = array


class Early:
    def __init__(self, shape, dtype, parts):
        self.shape = shape
        self.dtype = dtype
        self.parts = parts


class Leaving:
    def __init__(self, target, ref, sems):
        self.target = target
        self.ref = ref
        self.sems = sems
        self.copies = []
        self.shape = ref.shape
        self.dtype = ref.dtype

    def __getitem__(self, index):
        return self.ref[index]

    def __setitem__(self, index, value):
        self.ref[index] = value

    def leave(self, source, target):
        copy = pltpu.make_async_copy(self.ref.at[source], self.target.at[target], self.sems.at[len(self.copies)])
        copy.start()
        self.copies.append(copy)


class Near:
    def __init__(self, array):
        self.array = array


class Loose:
    def __init__(self, shape, dtype):
        self.shape = shape
        self.dtype = dtype


class Arriving:
    def __init__(self, copy, ref):
        self.copy = copy
        self.ref = ref
        self.shape = ref.shape

    def __getitem__(self, index):
        if self.copy is not None:
            self.copy.wait()
            self.copy = None
        return self.ref[index]


def near(shape, kind):
    return pltpu.VMEM(shape, kind)


def call(body, out_shape, scratch=(), deps=(), ints=None, floats=None, room=VMEM_BYTES):
    single = not isinstance(out_shape, (tuple, list))
    shapes = (out_shape,) if single else tuple(out_shape)
    early = [isinstance(out, Early) for out in shapes]
    away = [isinstance(out, (jax.ShapeDtypeStruct, Early)) for out in shapes]
    loose = [isinstance(out, Loose) for out in shapes]
    outs = tuple(
        pltpu.HBM(out.shape, out.dtype) if far else jax.ShapeDtypeStruct(out.shape, out.dtype) if free else out
        for out, far, free in zip(shapes, away, loose)
    )
    scalars = [array for array in (ints, floats) if array is not None]
    name = getattr(body, "func", body).__name__
    work = WORK.get(name, 0)

    def bare(arg):
        while isinstance(arg, (Pick, Free, Near, Late)):
            arg = arg.array
        return arg

    def placed(arg):
        inner = arg.array if isinstance(arg, (Pick, Late)) else arg
        if isinstance(inner, Free):
            return inner.array
        if isinstance(inner, Near):
            return pltpu.with_memory_space_constraint(inner.array, pltpu.VMEM)
        return pltpu.with_memory_space_constraint(inner, pltpu.HBM)

    def run(*args):
        fetched = [
            isinstance(arg, Late) or isinstance(arg, Pick) and not isinstance(arg.array, Near) for arg in args
        ]
        buffers = [
            pltpu.VMEM(arg.array.shape[1 if isinstance(arg, Pick) else 0 :], arg.array.dtype)
            for arg, own in zip(args, fetched)
            if own
        ]
        count = len(buffers)
        for out, parts in zip(shapes, early):
            if parts:
                buffers += [pltpu.VMEM(out.shape, out.dtype), pltpu.SemaphoreType.DMA((out.parts,))]
        if count:
            buffers.append(pltpu.SemaphoreType.DMA((count,)))

        def kernel(*refs):
            first = refs[: len(scalars)]
            inputs = refs[len(scalars) : len(scalars) + len(args)]
            rest = refs[len(scalars) + len(args) + len(deps) :]
            results, local = rest[: len(outs)], rest[len(outs) : len(outs) + len(buffers)]
            rest = rest[len(outs) + len(buffers) :]
            passed = []
            for arg, ref, own in zip(args, inputs, fetched):
                if isinstance(arg, Pick):
                    ref = ref.at[arg.index if isinstance(arg.index, int) else arg.index(first[0])]
                if own:
                    place = sum(isinstance(each, Arriving) for each in passed)
                    copy = pltpu.make_async_copy(ref, local[place], local[-1].at[place])
                    copy.start()
                    ref = Arriving(copy, local[place])
                passed.append(ref)
            leaving, done = [], count
            for result, parts in zip(results, early):
                if parts:
                    result = Leaving(result, local[done], local[done + 1])
                    done += 2
                leaving.append(result)
            body(*first, *passed, *leaving, *rest)
            for result in leaving:
                if isinstance(result, Leaving):
                    for copy in result.copies:
                        copy.wait()

        kernel.__name__ = name
        anywhere = pl.BlockSpec(memory_space=pl.ANY)
        results = pl.pallas_call(
            kernel,
            out_shape=outs,
            in_specs=[SMEM] * len(scalars)
            + [anywhere if own else VMEM for own in fetched]
            + [anywhere] * len(deps),
            out_specs=[anywhere if parts else VMEM for parts in early],
            scratch_shapes=buffers + list(scratch),
            compiler_params=pltpu.CompilerParams(vmem_limit_bytes=room),
            cost_estimate=pl.CostEstimate(flops=work * 1_000_000_000, bytes_accessed=0, transcendentals=0) if work else None,
        )(*scalars, *[placed(arg) for arg in args], *[placed(dep) for dep in deps])
        results = tuple(
            result if far else Free(result) if free else Near(result)
            for result, far, free in zip(results, away, loose)
        )
        return results[0] if single else results

    return run


SMEM = pl.BlockSpec(memory_space=pltpu.SMEM)
VMEM = pl.BlockSpec(memory_space=pltpu.VMEM)


def store_taps(cat_ref, line, values, line_rows, seg_count):
    depth = values.shape[1]
    for tap in range(3):
        start = ((line + 1) * WIDE + 1 - tap) * seg_count
        cat_ref[start : start + line_rows, tap * depth : (tap + 1) * depth] = values


def line_sums(values, row_of):
    return jnp.sum(values.reshape(-1, 8, values.shape[1]), axis=0) + row_of


def clear_taps(cat_ref, seg_count):
    depth = cat_ref.shape[1] // 3
    for tap in range(3):
        lanes = slice(tap * depth, (tap + 1) * depth)
        spans = [(0, WIDE + 1 - tap), (SIDE * WIDE + WIDE - tap, cat_ref.shape[0] // seg_count)]
        spans += [((line + 1) * WIDE + WIDE - tap, (line + 1) * WIDE + WIDE + 1 - tap) for line in range(SIDE - 1)]
        for first, last in spans:
            rows = (last - first) * seg_count
            cat_ref[first * seg_count : last * seg_count, lanes] = jnp.zeros((rows, depth), cat_ref.dtype)


def send_sums(sent_ref, total, cross):
    sums = jnp.concatenate([jnp.sum(total, axis=0, keepdims=True), jnp.sum(cross, axis=0, keepdims=True)], axis=0)
    if len(sent_ref.shape) == 2:
        sent_ref[0:2, :] = sums
        return
    for peer in range(sent_ref.shape[0]):
        sent_ref[peer, 0:2, :] = sums


def side_sums(got_ref, side):
    total = jnp.zeros((2, got_ref.shape[3]), F32)
    for clip in range(got_ref.shape[0]):
        for core in range(2):
            total += got_ref[clip, side * 2 + core, 0:2, :]
    return total


def norm_rows(sums, gain_vec, shift_vec, count):
    average = sums[0:1, :] / count
    inv_std = lax.rsqrt(sums[1:2, :] / count - average * average + EPSILON)
    return average, gain_vec * inv_std, shift_vec, inv_std


def line_mask(line_rows, seg_count, count):
    return (seg_index(line_rows, seg_count) < count).astype(F32)


def split_blocks(
    ints_ref, w_ref, gain_one_ref, shift_one_ref, gain_two_ref, shift_two_ref, near_ref, far_ref, *refs
):
    size = refs[0].shape[0] - 96
    small = jnp.concatenate(
        [ref[...] for ref in (gain_one_ref, shift_one_ref, gain_two_ref, shift_two_ref, near_ref, far_ref)]
        + [jnp.zeros((10, refs[0].shape[1]), F32)],
        axis=0,
    )
    pieces = []
    for _ in range(3):
        piece = small.astype(BF16)
        pieces.append(piece)
        small = small - piece.astype(F32)
    for bits, ref in enumerate(refs):
        start = (ints_ref[0] ^ bits) * size
        ref[:size, :] = w_ref[pl.ds(pl.multiple_of(start, size), size), :]
        for index, piece in enumerate(pieces):
            ref[size + 32 * index : size + 32 * (index + 1), :] = piece


def reduce_side(ints_ref, first_ref, second_ref, x_oth_ref, x_own_ref, oth_ref, own_ref, w_ref, *small_refs):
    core = ints_ref[3]
    rows, size = w_ref.shape[0], first_ref.shape[1]
    for index, ref in ((core, first_ref), (1 - core, second_ref)):
        w_ref[:, pl.ds(pl.multiple_of(index * size, size), size)] = ref[:rows, :]
        for small_ref in small_refs:
            pieces = [ref[rows + 32 * piece : rows + 32 * (piece + 1), :].astype(F32) for piece in range(3)]
            small_ref[index] = (pieces[0] + (pieces[1] + pieces[2]))[:24]
    oth_ref[...] = dot32(x_oth_ref[...], w_ref[...]).astype(BF16)
    own_ref[...] = dot32(x_own_ref[...], w_ref[...])


def add_near(own_ref, near_ref, out_ref):
    out_ref[...] = (own_ref[...] + near_ref[...].astype(F32)).astype(BF16)


def add_low(near_ref, far_ref, out_ref):
    half = out_ref.shape[1]
    out_ref[...] = (far_ref[...] + near_ref[:, half:].astype(F32)).astype(BF16)


def small_row(small_ref, row):
    return jnp.concatenate([small_ref[core, row : row + 1, :] for core in range(2)], axis=1)


def first_sums(seg_count, ints_ref, part_ref, near_ref, far_ref, low_ref, sent_ref):
    line_rows = SIDE * seg_count
    mask = line_mask(line_rows, seg_count, ints_ref[0])
    total = cross = jnp.zeros((8, low_ref.shape[1]), F32)
    for line in range(SIDE):
        rows = slice(line * line_rows, (line + 1) * line_rows)
        act = part_ref[rows, :] + near_ref[rows, :].astype(F32) + far_ref[rows, :].astype(F32)
        low_ref[rows, :] = act.astype(BF16)
        kept = act * mask
        total = line_sums(kept, total)
        cross = line_sums(kept * act, cross)
    send_sums(sent_ref, total, cross)


def conv_forward(
    seg_count, ints_ref, floats_ref, own_ref, oth_ref, got_ref, small_own_ref, small_oth_ref, w_ref,
    low_ref, sent_ref, hid_ref, cat_ref, acc_ref,
):
    line_rows = SIDE * seg_count
    half = own_ref.shape[1]
    side = ints_ref[1]
    clear_taps(cat_ref, seg_count)
    own, oth = [
        norm_rows(side_sums(got_ref, index), small_row(small_ref, 0), small_row(small_ref, 1), floats_ref[0])
        for index, small_ref in ((side, small_own_ref), (1 - side, small_oth_ref))
    ]
    average, scale, shift, _ = [jnp.concatenate(pieces, axis=1) for pieces in zip(own, oth)]
    for line in range(SIDE):
        rows = slice(line * line_rows, (line + 1) * line_rows)
        act = jnp.concatenate([own_ref[rows, :], oth_ref[rows, :]], axis=1).astype(F32)
        pre = (act - average) * scale + shift
        hid = (pre * jax.nn.sigmoid(pre)).astype(BF16)
        hid_ref[rows, :] = hid
        store_taps(cat_ref, line, hid, line_rows, seg_count)
    span = SIDE * WIDE * seg_count
    step = WIDE * seg_count
    for row_off in range(3):
        part = dot32(cat_ref[row_off * step : row_off * step + span, :], w_ref[row_off])
        if row_off == 0:
            acc_ref[...] = part
        else:
            acc_ref[...] += part
    mask = line_mask(line_rows, seg_count, ints_ref[0])
    total = cross = jnp.zeros((8, half), F32)
    for line in range(SIDE):
        rows = slice(line * line_rows, (line + 1) * line_rows)
        act = acc_ref[line * step : line * step + line_rows, :]
        low_ref[rows, :] = act.astype(BF16)
        kept = act * mask
        total = line_sums(kept, total)
        cross = line_sums(kept * act, cross)
    send_sums(sent_ref, total, cross)


def store_frames(pad_ref, line, values, line_rows, seg_count):
    start = ((line + 2) * EDGE + 2) * seg_count
    pad_ref[start : start + line_rows, :] = values


def load_frames(pad_ref, line, row_off, col_off, line_rows, seg_count):
    start = ((line + 2 + row_off) * EDGE + 2 + col_off) * seg_count
    return pad_ref[start : start + line_rows, :]


def tap_offsets():
    for index in range(9):
        yield index, index // 3 - 1, index % 3 - 1
    for index in range(9):
        yield 9 + index, 2 * (index // 3 - 1), 2 * (index % 3 - 1)


def next_mask(line_rows, seg_count, count):
    seg = seg_index(line_rows, seg_count)
    return (seg + 1 < jnp.minimum(count, seg_count)).astype(F32)


def gate_forward(
    seg_count, other, ints_ref, floats_ref, act_ref, got_ref, small_ref, gated_ref, *rest,
):
    hid_ref, gate_ref = (None, None) if other else rest[:2]
    roll_ref, pad_ref = rest[-2:]
    line_rows = SIDE * seg_count
    pad_ref[...] = jnp.zeros_like(pad_ref)
    roll_ref[...] = jnp.zeros_like(roll_ref)
    side = 1 - ints_ref[1] if other else ints_ref[1]
    sums = side_sums(got_ref, side)
    follows = next_mask(line_rows, seg_count, ints_ref[0])
    for core in range(act_ref.shape[1] // LANES):
        lanes = slice(core * LANES, (core + 1) * LANES)
        rows_for = small_ref.at[core]
        average, scale, shift, _ = norm_rows(sums[:, lanes], rows_for[2:3, :], rows_for[3:4, :], floats_ref[0])
        for line in range(SIDE):
            rows = slice(line * line_rows, (line + 1) * line_rows)
            act = act_ref[rows, lanes].astype(F32)
            pre = (act - average) * scale + shift
            roll_ref[rows, :] = pre * jax.nn.sigmoid(pre)
        for line in range(SIDE):
            first = line * line_rows
            here = roll_ref[first : first + line_rows, :]
            after = roll_ref[first + 1 : first + 1 + line_rows, :]
            store_frames(pad_ref, line, follows * (after - here), line_rows, seg_count)
        for line in range(SIDE):
            rows = slice(line * line_rows, (line + 1) * line_rows)
            total = jnp.zeros((line_rows, LANES), F32)
            for index, row_off, col_off in tap_offsets():
                kern = rows_for[4 + index : 5 + index, :]
                total += load_frames(pad_ref, line, row_off, col_off, line_rows, seg_count) * kern
            gate = jax.nn.sigmoid(total)
            hid = roll_ref[rows, :]
            gated_ref[rows, lanes] = (hid * (1.0 + gate)).astype(BF16)
            if not other:
                hid_ref[rows, lanes] = hid
                gate_ref[rows, lanes] = gate


def expand(
    seg_count, ints_ref, own_ref, oth_ref, near_own_ref, near_oth_ref, w_ref, bias_ref, act_ref, sent_ref,
):
    half = own_ref.shape[1]
    row_count = own_ref.shape[0]
    line_rows = SIDE * seg_count
    side = ints_ref[1]
    w_own = w_ref[pl.ds(pl.multiple_of(side * half, half), half), :]
    w_oth = w_ref[pl.ds(pl.multiple_of((1 - side) * half, half), half), :]
    total = cross = jnp.zeros((8, w_ref.shape[1]), F32)
    for clip, (left, right) in enumerate(((own_ref, oth_ref), (near_own_ref, near_oth_ref))):
        act_ref[clip] = dot32(left[...], w_own) + dot32(right[...], w_oth)
        mask = line_mask(line_rows, seg_count, ints_ref[2 * clip])
        for line in range(SIDE):
            act = act_ref[clip, line * line_rows : (line + 1) * line_rows, :]
            kept = act * mask
            total = line_sums(kept, total)
            cross = line_sums(kept * act, cross)
    send_sums(sent_ref, total, cross)
    sent_ref[2:3, :] = bias_ref[...]


def finish(
    seg_count, ints_ref, floats_ref, got_ref, gain_ref, shift_ref, flat_ref, act_own_ref, x_own_ref, grad_own_ref,
    act_oth_ref, x_oth_ref, grad_oth_ref, out_ref, resid_ref, pooled_ref, sent_ref,
):
    line_rows = SIDE * seg_count
    width = act_own_ref.shape[1]
    average, _, shift, inv_std = norm_rows(got_ref, gain_ref[...], shift_ref[...], floats_ref[0])
    gain = gain_ref[...]
    total = cross = jnp.zeros((8, width), F32)
    own, oth = (act_own_ref, x_own_ref, grad_own_ref), (act_oth_ref, x_oth_ref, grad_oth_ref)
    for clip, (act_ref, x_ref, grad_ref) in enumerate((own, oth)):
        place = ints_ref[3] if clip == 0 else 1 - ints_ref[3]
        mask = line_mask(line_rows, seg_count, ints_ref[2 * clip])
        flat = flat_ref[clip : clip + 1, :]
        pool = jnp.zeros((8, width), F32)
        for line in range(SIDE):
            rows = slice(line * line_rows, (line + 1) * line_rows)
            normed = (act_ref[rows, :] - average) * inv_std
            resid = x_ref[rows, :].astype(F32) + gain * normed + shift
            logistic = jax.nn.sigmoid(resid)
            output = mask * resid * logistic
            out_ref[clip, rows, :] = output.astype(BF16)
            pool = line_sums(output, pool)
            grad = (grad_ref[rows, :].astype(F32) + flat) * mask
            grad = grad * (logistic * (1.0 + resid * (1.0 - logistic)))
            resid_ref[clip, rows, :] = grad
            total = line_sums(grad, total)
            cross = line_sums(grad * normed, cross)
        out_ref.leave(clip, place)
        pooled_ref[clip : clip + 1, :] = jnp.sum(pool, axis=0, keepdims=True) * floats_ref[1 + clip]
    send_sums(sent_ref, total, cross)


def expand_backward(
    seg_count, clip, ints_ref, floats_ref, got_ref, back_ref, gain_ref, resid_ref, act_ref, w_ref,
    low_ref, *part_refs,
):
    line_rows = SIDE * seg_count
    half = w_ref.shape[0] // 2
    side = ints_ref[1]
    average, scale, _, inv_std = norm_rows(got_ref, gain_ref[...], gain_ref[...], floats_ref[0])
    back = back_ref[0:2, :] / floats_ref[0]
    mask = line_mask(line_rows, seg_count, ints_ref[2 * clip])
    for line in range(SIDE):
        rows = slice(line * line_rows, (line + 1) * line_rows)
        normed = (act_ref[rows, :] - average) * inv_std
        grad = scale * (resid_ref[rows, :] - mask * (back[0:1, :] + normed * back[1:2, :]))
        low_ref[rows, :] = grad.astype(BF16)
    for place, index in enumerate((side, 1 - side)):
        w_side = w_ref[pl.ds(pl.multiple_of(index * half, half), half), :]
        part = dot32(low_ref[...], w_side, ((1,), (1,)))
        if clip == 0:
            part_refs[place][...] = part
        else:
            part_refs[0][:, place * half : (place + 1) * half] = part.astype(BF16)


def gate_backward(
    seg_count, ints_ref, floats_ref, grad_ref, near_ref, far_ref, hid_ref, gate_ref, act_ref, got_ref, small_ref,
    logit_ref, low_ref, sent_ref, kern_grad_ref, field_ref, pad_ref, back_ref,
):
    line_rows = SIDE * seg_count
    pad_ref[...] = jnp.zeros_like(pad_ref)
    field_ref[...] = jnp.zeros_like(field_ref)
    back_ref[...] = jnp.zeros_like(back_ref)
    kern_grad_ref[...] = jnp.zeros_like(kern_grad_ref)
    side = ints_ref[1]
    sums = side_sums(got_ref, side)
    follows = next_mask(line_rows, seg_count, ints_ref[0])
    totals_all, cross_all = [], []
    for core in range(act_ref.shape[1] // LANES):
        lanes = slice(core * LANES, (core + 1) * LANES)
        rows_for = small_ref.at[core]
        average, scale, shift, inv_std = norm_rows(sums[:, lanes], rows_for[2:3, :], rows_for[3:4, :], floats_ref[0])

        def whole_grad(rows):
            return grad_ref[rows, lanes] + near_ref[rows, lanes].astype(F32) + far_ref[rows, lanes].astype(F32)

        for line in range(SIDE):
            first = line * line_rows
            rows = slice(first, first + line_rows)
            here = hid_ref[rows, lanes]
            if line < SIDE - 1:
                after = hid_ref[first + 1 : first + 1 + line_rows, lanes]
            else:
                after = jnp.concatenate([hid_ref[first + 1 : first + line_rows, lanes], here[:1, :]], axis=0)
            store_frames(pad_ref, line, follows * (after - here), line_rows, seg_count)
            gate = gate_ref[rows, lanes]
            store_frames(field_ref, line, whole_grad(rows) * here * gate * (1.0 - gate), line_rows, seg_count)
        totals = [jnp.zeros((8, LANES), F32) for _ in range(18)]
        for line in range(SIDE):
            field = load_frames(field_ref, line, 0, 0, line_rows, seg_count)
            back = jnp.zeros((line_rows, LANES), F32)
            for index, row_off, col_off in tap_offsets():
                shifted = load_frames(pad_ref, line, row_off, col_off, line_rows, seg_count)
                totals[index] = line_sums(field * shifted, totals[index])
                kern = rows_for[4 + index : 5 + index, :]
                back += load_frames(field_ref, line, -row_off, -col_off, line_rows, seg_count) * kern
            start = 8 + line * line_rows
            back_ref[start : start + line_rows, :] = follows * back
        kern_grad_ref[0:18, lanes] = jnp.concatenate(
            [jnp.sum(each, axis=0, keepdims=True) for each in totals], axis=0
        )
        total = cross = jnp.zeros((8, LANES), F32)
        for line in range(SIDE):
            first = line * line_rows
            rows = slice(first, first + line_rows)
            before = back_ref[first + 7 : first + 7 + line_rows, :]
            here = back_ref[first + 8 : first + 8 + line_rows, :]
            grad = whole_grad(rows) * (1.0 + gate_ref[rows, lanes]) + before - here
            centred = act_ref[rows, lanes].astype(F32) - average
            grad = grad * silu_slope(centred * scale + shift)
            low_ref[rows, lanes] = grad.astype(BF16)
            total = line_sums(grad, total)
            cross = line_sums(grad * (centred * inv_std), cross)
        totals_all.append(total)
        cross_all.append(cross)
    send_sums(sent_ref, jnp.concatenate(totals_all, axis=1), jnp.concatenate(cross_all, axis=1))
    for peer in range(sent_ref.shape[0]):
        sent_ref[peer, 2:4, :] = logit_ref[...]


def back_rows(got_ref, back_ref, small_ref, row, side, count):
    average, scale, shift, inv_std = norm_rows(
        side_sums(got_ref, side), small_row(small_ref, row), small_row(small_ref, row + 1), count
    )
    back = side_sums(back_ref, side) / count
    return average, inv_std, scale, back[0:1, :], back[1:2, :], shift


def conv_backward(
    seg_count, ints_ref, floats_ref, grad_ref, more_ref, act_ref, oth_ref, got_ref, back_ref, first_ref, got_one_ref,
    small_own_ref, small_oth_ref, w_ref, kern_grad_ref, low_ref, sent_ref, keep_ref, *rest,
):
    send_refs, (field_ref, cat_ref, acc_ref) = rest[:-3], rest[-3:]
    line_rows = SIDE * seg_count
    half = grad_ref.shape[1]
    step = WIDE * seg_count
    span = SIDE * step
    side = ints_ref[1]
    count = floats_ref[0]
    mask = line_mask(line_rows, seg_count, ints_ref[0])
    clear_taps(cat_ref, seg_count)
    field_ref[...] = jnp.zeros_like(field_ref)
    own = back_rows(got_ref, back_ref, small_own_ref, 2, side, count)
    oth = back_rows(got_ref, back_ref, small_oth_ref, 2, 1 - side, count)
    average, inv_std, scale, mean, mix, _ = [jnp.concatenate(pieces, axis=1) for pieces in zip(own, oth)]
    for line in range(SIDE):
        rows = slice(line * line_rows, (line + 1) * line_rows)
        act = jnp.concatenate([act_ref[rows, :], oth_ref[rows, :]], axis=1).astype(F32)
        grad = jnp.concatenate([grad_ref[rows, :], more_ref[rows, :]], axis=1).astype(F32)
        normed = (act - average) * inv_std
        low = (scale * (grad - mask * (mean + normed * mix))).astype(BF16)
        store_taps(cat_ref, line, low, line_rows, seg_count)
        field_ref[line * step : line * step + line_rows, :] = low[:, :half]
    size = half // 2
    core = ints_ref[3]
    keep_lanes, send_lanes = [pl.ds(pl.multiple_of(index * size, size), size) for index in (core, 1 - core)]
    keep_ref[:span, :] = field_ref[:, keep_lanes]
    keep_ref[span:, :] = kern_grad_ref[:, keep_lanes].astype(BF16)
    start = 0
    for ref in send_refs:
        rows = ref.shape[0]
        if start + rows <= span:
            ref[...] = field_ref[start : start + rows, send_lanes]
        else:
            ref[: span - start, :] = field_ref[start:, send_lanes]
            ref[span - start :, :] = kern_grad_ref[:, send_lanes].astype(BF16)
        start += rows
    for row_off in range(3):
        part = dot32(cat_ref[row_off * step : row_off * step + span, :], w_ref[row_off])
        if row_off == 0:
            acc_ref[...] = part
        else:
            acc_ref[...] += part
    average, scale, shift, inv_std = norm_rows(
        side_sums(got_one_ref, side), small_row(small_own_ref, 0), small_row(small_own_ref, 1), count
    )
    total = cross = jnp.zeros((8, half), F32)
    for line in range(SIDE):
        rows = slice(line * line_rows, (line + 1) * line_rows)
        centred = first_ref[rows, :].astype(F32) - average
        grad = acc_ref[line * step : line * step + line_rows, :]
        grad = grad * silu_slope(centred * scale + shift)
        low_ref[rows, :] = grad.astype(BF16)
        total = line_sums(grad, total)
        cross = line_sums(grad * (centred * inv_std), cross)
    send_sums(sent_ref, total, cross)


def split_rows(rows_ref, index, keep_ref, send_ref):
    size = keep_ref.shape[0]
    keep_ref[...] = rows_ref[pl.ds(pl.multiple_of(index * size, 16), size), :]
    send_ref[...] = rows_ref[pl.ds(pl.multiple_of((1 - index) * size, 16), size), :]


def taps_gradient(
    seg_count, ints_ref, hid_ref, field_ref, near_hid_ref, *rest,
):
    near_field_refs, (keep_ref, send_ref, taps_ref, own_ref, near_ref, sum_ref) = rest[:-6], rest[-6:]
    line_rows = SIDE * seg_count
    step = WIDE * seg_count
    span = SIDE * step
    clear_taps(taps_ref, seg_count)
    for source, turned in ((hid_ref, own_ref), (near_hid_ref, near_ref)):
        for line in range(SIDE):
            rows = slice(line * line_rows, (line + 1) * line_rows)
            store_taps(taps_ref, line, source[rows, :], line_rows, seg_count)
        for start in range(0, taps_ref.shape[1], LANES):
            turned[start : start + LANES, :] = taps_ref[:, start : start + LANES].T
    depth = taps_ref.shape[1]
    near_field = jnp.concatenate([ref[...] for ref in near_field_refs], axis=0)
    own, near = field_ref[:span, :], near_field[:span, :]
    for row_off in range(3):
        rows = slice(row_off * step, row_off * step + span)
        part = dot32(own_ref[:, rows], own) + dot32(near_ref[:, rows], near)
        sum_ref[row_off * depth : (row_off + 1) * depth, :] = part.astype(BF16)
    rest = sum_ref.shape[0] - 3 * depth
    count = field_ref.shape[0] - span
    sum_ref[3 * depth :, :] = jnp.zeros((rest, LANES), BF16)
    kern_grad = field_ref[span:, :].astype(F32) + near_field[span:, :].astype(F32)
    sum_ref[3 * depth : 3 * depth + count, :] = kern_grad.astype(BF16)
    split_rows(sum_ref, ints_ref[4], keep_ref, send_ref)


def sum_into(sum_ref, *refs):
    total = refs[0][...].astype(F32)
    for ref in refs[1:]:
        total += ref[...].astype(F32)
    sum_ref[...] = total.astype(sum_ref.dtype)


def store_blocks(ints_ref, rows_ref, refs):
    size = refs[0].shape[0]
    for bits, ref in enumerate(refs):
        start = pl.multiple_of((ints_ref[5] ^ bits) * size, 8)
        ref[...] = rows_ref[pl.ds(start, size), :].astype(ref.dtype)


def join_blocks(ints_ref, refs, out_ref):
    size = refs[0].shape[0]
    for bits, ref in enumerate(refs):
        start = pl.multiple_of((ints_ref[5] ^ bits) * size, 8)
        out_ref[pl.ds(start, size), :] = ref[...]


def sum_split(ints_ref, own_ref, got_ref, keep_ref, send_ref, sum_ref):
    sum_into(sum_ref, own_ref, got_ref)
    split_rows(sum_ref, ints_ref[4], keep_ref, send_ref)


def sum_blocks(ints_ref, own_ref, got_ref, *refs):
    sum_into(refs[-1], own_ref, got_ref)
    store_blocks(ints_ref, refs[-1], refs[:-1])


def sum_parts(*refs):
    sum_into(refs[-1], *refs[:-1])


def join_pair(ints_ref, own_ref, got_ref, out_ref):
    size = own_ref.shape[0]
    for index, ref in ((ints_ref[4], own_ref), (1 - ints_ref[4], got_ref)):
        out_ref[pl.ds(pl.multiple_of(index * size, 16), size), :] = ref[...]


def stage_one(places, ints_ref, pack_ref, pack_got_ref, reduce_ref, *refs):
    blocks, (keep_ref, send_ref, sum_ref) = refs[:places], refs[places:]
    sum_into(sum_ref, pack_ref, pack_got_ref)
    store_blocks(ints_ref, sum_ref, blocks)
    split_rows(reduce_ref, ints_ref[4], keep_ref, send_ref)


def stage_two(places, ints_ref, keep_ref, got_ref, *refs):
    pack, refs = refs[:places], refs[places:]
    outs, sum_ref = refs[:places], refs[places]
    total = pack[0][...].astype(F32)
    for ref in pack[1:]:
        total += ref[...].astype(F32)
    total = total.astype(BF16)
    sum_into(sum_ref, keep_ref, got_ref)
    rows, lanes = total.shape
    size = sum_ref.shape[0] // places
    for bits, ref in enumerate(outs):
        ref[:rows, :] = total
        start = pl.multiple_of((ints_ref[5] ^ bits) * size, 8)
        block = sum_ref[pl.ds(start, size), :].astype(BF16)
        for index in range(sum_ref.shape[1] // lanes):
            ref[rows + index * size : rows + (index + 1) * size, :] = block[:, index * lanes : (index + 1) * lanes]


def stage_three(places, rows, ints_ref, *refs):
    parts, (join_ref, columns_ref) = refs[:places], refs[places:]
    size = columns_ref.shape[1]
    for bits, ref in enumerate(parts):
        start = pl.multiple_of((ints_ref[5] ^ bits) * rows, 8)
        join_ref[pl.ds(start, rows), :] = ref[:rows, :]
    total = parts[0][rows:, :].astype(F32)
    for ref in parts[1:]:
        total += ref[rows:, :].astype(F32)
    total = total.astype(BF16)
    for place, side in enumerate((ints_ref[1], 1 - ints_ref[1])):
        for core in range(2):
            start = (2 * place + core) * size
            for clip in range(columns_ref.shape[0] // 4):
                columns_ref[clip * 4 + 2 * side + core] = total[start : start + size, :]


def join_places(ints_ref, *refs):
    join_blocks(ints_ref, refs[:-1], refs[-1])


def unpack_spatial(ints_ref, own_ref, got_ref, out_ref, near_ref, far_ref, rows_ref):
    join_pair(ints_ref, own_ref, got_ref, rows_ref)
    depth = out_ref.shape[1]
    half = depth // 2
    side = ints_ref[1]
    for tap in range(9):
        for place, index in enumerate((side, 1 - side)):
            start = tap * depth + place * half
            target = pl.ds(pl.multiple_of(index * half, half), half)
            out_ref[tap, target, :] = rows_ref[start : start + half, :].astype(F32)
    rest = rows_ref[9 * depth : 9 * depth + 32, :].astype(F32)
    near_ref[...] = rest[0:9, :]
    far_ref[...] = rest[9:18, :]


def unpack_wide(ints_ref, own_ref, got_ref, out_ref, classes_ref, rows_ref):
    join_pair(ints_ref, own_ref, got_ref, rows_ref)
    half = out_ref.shape[0] // 2
    for place, index in enumerate((ints_ref[1], 1 - ints_ref[1])):
        target = pl.ds(pl.multiple_of(index * half, half), half)
        out_ref[target, :] = rows_ref[place * half : (place + 1) * half, :].astype(F32)
    classes_ref[...] = rows_ref[2 * half :, :].astype(F32)


def last_norm(
    seg_count, ints_ref, floats_ref, grad_ref, more_ref, act_ref, oth_ref, got_ref, back_ref, small_own_ref, small_oth_ref,
    low_own_ref, low_oth_ref,
):
    line_rows = SIDE * seg_count
    side = ints_ref[1]
    mask = line_mask(line_rows, seg_count, ints_ref[0])
    half = grad_ref.shape[1]
    for place, (grads, acts) in enumerate(((grad_ref, act_ref), (more_ref, oth_ref))):
        index = side if place == 0 else 1 - side
        average, inv_std, scale, mean, mix, _ = back_rows(
            got_ref, back_ref, (small_own_ref, small_oth_ref)[place], 0, index, floats_ref[0]
        )
        for line in range(SIDE):
            rows = slice(line * line_rows, (line + 1) * line_rows)
            normed = (acts[rows, :].astype(F32) - average) * inv_std
            grad = scale * (grads[rows, :].astype(F32) - mask * (mean + normed * mix))
            (low_own_ref, low_oth_ref)[place][rows, :] = grad.astype(BF16)


def pick_rows(ints_ref, w_ref, out_ref):
    size = out_ref.shape[1]
    out_ref[...] = w_ref[:, pl.ds(pl.multiple_of((1 - ints_ref[1]) * size, size), size), :]


def join_back(ints_ref, w_ref, from_ref, pair_ref, out_ref):
    half = out_ref.shape[2]
    size = half // 2
    depth = 2 * half
    for tap in range(9):
        row_off, col = (8 - tap) // 3, (8 - tap) % 3
        own = w_ref[tap // 3, (tap % 3) * depth : (tap % 3) * depth + half, :]
        out_ref[row_off, col * depth : col * depth + half, :] = own.T
        for index, ref in ((ints_ref[3], from_ref), (1 - ints_ref[3], pair_ref)):
            start = pl.multiple_of(col * depth + half + index * size, size)
            out_ref[row_off, pl.ds(start, size), :] = ref[tap].T


def expand_gradient(
    ints_ref, own_ref, oth_ref, near_own_ref, near_oth_ref, low_ref, near_low_ref, classes_ref,
    keep_ref, send_ref, out_ref,
):
    half = own_ref.shape[1]
    for place, (first, second) in enumerate(((own_ref, near_own_ref), (oth_ref, near_oth_ref))):
        part = dot32(first[...], low_ref[...], ((0,), (0,))) + dot32(second[...], near_low_ref[...], ((0,), (0,)))
        out_ref[place * half : (place + 1) * half, :] = part.astype(BF16)
    rest = out_ref.shape[0] - 2 * half
    out_ref[2 * half :, :] = jnp.zeros((rest, out_ref.shape[1]), BF16)
    count = classes_ref.shape[0]
    out_ref[2 * half : 2 * half + count, :] = classes_ref[...].astype(BF16)
    split_rows(out_ref, ints_ref[4], keep_ref, send_ref)


def reduce_gradient(
    ints_ref, x_own_ref, own_ref, oth_ref, x_oth_ref, near_own_ref, near_oth_ref, keep_ref, send_ref, out_ref
):
    half = own_ref.shape[1]
    for place, (low, near) in enumerate(((own_ref, near_own_ref), (oth_ref, near_oth_ref))):
        part = dot32(x_own_ref[...], low[...], ((0,), (0,))) + dot32(x_oth_ref[...], near[...], ((0,), (0,)))
        out_ref[:, place * half : (place + 1) * half] = part.astype(BF16)
    split_rows(out_ref, ints_ref[4], keep_ref, send_ref)


def input_gradient(
    ints_ref, own_ref, oth_ref, w_own_ref, w_oth_ref, resid_ref, near_own_ref, near_oth_ref, out_ref
):
    core = ints_ref[3]
    w_own, w_oth = w_own_ref[...], w_oth_ref[...]
    for clip, (own, oth) in enumerate(((own_ref, oth_ref), (near_own_ref, near_oth_ref))):
        grad = dot32(own[...], w_own, ((1,), (1,))) + dot32(oth[...], w_oth, ((1,), (1,)))
        out_ref[core if clip == 0 else 1 - core] = resid_ref[clip] + grad


def per_device(
    clip_size,
    chan_size,
    frames_in,
    seg_counts,
    w_reduce,
    gain_one,
    shift_one,
    w_spatial,
    gain_two,
    shift_two,
    near_kern,
    far_kern,
    w_expand,
    gain_three,
    shift_three,
    w_classes,
    class_bias,
    out_grad,
    logit_grad,
):
    clip_count, seg_count, pixel_count, chan_local = frames_in.shape
    mid_local = w_reduce.shape[1]
    mid_width = w_spatial.shape[1]
    half = mid_width // 2
    row_count = seg_count * pixel_count
    class_count = w_classes.shape[1]
    chan_index = lax.axis_index("chan")
    clip_index = lax.axis_index("clip")
    side_index = chan_index // 2
    core_index = chan_index % 2
    everyone = clip_size * chan_size
    sds = jax.ShapeDtypeStruct

    def swap(array, bits):
        array = array.array if isinstance(array, (Near, Free)) else array
        return Free(lax.ppermute(array, "chan", [(i, i ^ bits) for i in range(chan_size)]))

    def own_first(array, index, size, axis):
        own = lax.dynamic_slice_in_dim(array, index * size, size, axis)
        oth = lax.dynamic_slice_in_dim(array, (1 - index) * size, size, axis)
        return own, oth

    def pair(own, oth):
        flip = core_index == 1
        return jnp.where(flip, oth, own), jnp.where(flip, own, oth)

    def swap_clip(array, bits):
        array = array.array if isinstance(array, (Near, Free)) else array
        return lax.ppermute(array, "clip", [(i, i ^ bits) for i in range(clip_size)])

    parity, place = clip_index % 2, clip_index // 2
    places = clip_size // 2
    groups = [list(range(first, clip_size, 2)) for first in range(2)]

    def sum_places(values):
        if places > 4:
            return lax.psum(values, "clip", axis_index_groups=groups)
        return sum([values] + [swap_clip(values, 2 * bits) for bits in range(1, places)])

    def share_all(sent):
        got = lax.all_to_all(sent, ("clip", "chan"), 0, 0)
        return Free(got.reshape((clip_size, chan_size) + sent.shape[1:]))

    def share_clip(sent):
        sent = sent.array
        return sum_places(sent + swap_clip(sent, 1))

    own_counts = lax.dynamic_slice_in_dim(seg_counts, clip_index * clip_count, clip_count)
    count_pair = jnp.concatenate(own_first(own_counts, core_index, 1, 0))
    valid_total = jnp.sum(seg_counts).astype(F32) * pixel_count
    count_scale = 1.0 / (count_pair.astype(F32) * pixel_count)
    ints = jnp.stack([count_pair[0], side_index, count_pair[1], core_index, parity, place])
    floats = jnp.concatenate([valid_total[None], count_scale])

    x_all = frames_in.transpose(0, 2, 1, 3).reshape(clip_count, row_count, chan_local)
    grad_all = out_grad.transpose(0, 2, 1, 3).reshape(clip_count, row_count, chan_local)
    x_own, x_oth = Pick(x_all, lambda ints: ints[3]), Pick(x_all, lambda ints: 1 - ints[3])
    grad_own, grad_oth = Pick(grad_all, lambda ints: ints[3]), Pick(grad_all, lambda ints: 1 - ints[3])
    half_f32, near_f32 = sds((row_count, half), F32), near((row_count, half), F32)
    half_low, near_low_half = sds((row_count, half), BF16), near((row_count, half), BF16)
    sums_shape = sds((everyone, 2, half), F32)
    pad_rows = 9 * WIDE * seg_count
    span = SIDE * WIDE * seg_count
    edge_rows = EDGE * EDGE * seg_count

    block_shape = sds((chan_local + 96, mid_local), BF16)
    chan = chan_index.astype(jnp.int32)[None]
    sent_blocks = call(split_blocks, (block_shape,) * chan_size, ints=chan)(
        w_reduce, gain_one[None], shift_one[None], gain_two[None], shift_two[None], near_kern, far_kern
    )
    got_blocks = {bits: swap(sent_blocks[bits], bits) for bits in (2, 3, 1)}

    def side_call(first, second, deps=()):
        return call(
            reduce_side,
            (
                near((row_count, half), BF16),
                near((row_count, half), F32),
                sds((chan_local, half), BF16),
                sds((2, 24, mid_local), F32),
            ),
            deps=deps,
            ints=ints,
        )(first, second, x_oth, x_own)

    oth_one, own_one, w_own_side, small_own = side_call(sent_blocks[0], got_blocks[1])
    near_one = swap(oth_one, 1)
    oth_far, own_far, w_oth_side, small_oth = side_call(got_blocks[2], got_blocks[3], (small_own,))
    far_one = swap(call(add_near, near((row_count, half), BF16))(own_far, swap(oth_far, 1)), 2)

    w_pair = jnp.concatenate(pair(w_spatial, swap(w_spatial, 1).array), axis=2)
    w_fwd_own, w_fwd_oth = own_first(w_pair, side_index, half, 1)
    w_fwd = jnp.concatenate([w_fwd_own, w_fwd_oth], axis=1).reshape(3, 3 * mid_width, half)

    act_one, sent_one = call(
        functools.partial(first_sums, seg_count), (half_low, sums_shape), deps=(w_fwd,), ints=ints,
    )(own_one, near_one, far_one)
    act_one_oth = swap(act_one, 2)
    got_one = share_all(sent_one)

    to_side = call(pick_rows, sds((9, half, mid_local), BF16), ints=ints)(w_spatial)

    act_two, sent_two, hid_one = call(
        functools.partial(conv_forward, seg_count),
        (half_low, sums_shape, sds((row_count, mid_width), BF16)),
        [pltpu.VMEM((pad_rows, 3 * mid_width), BF16), pltpu.VMEM((span, half), F32)],
        deps=(to_side,),
        ints=ints,
        floats=floats,
    )(act_one, act_one_oth, got_one, small_own, small_oth, w_fwd)
    act_two_oth = swap(act_two, 2)
    got_two = share_all(sent_two)

    def gate_call(act, other):
        return call(
            functools.partial(gate_forward, seg_count, other),
            (near_low_half,) if other else (near_low_half, near_f32, near_f32),
            [pltpu.VMEM((row_count + 8, LANES), F32), pltpu.VMEM((edge_rows, LANES), F32)],
            ints=ints,
            floats=floats,
        )(act, got_two, small_oth if other else small_own)

    gated_own, hid_two, gate = gate_call(act_two, False)
    near_own = swap(gated_own, 1)
    gated_oth = gate_call(act_two_oth, True)[0]
    near_oth = swap(gated_oth, 1)

    near_hid = swap(hid_one, 1)

    bias_row = jnp.sum(logit_grad.astype(F32), axis=0)
    bias_row = jnp.pad(bias_row, (0, chan_local - class_count))[None]
    act_three, sent_three = call(
        functools.partial(expand, seg_count),
        (near((2, row_count, chan_local), F32), near((3, chan_local), F32)),
        ints=ints,
    )(gated_own, gated_oth, near_own, near_oth, w_expand, bias_row)
    got_three = share_clip(sent_three)

    from_side = swap(to_side, 2)
    from_pair = swap(from_side, 1)


    logit_pair = jnp.concatenate(own_first(logit_grad, core_index, 1, 0))
    grad_pooled = dot32(logit_pair, w_classes, ((1,), (1,))) * count_scale[:, None]
    output, grad_resid, pooled, sent_back = call(
        functools.partial(finish, seg_count),
        (
            Early((2, row_count, chan_local), BF16, 2),
            near((2, row_count, chan_local), F32),
            near((2, chan_local), F32),
            near((2, chan_local), F32),
        ),
        deps=(from_side,),
        ints=ints,
        floats=floats,
    )(
        got_three, gain_three[None], shift_three[None], grad_pooled,
        Pick(act_three, 0), x_own, grad_own, Pick(act_three, 1), x_oth, grad_oth,
    )
    got_back = share_clip(sent_back)
    pooled = pooled.array.astype(BF16)

    def back_call(clip):
        outs = [near((row_count, chan_local), BF16)]
        if clip == 0:
            outs += [near((row_count, half), F32)] * 2
        else:
            outs += [near((row_count, mid_width), BF16)]
        return call(
            functools.partial(expand_backward, seg_count, clip), tuple(outs), ints=ints, floats=floats,
        )(got_three, got_back, gain_three[None], Pick(grad_resid, clip), Pick(act_three, clip), w_expand)

    low_three_oth, back_oth = back_call(1)
    near_back = swap(back_oth, 1)
    low_three_own, back_own, back_far = back_call(0)

    unit = 16 * clip_size
    def halves(rows, width):
        return (sds((rows // 2, width), BF16),) * 2

    def to_places(blocks):
        if places > 4:
            order = place ^ jnp.arange(places)
            sent = jnp.stack([block.array if isinstance(block, (Free, Near)) else block for block in blocks])[order]
            return list(lax.all_to_all(sent, "clip", 0, 0, axis_index_groups=groups)[order])
        return [blocks[0]] + [swap_clip(blocks[bits], 2 * bits) for bits in range(1, places)]

    def blocks_of(rows, width):
        return (sds((rows // places, width), BF16),) * places

    grad_classes = dot32(logit_pair, pooled, ((0,), (0,)))
    wide_rows = (-(-(mid_width + class_count) // unit) + 1) * unit
    wide_keep, wide_send = call(
        expand_gradient, halves(wide_rows, chan_local), [pltpu.VMEM((wide_rows, chan_local), BF16)], ints=ints,
    )(gated_own, gated_oth, near_own, near_oth, low_three_own, low_three_oth, grad_classes)

    far_back = swap(call(add_low, near_low_half, deps=())(near_back, back_far), 2)
    grad_bias = got_three[2, :class_count]
    wide_blocks = call(
        sum_blocks,
        blocks_of(wide_rows // 2, chan_local),
        [pltpu.VMEM((wide_rows // 2, chan_local), BF16)],
        deps=(grad_bias,),
        ints=ints,
    )(wide_keep, swap_clip(wide_send, 1))
    wide_got = to_places(wide_blocks)

    w_back = call(
        join_back, sds((3, 3 * mid_width, half), BF16), deps=(wide_send,), ints=ints,
    )(w_fwd, from_side, from_pair)

    logits_part = jnp.concatenate(own_first(dot32(pooled, w_classes), core_index, 1, 0))
    logits_wide = jnp.pad(logits_part, ((0, 0), (0, half - class_count)))
    slope_two, sent_back_two, kern_grad = call(
        functools.partial(gate_backward, seg_count),
        (half_low, sds((everyone, 4, half), F32), sds((32, half), F32)),
        [
            pltpu.VMEM((edge_rows, LANES), F32),
            pltpu.VMEM((edge_rows, LANES), F32),
            pltpu.VMEM((row_count + 8, LANES), F32),
        ],
        deps=(w_back,),
        ints=ints,
        floats=floats,
    )(back_own, near_back, far_back, hid_two, gate, act_two, got_two, small_own, logits_wide)
    slope_two_oth = swap(slope_two, 2)
    got_back_two = share_all(sent_back_two)
    field_rows = (span + 32,)
    slope_one_low, sent_back_one, field_keep, *field_send = call(
        functools.partial(conv_backward, seg_count),
        (half_low, sums_shape, sds((span + 32, mid_local), BF16))
        + tuple(sds((rows, mid_local), BF16) for rows in field_rows),
        [
            pltpu.VMEM((span, half), BF16),
            pltpu.VMEM((pad_rows, 3 * mid_width), BF16),
            pltpu.VMEM((span, half), F32),
        ],
        deps=(wide_blocks[0], near_hid),
        ints=ints,
        floats=floats,
    )(
        slope_two, slope_two_oth, act_two, act_two_oth.array, got_two, got_back_two, act_one, got_one,
        small_own, small_oth, w_back, kern_grad,
    )
    slope_one_oth = swap(slope_one_low, 2)
    got_back_one = share_all(sent_back_one)

    pack_rows = -(-(9 * mid_width + 32) // unit) * unit
    pack_keep, pack_pair = call(
        functools.partial(taps_gradient, seg_count),
        halves(pack_rows, mid_local),
        [pltpu.VMEM((pad_rows, 3 * mid_width), BF16)]
        + [pltpu.VMEM((3 * mid_width, pad_rows), BF16)] * 2
        + [pltpu.VMEM((pack_rows, mid_local), BF16)],
        ints=ints,
        room=40 * 1024 * 1024,
    )(hid_one, field_keep, near_hid, *[swap(each, 1) for each in field_send])

    wide_part = call(sum_parts, sds((wide_rows // clip_size, chan_local), BF16), deps=(pack_pair,))(*wide_got)

    low_pair = call(
        functools.partial(last_norm, seg_count),
        (half_low,) * 2,
        deps=(pack_pair, wide_part),
        ints=ints,
        floats=floats,
    )(slope_one_low, slope_one_oth, act_one, act_one_oth.array, got_one, got_back_one, small_own, small_oth)
    near_pair = [swap(low, 1) for low in low_pair]
    pack_other = swap_clip(pack_pair, 1)
    reduce_keep, reduce_send = call(
        reduce_gradient,
        (Loose((chan_local // 2, mid_width), BF16), Loose((chan_local // 2, mid_width), BF16)),
        [pltpu.VMEM((chan_local, mid_width), BF16)],
        ints=ints,
    )(x_own, *low_pair, x_oth, *near_pair)

    share = chan_local // clip_size
    loose_blocks = (Loose((pack_rows // clip_size, mid_local), BF16),) * places
    pack_blocks = call(
        sum_blocks,
        loose_blocks,
        [pltpu.VMEM((pack_rows // 2, mid_local), BF16)],
        deps=(reduce_send,),
        ints=ints,
    )(pack_keep, Free(pack_other))
    pack_got = to_places(pack_blocks)
    wide_join = call(
        join_places, sds((wide_rows // 2, chan_local), BF16), deps=(pack_blocks[0],), ints=ints,
    )(*[Free(each) for each in to_places([wide_part] * places)])
    wide_other = swap_clip(wide_join, 1)
    reduce_got = swap_clip(reduce_send, 1)
    part_rows = pack_rows // clip_size
    parts = call(
        functools.partial(stage_two, places),
        (Loose((part_rows + chan_size * share, mid_local), BF16),) * places,
        [pltpu.VMEM((chan_local // 2, mid_width), F32)],
        deps=(wide_join,),
        ints=ints,
    )(reduce_keep, Free(reduce_got), *[Free(each) if index else each for index, each in enumerate(pack_got)])
    parts_got = to_places(parts)
    grad_frames = call(
        input_gradient, sds((2, row_count, chan_local), F32), deps=(parts[0],), ints=ints,
    )(*low_pair, w_own_side, w_oth_side, grad_resid, *near_pair)
    pack_join, columns = call(
        functools.partial(stage_three, places, part_rows),
        (Loose((pack_rows // 2, mid_local), BF16), sds((everyone, share, mid_local), BF16)),
        deps=(wide_other, grad_frames),
        ints=ints,
    )(*[Free(each) if index else each for index, each in enumerate(parts_got)])
    pack_other = swap_clip(pack_join, 1)
    reduce_got = lax.all_to_all(columns, ("clip", "chan"), 0, 0)
    reduce_got = reduce_got.reshape(places, 2, chan_size, share, mid_local).transpose(2, 1, 0, 3, 4)
    grad_w_reduce = reduce_got.reshape(chan_size * chan_local, mid_local).astype(F32)
    grad_w_expand, classes_got = call(
        unpack_wide,
        (sds((mid_width, chan_local), F32), sds((wide_rows - mid_width, chan_local), F32)),
        [pltpu.VMEM((wide_rows, chan_local), BF16)],
        deps=(pack_join,),
        ints=ints,
    )(wide_join, Free(wide_other))
    grad_w_classes = classes_got[:class_count].T
    grad_spatial, grad_near, grad_far = call(
        unpack_spatial,
        (sds((9, mid_width, mid_local), F32),) + (sds((9, mid_local), F32),) * 2,
        [pltpu.VMEM((pack_rows, mid_local), BF16)],
        ints=ints,
    )(pack_join, Free(pack_other))

    mine = lax.dynamic_index_in_dim(got_back_two.array, clip_index, 0, keepdims=False)
    logits = jnp.sum(mine, axis=0)[2:, :class_count] + class_bias

    def own_sums(got):
        got = got.array
        sums = jnp.sum(got.reshape((clip_size, 2, 2) + got.shape[2:]), axis=(0, 2))
        sums = lax.dynamic_index_in_dim(sums, side_index, 0, keepdims=False)
        return lax.dynamic_slice_in_dim(sums[:2], core_index * mid_local, mid_local, 1)

    grads_one = own_sums(got_back_one)
    grads_two = own_sums(got_back_two)
    grads_three = got_back

    def whole(array):
        return array.reshape(2, pixel_count, seg_count, chan_local).transpose(0, 2, 1, 3)

    return (
        whole(output),
        logits,
        whole(grad_frames),
        grad_w_reduce,
        grads_one[1],
        grads_one[0],
        grad_spatial,
        grads_two[1],
        grads_two[0],
        grad_near,
        grad_far,
        grad_w_expand,
        grads_three[1],
        grads_three[0],
        grad_w_classes,
        grad_bias,
    )


def solution(mesh):
    in_specs = (
        P("clip", None, None, "chan"),
        P(),
        P(None, "chan"),
        P("chan"),
        P("chan"),
        P(None, None, "chan"),
        P("chan"),
        P("chan"),
        P(None, "chan"),
        P(None, "chan"),
        P(None, "chan"),
        P("chan"),
        P("chan"),
        P("chan", None),
        P(),
        P("clip", None, None, "chan"),
        P("clip", None),
    )
    out_specs = (
        P("clip", None, None, "chan"),
        P("clip", None),
        P("clip", None, None, "chan"),
        P(None, "chan"),
        P("chan"),
        P("chan"),
        P(None, None, "chan"),
        P("chan"),
        P("chan"),
        P(None, "chan"),
        P(None, "chan"),
        P(None, "chan"),
        P("chan"),
        P("chan"),
        P("chan", None),
        P(),
    )
    body = functools.partial(per_device, mesh.shape["clip"], mesh.shape["chan"])
    return jax.shard_map(
        body, mesh=mesh, in_specs=in_specs, out_specs=out_specs, check_vma=False
    )
```

```python
import functools

import jax
import jax.numpy as jnp
from jax import lax
from jax.experimental import pallas as pl
from jax.experimental.pallas import tpu as pltpu
from jax.sharding import PartitionSpec as P

SIDE = 7
WIDE = SIDE + 1
EDGE = SIDE + 4
EPSILON = 1e-05
LANES = 128
F32 = jnp.float32
WORK = {"taps_gradient": 20, "unpack_spatial": 20, "last_norm": 1, "stage_two": 50}
BF16 = jnp.bfloat16
VMEM_BYTES = 20 * 1024 * 1024


def silu_slope(pre_act):
    logistic = jax.nn.sigmoid(pre_act)
    return logistic * (1.0 + pre_act * (1.0 - logistic))


def seg_index(row_count, seg_count):
    return lax.broadcasted_iota(jnp.int32, (row_count, 1), 0) % seg_count


def dot32(left, right, dims=((1,), (0,))):
    return lax.dot_general(left, right, (dims, ((), ())), preferred_element_type=F32)


class Pick:
    def __init__(self, array, index):
        self.array = array
        self.index = index


class Free:
    def __init__(self, array):
        self.array = array


class Late:
    def __init__(self, array):
        self.array = array


class Early:
    def __init__(self, shape, dtype, parts):
        self.shape = shape
        self.dtype = dtype
        self.parts = parts


class Leaving:
    def __init__(self, target, ref, sems):
        self.target = target
        self.ref = ref
        self.sems = sems
        self.copies = []
        self.shape = ref.shape
        self.dtype = ref.dtype

    def __getitem__(self, index):
        return self.ref[index]

    def __setitem__(self, index, value):
        self.ref[index] = value

    def leave(self, source, target):
        copy = pltpu.make_async_copy(self.ref.at[source], self.target.at[target], self.sems.at[len(self.copies)])
        copy.start()
        self.copies.append(copy)


class Near:
    def __init__(self, array):
        self.array = array


class Loose:
    def __init__(self, shape, dtype):
        self.shape = shape
        self.dtype = dtype


class Arriving:
    def __init__(self, copy, ref):
        self.copy = copy
        self.ref = ref
        self.shape = ref.shape

    def __getitem__(self, index):
        if self.copy is not None:
            self.copy.wait()
            self.copy = None
        return self.ref[index]


def near(shape, kind):
    return pltpu.VMEM(shape, kind)


def call(body, out_shape, scratch=(), deps=(), ints=None, floats=None, room=VMEM_BYTES):
    single = not isinstance(out_shape, (tuple, list))
    shapes = (out_shape,) if single else tuple(out_shape)
    early = [isinstance(out, Early) for out in shapes]
    away = [isinstance(out, (jax.ShapeDtypeStruct, Early)) for out in shapes]
    loose = [isinstance(out, Loose) for out in shapes]
    outs = tuple(
        pltpu.HBM(out.shape, out.dtype) if far else jax.ShapeDtypeStruct(out.shape, out.dtype) if free else out
        for out, far, free in zip(shapes, away, loose)
    )
    scalars = [array for array in (ints, floats) if array is not None]
    name = getattr(body, "func", body).__name__
    work = WORK.get(name, 0)

    def bare(arg):
        while isinstance(arg, (Pick, Free, Near, Late)):
            arg = arg.array
        return arg

    def placed(arg):
        inner = arg.array if isinstance(arg, (Pick, Late)) else arg
        if isinstance(inner, Free):
            return inner.array
        if isinstance(inner, Near):
            return pltpu.with_memory_space_constraint(inner.array, pltpu.VMEM)
        return pltpu.with_memory_space_constraint(inner, pltpu.HBM)

    def run(*args):
        fetched = [
            isinstance(arg, Late) or isinstance(arg, Pick) and not isinstance(arg.array, Near) for arg in args
        ]
        buffers = [
            pltpu.VMEM(arg.array.shape[1 if isinstance(arg, Pick) else 0 :], arg.array.dtype)
            for arg, own in zip(args, fetched)
            if own
        ]
        count = len(buffers)
        for out, parts in zip(shapes, early):
            if parts:
                buffers += [pltpu.VMEM(out.shape, out.dtype), pltpu.SemaphoreType.DMA((out.parts,))]
        if count:
            buffers.append(pltpu.SemaphoreType.DMA((count,)))

        def kernel(*refs):
            first = refs[: len(scalars)]
            inputs = refs[len(scalars) : len(scalars) + len(args)]
            rest = refs[len(scalars) + len(args) + len(deps) :]
            results, local = rest[: len(outs)], rest[len(outs) : len(outs) + len(buffers)]
            rest = rest[len(outs) + len(buffers) :]
            passed = []
            for arg, ref, own in zip(args, inputs, fetched):
                if isinstance(arg, Pick):
                    ref = ref.at[arg.index if isinstance(arg.index, int) else arg.index(first[0])]
                if own:
                    place = sum(isinstance(each, Arriving) for each in passed)
                    copy = pltpu.make_async_copy(ref, local[place], local[-1].at[place])
                    copy.start()
                    ref = Arriving(copy, local[place])
                passed.append(ref)
            leaving, done = [], count
            for result, parts in zip(results, early):
                if parts:
                    result = Leaving(result, local[done], local[done + 1])
                    done += 2
                leaving.append(result)
            body(*first, *passed, *leaving, *rest)
            for result in leaving:
                if isinstance(result, Leaving):
                    for copy in result.copies:
                        copy.wait()

        kernel.__name__ = name
        anywhere = pl.BlockSpec(memory_space=pl.ANY)
        results = pl.pallas_call(
            kernel,
            out_shape=outs,
            in_specs=[SMEM] * len(scalars)
            + [anywhere if own else VMEM for own in fetched]
            + [anywhere] * len(deps),
            out_specs=[anywhere if parts else VMEM for parts in early],
            scratch_shapes=buffers + list(scratch),
            compiler_params=pltpu.CompilerParams(vmem_limit_bytes=room),
            cost_estimate=pl.CostEstimate(flops=work * 1_000_000_000, bytes_accessed=0, transcendentals=0) if work else None,
        )(*scalars, *[placed(arg) for arg in args], *[placed(dep) for dep in deps])
        results = tuple(
            result if far else Free(result) if free else Near(result)
            for result, far, free in zip(results, away, loose)
        )
        return results[0] if single else results

    return run


SMEM = pl.BlockSpec(memory_space=pltpu.SMEM)
VMEM = pl.BlockSpec(memory_space=pltpu.VMEM)


def store_taps(cat_ref, line, values, line_rows, seg_count):
    depth = values.shape[1]
    for tap in range(3):
        start = ((line + 1) * WIDE + 1 - tap) * seg_count
        cat_ref[start : start + line_rows, tap * depth : (tap + 1) * depth] = values


def line_sums(values, row_of):
    return jnp.sum(values.reshape(-1, 8, values.shape[1]), axis=0) + row_of


def clear_taps(cat_ref, seg_count):
    depth = cat_ref.shape[1] // 3
    for tap in range(3):
        lanes = slice(tap * depth, (tap + 1) * depth)
        spans = [(0, WIDE + 1 - tap), (SIDE * WIDE + WIDE - tap, cat_ref.shape[0] // seg_count)]
        spans += [((line + 1) * WIDE + WIDE - tap, (line + 1) * WIDE + WIDE + 1 - tap) for line in range(SIDE - 1)]
        for first, last in spans:
            rows = (last - first) * seg_count
            cat_ref[first * seg_count : last * seg_count, lanes] = jnp.zeros((rows, depth), cat_ref.dtype)


def send_sums(sent_ref, total, cross):
    sums = jnp.concatenate([jnp.sum(total, axis=0, keepdims=True), jnp.sum(cross, axis=0, keepdims=True)], axis=0)
    if len(sent_ref.shape) == 2:
        sent_ref[0:2, :] = sums
        return
    for peer in range(sent_ref.shape[0]):
        sent_ref[peer, 0:2, :] = sums


def side_sums(got_ref, side):
    total = jnp.zeros((2, got_ref.shape[3]), F32)
    for clip in range(got_ref.shape[0]):
        for core in range(2):
            total += got_ref[clip, side * 2 + core, 0:2, :]
    return total


def norm_rows(sums, gain_vec, shift_vec, count):
    average = sums[0:1, :] / count
    inv_std = lax.rsqrt(sums[1:2, :] / count - average * average + EPSILON)
    return average, gain_vec * inv_std, shift_vec, inv_std


def line_mask(line_rows, seg_count, count):
    return (seg_index(line_rows, seg_count) < count).astype(F32)


def split_blocks(
    ints_ref, w_ref, gain_one_ref, shift_one_ref, gain_two_ref, shift_two_ref, near_ref, far_ref, *refs
):
    size = refs[0].shape[0] - 96
    small = jnp.concatenate(
        [ref[...] for ref in (gain_one_ref, shift_one_ref, gain_two_ref, shift_two_ref, near_ref, far_ref)]
        + [jnp.zeros((10, refs[0].shape[1]), F32)],
        axis=0,
    )
    pieces = []
    for _ in range(3):
        piece = small.astype(BF16)
        pieces.append(piece)
        small = small - piece.astype(F32)
    for bits, ref in enumerate(refs):
        start = (ints_ref[0] ^ bits) * size
        ref[:size, :] = w_ref[pl.ds(pl.multiple_of(start, size), size), :]
        for index, piece in enumerate(pieces):
            ref[size + 32 * index : size + 32 * (index + 1), :] = piece


def reduce_side(ints_ref, first_ref, second_ref, x_oth_ref, x_own_ref, oth_ref, own_ref, w_ref, *small_refs):
    core = ints_ref[3]
    rows, size = w_ref.shape[0], first_ref.shape[1]
    for index, ref in ((core, first_ref), (1 - core, second_ref)):
        w_ref[:, pl.ds(pl.multiple_of(index * size, size), size)] = ref[:rows, :]
        for small_ref in small_refs:
            pieces = [ref[rows + 32 * piece : rows + 32 * (piece + 1), :].astype(F32) for piece in range(3)]
            small_ref[index] = (pieces[0] + (pieces[1] + pieces[2]))[:24]
    oth_ref[...] = dot32(x_oth_ref[...], w_ref[...]).astype(BF16)
    own_ref[...] = dot32(x_own_ref[...], w_ref[...])


def add_near(own_ref, near_ref, out_ref):
    out_ref[...] = (own_ref[...] + near_ref[...].astype(F32)).astype(BF16)


def add_low(near_ref, far_ref, out_ref):
    half = out_ref.shape[1]
    out_ref[...] = (far_ref[...] + near_ref[:, half:].astype(F32)).astype(BF16)


def small_row(small_ref, row):
    return jnp.concatenate([small_ref[core, row : row + 1, :] for core in range(2)], axis=1)


def first_sums(seg_count, ints_ref, part_ref, near_ref, far_ref, low_ref, sent_ref):
    line_rows = SIDE * seg_count
    mask = line_mask(line_rows, seg_count, ints_ref[0])
    total = cross = jnp.zeros((8, low_ref.shape[1]), F32)
    for line in range(SIDE):
        rows = slice(line * line_rows, (line + 1) * line_rows)
        act = part_ref[rows, :] + near_ref[rows, :].astype(F32) + far_ref[rows, :].astype(F32)
        low_ref[rows, :] = act.astype(BF16)
        kept = act * mask
        total = line_sums(kept, total)
        cross = line_sums(kept * act, cross)
    send_sums(sent_ref, total, cross)


def conv_forward(
    seg_count, ints_ref, floats_ref, own_ref, oth_ref, got_ref, small_own_ref, small_oth_ref, w_ref,
    low_ref, sent_ref, hid_ref, cat_ref, acc_ref,
):
    line_rows = SIDE * seg_count
    half = own_ref.shape[1]
    side = ints_ref[1]
    clear_taps(cat_ref, seg_count)
    own, oth = [
        norm_rows(side_sums(got_ref, index), small_row(small_ref, 0), small_row(small_ref, 1), floats_ref[0])
        for index, small_ref in ((side, small_own_ref), (1 - side, small_oth_ref))
    ]
    average, scale, shift, _ = [jnp.concatenate(pieces, axis=1) for pieces in zip(own, oth)]
    for line in range(SIDE):
        rows = slice(line * line_rows, (line + 1) * line_rows)
        act = jnp.concatenate([own_ref[rows, :], oth_ref[rows, :]], axis=1).astype(F32)
        pre = (act - average) * scale + shift
        hid = (pre * jax.nn.sigmoid(pre)).astype(BF16)
        hid_ref[rows, :] = hid
        store_taps(cat_ref, line, hid, line_rows, seg_count)
    span = SIDE * WIDE * seg_count
    step = WIDE * seg_count
    for row_off in range(3):
        part = dot32(cat_ref[row_off * step : row_off * step + span, :], w_ref[row_off])
        if row_off == 0:
            acc_ref[...] = part
        else:
            acc_ref[...] += part
    mask = line_mask(line_rows, seg_count, ints_ref[0])
    total = cross = jnp.zeros((8, half), F32)
    for line in range(SIDE):
        rows = slice(line * line_rows, (line + 1) * line_rows)
        act = acc_ref[line * step : line * step + line_rows, :]
        low_ref[rows, :] = act.astype(BF16)
        kept = act * mask
        total = line_sums(kept, total)
        cross = line_sums(kept * act, cross)
    send_sums(sent_ref, total, cross)


def store_frames(pad_ref, line, values, line_rows, seg_count):
    start = ((line + 2) * EDGE + 2) * seg_count
    pad_ref[start : start + line_rows, :] = values


def load_frames(pad_ref, line, row_off, col_off, line_rows, seg_count):
    start = ((line + 2 + row_off) * EDGE + 2 + col_off) * seg_count
    return pad_ref[start : start + line_rows, :]


def tap_offsets():
    for index in range(9):
        yield index, index // 3 - 1, index % 3 - 1
    for index in range(9):
        yield 9 + index, 2 * (index // 3 - 1), 2 * (index % 3 - 1)


def next_mask(line_rows, seg_count, count):
    seg = seg_index(line_rows, seg_count)
    return (seg + 1 < jnp.minimum(count, seg_count)).astype(F32)


def gate_forward(
    seg_count, other, ints_ref, floats_ref, act_ref, got_ref, small_ref, gated_ref, *rest,
):
    hid_ref, gate_ref = (None, None) if other else rest[:2]
    roll_ref, pad_ref = rest[-2:]
    line_rows = SIDE * seg_count
    pad_ref[...] = jnp.zeros_like(pad_ref)
    roll_ref[...] = jnp.zeros_like(roll_ref)
    side = 1 - ints_ref[1] if other else ints_ref[1]
    sums = side_sums(got_ref, side)
    follows = next_mask(line_rows, seg_count, ints_ref[0])
    for core in range(act_ref.shape[1] // LANES):
        lanes = slice(core * LANES, (core + 1) * LANES)
        rows_for = small_ref.at[core]
        average, scale, shift, _ = norm_rows(sums[:, lanes], rows_for[2:3, :], rows_for[3:4, :], floats_ref[0])
        for line in range(SIDE):
            rows = slice(line * line_rows, (line + 1) * line_rows)
            act = act_ref[rows, lanes].astype(F32)
            pre = (act - average) * scale + shift
            roll_ref[rows, :] = pre * jax.nn.sigmoid(pre)
        for line in range(SIDE):
            first = line * line_rows
            here = roll_ref[first : first + line_rows, :]
            after = roll_ref[first + 1 : first + 1 + line_rows, :]
            store_frames(pad_ref, line, follows * (after - here), line_rows, seg_count)
        for line in range(SIDE):
            rows = slice(line * line_rows, (line + 1) * line_rows)
            total = jnp.zeros((line_rows, LANES), F32)
            for index, row_off, col_off in tap_offsets():
                kern = rows_for[4 + index : 5 + index, :]
                total += load_frames(pad_ref, line, row_off, col_off, line_rows, seg_count) * kern
            gate = jax.nn.sigmoid(total)
            hid = roll_ref[rows, :]
            gated_ref[rows, lanes] = (hid * (1.0 + gate)).astype(BF16)
            if not other:
                hid_ref[rows, lanes] = hid
                gate_ref[rows, lanes] = gate


def expand(
    seg_count, ints_ref, own_ref, oth_ref, near_own_ref, near_oth_ref, w_ref, bias_ref, act_ref, sent_ref,
):
    half = own_ref.shape[1]
    row_count = own_ref.shape[0]
    line_rows = SIDE * seg_count
    side = ints_ref[1]
    w_own = w_ref[pl.ds(pl.multiple_of(side * half, half), half), :]
    w_oth = w_ref[pl.ds(pl.multiple_of((1 - side) * half, half), half), :]
    total = cross = jnp.zeros((8, w_ref.shape[1]), F32)
    for clip, (left, right) in enumerate(((own_ref, oth_ref), (near_own_ref, near_oth_ref))):
        act_ref[clip] = dot32(left[...], w_own) + dot32(right[...], w_oth)
        mask = line_mask(line_rows, seg_count, ints_ref[2 * clip])
        for line in range(SIDE):
            act = act_ref[clip, line * line_rows : (line + 1) * line_rows, :]
            kept = act * mask
            total = line_sums(kept, total)
            cross = line_sums(kept * act, cross)
    send_sums(sent_ref, total, cross)
    sent_ref[2:3, :] = bias_ref[...]


def finish(
    seg_count, ints_ref, floats_ref, got_ref, gain_ref, shift_ref, flat_ref, act_own_ref, x_own_ref, grad_own_ref,
    act_oth_ref, x_oth_ref, grad_oth_ref, out_ref, resid_ref, pooled_ref, sent_ref,
):
    line_rows = SIDE * seg_count
    width = act_own_ref.shape[1]
    average, _, shift, inv_std = norm_rows(got_ref, gain_ref[...], shift_ref[...], floats_ref[0])
    gain = gain_ref[...]
    total = cross = jnp.zeros((8, width), F32)
    own, oth = (act_own_ref, x_own_ref, grad_own_ref), (act_oth_ref, x_oth_ref, grad_oth_ref)
    for clip, (act_ref, x_ref, grad_ref) in enumerate((own, oth)):
        place = ints_ref[3] if clip == 0 else 1 - ints_ref[3]
        mask = line_mask(line_rows, seg_count, ints_ref[2 * clip])
        flat = flat_ref[clip : clip + 1, :]
        pool = jnp.zeros((8, width), F32)
        for line in range(SIDE):
            rows = slice(line * line_rows, (line + 1) * line_rows)
            normed = (act_ref[rows, :] - average) * inv_std
            resid = x_ref[rows, :].astype(F32) + gain * normed + shift
            logistic = jax.nn.sigmoid(resid)
            output = mask * resid * logistic
            out_ref[clip, rows, :] = output.astype(BF16)
            pool = line_sums(output, pool)
            grad = (grad_ref[rows, :].astype(F32) + flat) * mask
            grad = grad * (logistic * (1.0 + resid * (1.0 - logistic)))
            resid_ref[clip, rows, :] = grad
            total = line_sums(grad, total)
            cross = line_sums(grad * normed, cross)
        out_ref.leave(clip, place)
        pooled_ref[clip : clip + 1, :] = jnp.sum(pool, axis=0, keepdims=True) * floats_ref[1 + clip]
    send_sums(sent_ref, total, cross)


def expand_backward(
    seg_count, clip, ints_ref, floats_ref, got_ref, back_ref, gain_ref, resid_ref, act_ref, w_ref,
    low_ref, *part_refs,
):
    line_rows = SIDE * seg_count
    half = w_ref.shape[0] // 2
    side = ints_ref[1]
    average, scale, _, inv_std = norm_rows(got_ref, gain_ref[...], gain_ref[...], floats_ref[0])
    back = back_ref[0:2, :] / floats_ref[0]
    mask = line_mask(line_rows, seg_count, ints_ref[2 * clip])
    for line in range(SIDE):
        rows = slice(line * line_rows, (line + 1) * line_rows)
        normed = (act_ref[rows, :] - average) * inv_std
        grad = scale * (resid_ref[rows, :] - mask * (back[0:1, :] + normed * back[1:2, :]))
        low_ref[rows, :] = grad.astype(BF16)
    for place, index in enumerate((side, 1 - side)):
        w_side = w_ref[pl.ds(pl.multiple_of(index * half, half), half), :]
        part = dot32(low_ref[...], w_side, ((1,), (1,)))
        if clip == 0:
            part_refs[place][...] = part
        else:
            part_refs[0][:, place * half : (place + 1) * half] = part.astype(BF16)


def gate_backward(
    seg_count, ints_ref, floats_ref, grad_ref, near_ref, far_ref, hid_ref, gate_ref, act_ref, got_ref, small_ref,
    logit_ref, low_ref, sent_ref, kern_grad_ref, field_ref, pad_ref, back_ref,
):
    line_rows = SIDE * seg_count
    pad_ref[...] = jnp.zeros_like(pad_ref)
    field_ref[...] = jnp.zeros_like(field_ref)
    back_ref[...] = jnp.zeros_like(back_ref)
    kern_grad_ref[...] = jnp.zeros_like(kern_grad_ref)
    side = ints_ref[1]
    sums = side_sums(got_ref, side)
    follows = next_mask(line_rows, seg_count, ints_ref[0])
    totals_all, cross_all = [], []
    for core in range(act_ref.shape[1] // LANES):
        lanes = slice(core * LANES, (core + 1) * LANES)
        rows_for = small_ref.at[core]
        average, scale, shift, inv_std = norm_rows(sums[:, lanes], rows_for[2:3, :], rows_for[3:4, :], floats_ref[0])

        def whole_grad(rows):
            return grad_ref[rows, lanes] + near_ref[rows, lanes].astype(F32) + far_ref[rows, lanes].astype(F32)

        for line in range(SIDE):
            first = line * line_rows
            rows = slice(first, first + line_rows)
            here = hid_ref[rows, lanes]
            if line < SIDE - 1:
                after = hid_ref[first + 1 : first + 1 + line_rows, lanes]
            else:
                after = jnp.concatenate([hid_ref[first + 1 : first + line_rows, lanes], here[:1, :]], axis=0)
            store_frames(pad_ref, line, follows * (after - here), line_rows, seg_count)
            gate = gate_ref[rows, lanes]
            store_frames(field_ref, line, whole_grad(rows) * here * gate * (1.0 - gate), line_rows, seg_count)
        totals = [jnp.zeros((8, LANES), F32) for _ in range(18)]
        for line in range(SIDE):
            field = load_frames(field_ref, line, 0, 0, line_rows, seg_count)
            back = jnp.zeros((line_rows, LANES), F32)
            for index, row_off, col_off in tap_offsets():
                shifted = load_frames(pad_ref, line, row_off, col_off, line_rows, seg_count)
                totals[index] = line_sums(field * shifted, totals[index])
                kern = rows_for[4 + index : 5 + index, :]
                back += load_frames(field_ref, line, -row_off, -col_off, line_rows, seg_count) * kern
            start = 8 + line * line_rows
            back_ref[start : start + line_rows, :] = follows * back
        kern_grad_ref[0:18, lanes] = jnp.concatenate(
            [jnp.sum(each, axis=0, keepdims=True) for each in totals], axis=0
        )
        total = cross = jnp.zeros((8, LANES), F32)
        for line in range(SIDE):
            first = line * line_rows
            rows = slice(first, first + line_rows)
            before = back_ref[first + 7 : first + 7 + line_rows, :]
            here = back_ref[first + 8 : first + 8 + line_rows, :]
            grad = whole_grad(rows) * (1.0 + gate_ref[rows, lanes]) + before - here
            centred = act_ref[rows, lanes].astype(F32) - average
            grad = grad * silu_slope(centred * scale + shift)
            low_ref[rows, lanes] = grad.astype(BF16)
            total = line_sums(grad, total)
            cross = line_sums(grad * (centred * inv_std), cross)
        totals_all.append(total)
        cross_all.append(cross)
    send_sums(sent_ref, jnp.concatenate(totals_all, axis=1), jnp.concatenate(cross_all, axis=1))
    for peer in range(sent_ref.shape[0]):
        sent_ref[peer, 2:4, :] = logit_ref[...]


def back_rows(got_ref, back_ref, small_ref, row, side, count):
    average, scale, shift, inv_std = norm_rows(
        side_sums(got_ref, side), small_row(small_ref, row), small_row(small_ref, row + 1), count
    )
    back = side_sums(back_ref, side) / count
    return average, inv_std, scale, back[0:1, :], back[1:2, :], shift


def conv_backward(
    seg_count, ints_ref, floats_ref, grad_ref, more_ref, act_ref, oth_ref, got_ref, back_ref, first_ref, got_one_ref,
    small_own_ref, small_oth_ref, w_ref, kern_grad_ref, low_ref, sent_ref, keep_ref, *rest,
):
    send_refs, (field_ref, cat_ref, acc_ref) = rest[:-3], rest[-3:]
    line_rows = SIDE * seg_count
    half = grad_ref.shape[1]
    step = WIDE * seg_count
    span = SIDE * step
    side = ints_ref[1]
    count = floats_ref[0]
    mask = line_mask(line_rows, seg_count, ints_ref[0])
    clear_taps(cat_ref, seg_count)
    field_ref[...] = jnp.zeros_like(field_ref)
    own = back_rows(got_ref, back_ref, small_own_ref, 2, side, count)
    oth = back_rows(got_ref, back_ref, small_oth_ref, 2, 1 - side, count)
    average, inv_std, scale, mean, mix, _ = [jnp.concatenate(pieces, axis=1) for pieces in zip(own, oth)]
    for line in range(SIDE):
        rows = slice(line * line_rows, (line + 1) * line_rows)
        act = jnp.concatenate([act_ref[rows, :], oth_ref[rows, :]], axis=1).astype(F32)
        grad = jnp.concatenate([grad_ref[rows, :], more_ref[rows, :]], axis=1).astype(F32)
        normed = (act - average) * inv_std
        low = (scale * (grad - mask * (mean + normed * mix))).astype(BF16)
        store_taps(cat_ref, line, low, line_rows, seg_count)
        field_ref[line * step : line * step + line_rows, :] = low[:, :half]
    size = half // 2
    core = ints_ref[3]
    keep_lanes, send_lanes = [pl.ds(pl.multiple_of(index * size, size), size) for index in (core, 1 - core)]
    keep_ref[:span, :] = field_ref[:, keep_lanes]
    keep_ref[span:, :] = kern_grad_ref[:, keep_lanes].astype(BF16)
    start = 0
    for ref in send_refs:
        rows = ref.shape[0]
        if start + rows <= span:
            ref[...] = field_ref[start : start + rows, send_lanes]
        else:
            ref[: span - start, :] = field_ref[start:, send_lanes]
            ref[span - start :, :] = kern_grad_ref[:, send_lanes].astype(BF16)
        start += rows
    for row_off in range(3):
        part = dot32(cat_ref[row_off * step : row_off * step + span, :], w_ref[row_off])
        if row_off == 0:
            acc_ref[...] = part
        else:
            acc_ref[...] += part
    average, scale, shift, inv_std = norm_rows(
        side_sums(got_one_ref, side), small_row(small_own_ref, 0), small_row(small_own_ref, 1), count
    )
    total = cross = jnp.zeros((8, half), F32)
    for line in range(SIDE):
        rows = slice(line * line_rows, (line + 1) * line_rows)
        centred = first_ref[rows, :].astype(F32) - average
        grad = acc_ref[line * step : line * step + line_rows, :]
        grad = grad * silu_slope(centred * scale + shift)
        low_ref[rows, :] = grad.astype(BF16)
        total = line_sums(grad, total)
        cross = line_sums(grad * (centred * inv_std), cross)
    send_sums(sent_ref, total, cross)


def split_rows(rows_ref, index, keep_ref, send_ref):
    size = keep_ref.shape[0]
    keep_ref[...] = rows_ref[pl.ds(pl.multiple_of(index * size, 16), size), :]
    send_ref[...] = rows_ref[pl.ds(pl.multiple_of((1 - index) * size, 16), size), :]


def taps_gradient(
    seg_count, ints_ref, hid_ref, field_ref, near_hid_ref, *rest,
):
    near_field_refs, (keep_ref, send_ref, taps_ref, own_ref, near_ref, sum_ref) = rest[:-6], rest[-6:]
    line_rows = SIDE * seg_count
    step = WIDE * seg_count
    span = SIDE * step
    clear_taps(taps_ref, seg_count)
    for source, turned in ((hid_ref, own_ref), (near_hid_ref, near_ref)):
        for line in range(SIDE):
            rows = slice(line * line_rows, (line + 1) * line_rows)
            store_taps(taps_ref, line, source[rows, :], line_rows, seg_count)
        for start in range(0, taps_ref.shape[1], LANES):
            turned[start : start + LANES, :] = taps_ref[:, start : start + LANES].T
    depth = taps_ref.shape[1]
    near_field = jnp.concatenate([ref[...] for ref in near_field_refs], axis=0)
    own, near = field_ref[:span, :], near_field[:span, :]
    for row_off in range(3):
        rows = slice(row_off * step, row_off * step + span)
        part = dot32(own_ref[:, rows], own) + dot32(near_ref[:, rows], near)
        sum_ref[row_off * depth : (row_off + 1) * depth, :] = part.astype(BF16)
    rest = sum_ref.shape[0] - 3 * depth
    count = field_ref.shape[0] - span
    sum_ref[3 * depth :, :] = jnp.zeros((rest, LANES), BF16)
    kern_grad = field_ref[span:, :].astype(F32) + near_field[span:, :].astype(F32)
    sum_ref[3 * depth : 3 * depth + count, :] = kern_grad.astype(BF16)
    split_rows(sum_ref, ints_ref[4], keep_ref, send_ref)


def sum_into(sum_ref, *refs):
    total = refs[0][...].astype(F32)
    for ref in refs[1:]:
        total += ref[...].astype(F32)
    sum_ref[...] = total.astype(sum_ref.dtype)


def store_blocks(ints_ref, rows_ref, refs):
    size = refs[0].shape[0]
    for bits, ref in enumerate(refs):
        start = pl.multiple_of((ints_ref[5] ^ bits) * size, 8)
        ref[...] = rows_ref[pl.ds(start, size), :].astype(ref.dtype)


def join_blocks(ints_ref, refs, out_ref):
    size = refs[0].shape[0]
    for bits, ref in enumerate(refs):
        start = pl.multiple_of((ints_ref[5] ^ bits) * size, 8)
        out_ref[pl.ds(start, size), :] = ref[...]


def sum_split(ints_ref, own_ref, got_ref, keep_ref, send_ref, sum_ref):
    sum_into(sum_ref, own_ref, got_ref)
    split_rows(sum_ref, ints_ref[4], keep_ref, send_ref)


def sum_blocks(ints_ref, own_ref, got_ref, *refs):
    sum_into(refs[-1], own_ref, got_ref)
    store_blocks(ints_ref, refs[-1], refs[:-1])


def sum_parts(*refs):
    sum_into(refs[-1], *refs[:-1])


def join_pair(ints_ref, own_ref, got_ref, out_ref):
    size = own_ref.shape[0]
    for index, ref in ((ints_ref[4], own_ref), (1 - ints_ref[4], got_ref)):
        out_ref[pl.ds(pl.multiple_of(index * size, 16), size), :] = ref[...]


def stage_one(places, ints_ref, pack_ref, pack_got_ref, reduce_ref, *refs):
    blocks, (keep_ref, send_ref, sum_ref) = refs[:places], refs[places:]
    sum_into(sum_ref, pack_ref, pack_got_ref)
    store_blocks(ints_ref, sum_ref, blocks)
    split_rows(reduce_ref, ints_ref[4], keep_ref, send_ref)


def stage_two(places, ints_ref, keep_ref, got_ref, *refs):
    pack, refs = refs[:places], refs[places:]
    outs, sum_ref = refs[:places], refs[places]
    total = pack[0][...].astype(F32)
    for ref in pack[1:]:
        total += ref[...].astype(F32)
    total = total.astype(BF16)
    sum_into(sum_ref, keep_ref, got_ref)
    rows, lanes = total.shape
    size = sum_ref.shape[0] // places
    for bits, ref in enumerate(outs):
        ref[:rows, :] = total
        start = pl.multiple_of((ints_ref[5] ^ bits) * size, 8)
        block = sum_ref[pl.ds(start, size), :].astype(BF16)
        for index in range(sum_ref.shape[1] // lanes):
            ref[rows + index * size : rows + (index + 1) * size, :] = block[:, index * lanes : (index + 1) * lanes]


def stage_three(places, rows, ints_ref, *refs):
    parts, (join_ref, columns_ref) = refs[:places], refs[places:]
    size = columns_ref.shape[1]
    for bits, ref in enumerate(parts):
        start = pl.multiple_of((ints_ref[5] ^ bits) * rows, 8)
        join_ref[pl.ds(start, rows), :] = ref[:rows, :]
    total = parts[0][rows:, :].astype(F32)
    for ref in parts[1:]:
        total += ref[rows:, :].astype(F32)
    total = total.astype(BF16)
    for place, side in enumerate((ints_ref[1], 1 - ints_ref[1])):
        for core in range(2):
            start = (2 * place + core) * size
            for clip in range(columns_ref.shape[0] // 4):
                columns_ref[clip * 4 + 2 * side + core] = total[start : start + size, :]


def join_places(ints_ref, *refs):
    join_blocks(ints_ref, refs[:-1], refs[-1])


def unpack_spatial(ints_ref, own_ref, got_ref, out_ref, near_ref, far_ref, rows_ref):
    join_pair(ints_ref, own_ref, got_ref, rows_ref)
    depth = out_ref.shape[1]
    half = depth // 2
    side = ints_ref[1]
    for tap in range(9):
        for place, index in enumerate((side, 1 - side)):
            start = tap * depth + place * half
            target = pl.ds(pl.multiple_of(index * half, half), half)
            out_ref[tap, target, :] = rows_ref[start : start + half, :].astype(F32)
    rest = rows_ref[9 * depth : 9 * depth + 32, :].astype(F32)
    near_ref[...] = rest[0:9, :]
    far_ref[...] = rest[9:18, :]


def unpack_wide(ints_ref, own_ref, got_ref, out_ref, classes_ref, rows_ref):
    join_pair(ints_ref, own_ref, got_ref, rows_ref)
    half = out_ref.shape[0] // 2
    for place, index in enumerate((ints_ref[1], 1 - ints_ref[1])):
        target = pl.ds(pl.multiple_of(index * half, half), half)
        out_ref[target, :] = rows_ref[place * half : (place + 1) * half, :].astype(F32)
    classes_ref[...] = rows_ref[2 * half :, :].astype(F32)


def last_norm(
    seg_count, ints_ref, floats_ref, grad_ref, more_ref, act_ref, oth_ref, got_ref, back_ref, small_own_ref, small_oth_ref,
    low_own_ref, low_oth_ref,
):
    line_rows = SIDE * seg_count
    side = ints_ref[1]
    mask = line_mask(line_rows, seg_count, ints_ref[0])
    half = grad_ref.shape[1]
    for place, (grads, acts) in enumerate(((grad_ref, act_ref), (more_ref, oth_ref))):
        index = side if place == 0 else 1 - side
        average, inv_std, scale, mean, mix, _ = back_rows(
            got_ref, back_ref, (small_own_ref, small_oth_ref)[place], 0, index, floats_ref[0]
        )
        for line in range(SIDE):
            rows = slice(line * line_rows, (line + 1) * line_rows)
            normed = (acts[rows, :].astype(F32) - average) * inv_std
            grad = scale * (grads[rows, :].astype(F32) - mask * (mean + normed * mix))
            (low_own_ref, low_oth_ref)[place][rows, :] = grad.astype(BF16)


def pick_rows(ints_ref, w_ref, out_ref):
    size = out_ref.shape[1]
    out_ref[...] = w_ref[:, pl.ds(pl.multiple_of((1 - ints_ref[1]) * size, size), size), :]


def join_back(ints_ref, w_ref, from_ref, pair_ref, out_ref):
    half = out_ref.shape[2]
    size = half // 2
    depth = 2 * half
    for tap in range(9):
        row_off, col = (8 - tap) // 3, (8 - tap) % 3
        own = w_ref[tap // 3, (tap % 3) * depth : (tap % 3) * depth + half, :]
        out_ref[row_off, col * depth : col * depth + half, :] = own.T
        for index, ref in ((ints_ref[3], from_ref), (1 - ints_ref[3], pair_ref)):
            start = pl.multiple_of(col * depth + half + index * size, size)
            out_ref[row_off, pl.ds(start, size), :] = ref[tap].T


def expand_gradient(
    ints_ref, own_ref, oth_ref, near_own_ref, near_oth_ref, low_ref, near_low_ref, classes_ref,
    keep_ref, send_ref, out_ref,
):
    half = own_ref.shape[1]
    for place, (first, second) in enumerate(((own_ref, near_own_ref), (oth_ref, near_oth_ref))):
        part = dot32(first[...], low_ref[...], ((0,), (0,))) + dot32(second[...], near_low_ref[...], ((0,), (0,)))
        out_ref[place * half : (place + 1) * half, :] = part.astype(BF16)
    rest = out_ref.shape[0] - 2 * half
    out_ref[2 * half :, :] = jnp.zeros((rest, out_ref.shape[1]), BF16)
    count = classes_ref.shape[0]
    out_ref[2 * half : 2 * half + count, :] = classes_ref[...].astype(BF16)
    split_rows(out_ref, ints_ref[4], keep_ref, send_ref)


def reduce_gradient(
    ints_ref, x_own_ref, own_ref, oth_ref, x_oth_ref, near_own_ref, near_oth_ref, keep_ref, send_ref, out_ref
):
    half = own_ref.shape[1]
    for place, (low, near) in enumerate(((own_ref, near_own_ref), (oth_ref, near_oth_ref))):
        part = dot32(x_own_ref[...], low[...], ((0,), (0,))) + dot32(x_oth_ref[...], near[...], ((0,), (0,)))
        out_ref[:, place * half : (place + 1) * half] = part.astype(BF16)
    split_rows(out_ref, ints_ref[4], keep_ref, send_ref)


def input_gradient(
    ints_ref, own_ref, oth_ref, w_own_ref, w_oth_ref, resid_ref, near_own_ref, near_oth_ref, out_ref
):
    core = ints_ref[3]
    w_own, w_oth = w_own_ref[...], w_oth_ref[...]
    for clip, (own, oth) in enumerate(((own_ref, oth_ref), (near_own_ref, near_oth_ref))):
        grad = dot32(own[...], w_own, ((1,), (1,))) + dot32(oth[...], w_oth, ((1,), (1,)))
        out_ref[core if clip == 0 else 1 - core] = resid_ref[clip] + grad


def per_device(
    clip_size,
    chan_size,
    frames_in,
    seg_counts,
    w_reduce,
    gain_one,
    shift_one,
    w_spatial,
    gain_two,
    shift_two,
    near_kern,
    far_kern,
    w_expand,
    gain_three,
    shift_three,
    w_classes,
    class_bias,
    out_grad,
    logit_grad,
):
    clip_count, seg_count, pixel_count, chan_local = frames_in.shape
    mid_local = w_reduce.shape[1]
    mid_width = w_spatial.shape[1]
    half = mid_width // 2
    row_count = seg_count * pixel_count
    class_count = w_classes.shape[1]
    chan_index = lax.axis_index("chan")
    clip_index = lax.axis_index("clip")
    side_index = chan_index // 2
    core_index = chan_index % 2
    everyone = clip_size * chan_size
    sds = jax.ShapeDtypeStruct

    def swap(array, bits):
        array = array.array if isinstance(array, (Near, Free)) else array
        return Free(lax.ppermute(array, "chan", [(i, i ^ bits) for i in range(chan_size)]))

    def own_first(array, index, size, axis):
        own = lax.dynamic_slice_in_dim(array, index * size, size, axis)
        oth = lax.dynamic_slice_in_dim(array, (1 - index) * size, size, axis)
        return own, oth

    def pair(own, oth):
        flip = core_index == 1
        return jnp.where(flip, oth, own), jnp.where(flip, own, oth)

    def swap_clip(array, bits):
        array = array.array if isinstance(array, (Near, Free)) else array
        return lax.ppermute(array, "clip", [(i, i ^ bits) for i in range(clip_size)])

    parity, place = clip_index % 2, clip_index // 2
    places = clip_size // 2
    groups = [list(range(first, clip_size, 2)) for first in range(2)]

    def sum_places(values):
        if places > 4:
            return lax.psum(values, "clip", axis_index_groups=groups)
        return sum([values] + [swap_clip(values, 2 * bits) for bits in range(1, places)])

    def share_all(sent):
        got = lax.all_to_all(sent, ("clip", "chan"), 0, 0)
        return Free(got.reshape((clip_size, chan_size) + sent.shape[1:]))

    def share_clip(sent):
        sent = sent.array
        return sum_places(sent + swap_clip(sent, 1))

    own_counts = lax.dynamic_slice_in_dim(seg_counts, clip_index * clip_count, clip_count)
    count_pair = jnp.concatenate(own_first(own_counts, core_index, 1, 0))
    valid_total = jnp.sum(seg_counts).astype(F32) * pixel_count
    count_scale = 1.0 / (count_pair.astype(F32) * pixel_count)
    ints = jnp.stack([count_pair[0], side_index, count_pair[1], core_index, parity, place])
    floats = jnp.concatenate([valid_total[None], count_scale])

    x_all = frames_in.transpose(0, 2, 1, 3).reshape(clip_count, row_count, chan_local)
    grad_all = out_grad.transpose(0, 2, 1, 3).reshape(clip_count, row_count, chan_local)
    x_own, x_oth = Pick(x_all, lambda ints: ints[3]), Pick(x_all, lambda ints: 1 - ints[3])
    grad_own, grad_oth = Pick(grad_all, lambda ints: ints[3]), Pick(grad_all, lambda ints: 1 - ints[3])
    half_f32, near_f32 = sds((row_count, half), F32), near((row_count, half), F32)
    half_low, near_low_half = sds((row_count, half), BF16), near((row_count, half), BF16)
    sums_shape = sds((everyone, 2, half), F32)
    pad_rows = 9 * WIDE * seg_count
    span = SIDE * WIDE * seg_count
    edge_rows = EDGE * EDGE * seg_count

    block_shape = Loose((chan_local + 96, mid_local), BF16)
    chan = chan_index.astype(jnp.int32)[None]
    sent_blocks = call(split_blocks, (block_shape,) * chan_size, ints=chan)(
        w_reduce, gain_one[None], shift_one[None], gain_two[None], shift_two[None], near_kern, far_kern
    )
    got_blocks = {bits: swap(sent_blocks[bits], bits) for bits in (2, 3, 1)}

    def side_call(first, second, deps=()):
        return call(
            reduce_side,
            (
                near((row_count, half), BF16),
                near((row_count, half), F32),
                sds((chan_local, half), BF16),
                sds((2, 24, mid_local), F32),
            ),
            deps=deps,
            ints=ints,
        )(first, second, x_oth, x_own)

    oth_one, own_one, w_own_side, small_own = side_call(sent_blocks[0], got_blocks[1])
    near_one = swap(oth_one, 1)
    oth_far, own_far, w_oth_side, small_oth = side_call(got_blocks[2], got_blocks[3], (small_own,))
    far_one = swap(call(add_near, near((row_count, half), BF16))(own_far, swap(oth_far, 1)), 2)

    w_pair = jnp.concatenate(pair(w_spatial, swap(w_spatial, 1).array), axis=2)
    w_fwd_own, w_fwd_oth = own_first(w_pair, side_index, half, 1)
    w_fwd = jnp.concatenate([w_fwd_own, w_fwd_oth], axis=1).reshape(3, 3 * mid_width, half)

    act_one, sent_one = call(
        functools.partial(first_sums, seg_count), (half_low, sums_shape), deps=(w_fwd,), ints=ints,
    )(own_one, near_one, far_one)
    act_one_oth = swap(act_one, 2)
    got_one = share_all(sent_one)

    to_side = call(pick_rows, sds((9, half, mid_local), BF16), ints=ints)(w_spatial)

    act_two, sent_two, hid_one = call(
        functools.partial(conv_forward, seg_count),
        (half_low, sums_shape, sds((row_count, mid_width), BF16)),
        [pltpu.VMEM((pad_rows, 3 * mid_width), BF16), pltpu.VMEM((span, half), F32)],
        deps=(to_side,),
        ints=ints,
        floats=floats,
    )(act_one, act_one_oth, got_one, small_own, small_oth, w_fwd)
    act_two_oth = swap(act_two, 2)
    got_two = share_all(sent_two)

    def gate_call(act, other):
        return call(
            functools.partial(gate_forward, seg_count, other),
            (near_low_half,) if other else (near_low_half, near_f32, near_f32),
            [pltpu.VMEM((row_count + 8, LANES), F32), pltpu.VMEM((edge_rows, LANES), F32)],
            ints=ints,
            floats=floats,
        )(act, got_two, small_oth if other else small_own)

    gated_own, hid_two, gate = gate_call(act_two, False)
    near_own = swap(gated_own, 1)
    gated_oth = gate_call(act_two_oth, True)[0]
    near_oth = swap(gated_oth, 1)

    near_hid = swap(hid_one, 1)

    bias_row = jnp.sum(logit_grad.astype(F32), axis=0)
    bias_row = jnp.pad(bias_row, (0, chan_local - class_count))[None]
    act_three, sent_three = call(
        functools.partial(expand, seg_count),
        (near((2, row_count, chan_local), F32), near((3, chan_local), F32)),
        ints=ints,
    )(gated_own, gated_oth, near_own, near_oth, w_expand, bias_row)
    got_three = share_clip(sent_three)

    from_side = swap(to_side, 2)
    from_pair = swap(from_side, 1)


    logit_pair = jnp.concatenate(own_first(logit_grad, core_index, 1, 0))
    grad_pooled = dot32(logit_pair, w_classes, ((1,), (1,))) * count_scale[:, None]
    output, grad_resid, pooled, sent_back = call(
        functools.partial(finish, seg_count),
        (
            Early((2, row_count, chan_local), BF16, 2),
            near((2, row_count, chan_local), F32),
            near((2, chan_local), F32),
            near((2, chan_local), F32),
        ),
        deps=(from_side,),
        ints=ints,
        floats=floats,
    )(
        got_three, gain_three[None], shift_three[None], grad_pooled,
        Pick(act_three, 0), x_own, grad_own, Pick(act_three, 1), x_oth, grad_oth,
    )
    got_back = share_clip(sent_back)
    pooled = pooled.array.astype(BF16)

    def back_call(clip):
        outs = [near((row_count, chan_local), BF16)]
        if clip == 0:
            outs += [near((row_count, half), F32)] * 2
        else:
            outs += [near((row_count, mid_width), BF16)]
        return call(
            functools.partial(expand_backward, seg_count, clip), tuple(outs), ints=ints, floats=floats,
        )(got_three, got_back, gain_three[None], Pick(grad_resid, clip), Pick(act_three, clip), w_expand)

    low_three_oth, back_oth = back_call(1)
    near_back = swap(back_oth, 1)
    low_three_own, back_own, back_far = back_call(0)

    unit = 16 * clip_size
    def halves(rows, width):
        return (sds((rows // 2, width), BF16),) * 2

    def to_places(blocks):
        if places > 4:
            order = place ^ jnp.arange(places)
            sent = jnp.stack([block.array if isinstance(block, (Free, Near)) else block for block in blocks])[order]
            return list(lax.all_to_all(sent, "clip", 0, 0, axis_index_groups=groups)[order])
        return [blocks[0]] + [swap_clip(blocks[bits], 2 * bits) for bits in range(1, places)]

    def blocks_of(rows, width):
        return (sds((rows // places, width), BF16),) * places

    grad_classes = dot32(logit_pair, pooled, ((0,), (0,)))
    wide_rows = -(-(mid_width + class_count) // unit) * unit
    wide_keep, wide_send = call(
        expand_gradient, halves(wide_rows, chan_local), [pltpu.VMEM((wide_rows, chan_local), BF16)], ints=ints,
    )(gated_own, gated_oth, near_own, near_oth, low_three_own, low_three_oth, grad_classes)

    far_back = swap(call(add_low, near_low_half, deps=())(near_back, back_far), 2)
    grad_bias = got_three[2, :class_count]
    wide_blocks = call(
        sum_blocks,
        blocks_of(wide_rows // 2, chan_local),
        [pltpu.VMEM((wide_rows // 2, chan_local), BF16)],
        deps=(grad_bias,),
        ints=ints,
    )(wide_keep, swap_clip(wide_send, 1))
    wide_got = to_places(wide_blocks)

    w_back = call(
        join_back, sds((3, 3 * mid_width, half), BF16), deps=(wide_send,), ints=ints,
    )(w_fwd, from_side, from_pair)

    logits_part = jnp.concatenate(own_first(dot32(pooled, w_classes), core_index, 1, 0))
    logits_wide = jnp.pad(logits_part, ((0, 0), (0, half - class_count)))
    slope_two, sent_back_two, kern_grad = call(
        functools.partial(gate_backward, seg_count),
        (half_low, sds((everyone, 4, half), F32), sds((32, half), F32)),
        [
            pltpu.VMEM((edge_rows, LANES), F32),
            pltpu.VMEM((edge_rows, LANES), F32),
            pltpu.VMEM((row_count + 8, LANES), F32),
        ],
        deps=(w_back,),
        ints=ints,
        floats=floats,
    )(back_own, near_back, far_back, hid_two, gate, act_two, got_two, small_own, logits_wide)
    slope_two_oth = swap(slope_two, 2)
    got_back_two = share_all(sent_back_two)
    field_rows = ((span + 32) // 48 * 16,) * 2
    field_rows += (span + 32 - sum(field_rows),)
    slope_one_low, sent_back_one, field_keep, *field_send = call(
        functools.partial(conv_backward, seg_count),
        (half_low, sums_shape, sds((span + 32, mid_local), BF16))
        + tuple(sds((rows, mid_local), BF16) for rows in field_rows),
        [
            pltpu.VMEM((span, half), BF16),
            pltpu.VMEM((pad_rows, 3 * mid_width), BF16),
            pltpu.VMEM((span, half), F32),
        ],
        deps=(wide_blocks[0], near_hid),
        ints=ints,
        floats=floats,
    )(
        slope_two, slope_two_oth, act_two, act_two_oth.array, got_two, got_back_two, act_one, got_one,
        small_own, small_oth, w_back, kern_grad,
    )
    slope_one_oth = swap(slope_one_low, 2)
    got_back_one = share_all(sent_back_one)

    pack_rows = -(-(9 * mid_width + 32) // unit) * unit
    wide_part = call(sum_parts, sds((wide_rows // clip_size, chan_local), BF16), deps=(sent_back_one,))(*wide_got)
    pack_keep, pack_pair = call(
        functools.partial(taps_gradient, seg_count),
        halves(pack_rows, mid_local),
        [pltpu.VMEM((pad_rows, 3 * mid_width), BF16)]
        + [pltpu.VMEM((3 * mid_width, pad_rows), BF16)] * 2
        + [pltpu.VMEM((pack_rows, mid_local), BF16)],
        deps=(wide_part,),
        ints=ints,
        room=40 * 1024 * 1024,
    )(hid_one, field_keep, near_hid, *[swap(each, 1) for each in field_send])


    low_pair = call(
        functools.partial(last_norm, seg_count),
        (half_low,) * 2,
        deps=(pack_pair,),
        ints=ints,
        floats=floats,
    )(slope_one_low, slope_one_oth, act_one, act_one_oth.array, got_one, got_back_one, small_own, small_oth)
    near_pair = [swap(low, 1) for low in low_pair]
    pack_other = swap_clip(pack_pair, 1)
    reduce_keep, reduce_send = call(
        reduce_gradient,
        (sds((chan_local // 2, mid_width), BF16), Loose((chan_local // 2, mid_width), BF16)),
        [pltpu.VMEM((chan_local, mid_width), BF16)],
        ints=ints,
    )(x_own, *low_pair, x_oth, *near_pair)

    share = chan_local // clip_size
    loose_blocks = (sds((pack_rows // clip_size, mid_local), BF16),) * places
    pack_blocks = call(
        sum_blocks,
        loose_blocks,
        [pltpu.VMEM((pack_rows // 2, mid_local), BF16)],
        deps=(reduce_send,),
        ints=ints,
    )(pack_keep, Free(pack_other))
    pack_got = to_places(pack_blocks)
    wide_join = call(
        join_places, sds((wide_rows // 2, chan_local), BF16), deps=(pack_blocks[0],), ints=ints,
    )(*[Free(each) for each in to_places([wide_part] * places)])
    wide_other = swap_clip(wide_join, 1)
    reduce_got = swap_clip(reduce_send, 1)
    part_rows = pack_rows // clip_size
    parts = call(
        functools.partial(stage_two, places),
        (Loose((part_rows + chan_size * share, mid_local), BF16),) * places,
        [pltpu.VMEM((chan_local // 2, mid_width), F32)],
        deps=(wide_join,),
        ints=ints,
    )(reduce_keep, Free(reduce_got), *[Free(each) if index else each for index, each in enumerate(pack_got)])
    parts_got = to_places(parts)
    grad_frames = call(
        input_gradient, sds((2, row_count, chan_local), F32), deps=(parts[0],), ints=ints,
    )(*low_pair, w_own_side, w_oth_side, grad_resid, *near_pair)
    pack_join, columns = call(
        functools.partial(stage_three, places, part_rows),
        (Loose((pack_rows // 2, mid_local), BF16), sds((everyone, share, mid_local), BF16)),
        deps=(wide_other, grad_frames),
        ints=ints,
    )(*[Free(each) if index else each for index, each in enumerate(parts_got)])
    pack_other = swap_clip(pack_join, 1)
    reduce_got = lax.all_to_all(columns, ("clip", "chan"), 0, 0)
    reduce_got = reduce_got.reshape(places, 2, chan_size, share, mid_local).transpose(2, 1, 0, 3, 4)
    grad_w_reduce = reduce_got.reshape(chan_size * chan_local, mid_local).astype(F32)
    grad_w_expand, classes_got = call(
        unpack_wide,
        (sds((mid_width, chan_local), F32), sds((wide_rows - mid_width, chan_local), F32)),
        [pltpu.VMEM((wide_rows, chan_local), BF16)],
        deps=(pack_join,),
        ints=ints,
    )(wide_join, Free(wide_other))
    grad_w_classes = classes_got[:class_count].T
    grad_spatial, grad_near, grad_far = call(
        unpack_spatial,
        (sds((9, mid_width, mid_local), F32),) + (sds((9, mid_local), F32),) * 2,
        [pltpu.VMEM((pack_rows, mid_local), BF16)],
        ints=ints,
    )(pack_join, Free(pack_other))

    mine = lax.dynamic_index_in_dim(got_back_two.array, clip_index, 0, keepdims=False)
    logits = jnp.sum(mine, axis=0)[2:, :class_count] + class_bias

    def own_sums(got):
        got = got.array
        sums = jnp.sum(got.reshape((clip_size, 2, 2) + got.shape[2:]), axis=(0, 2))
        sums = lax.dynamic_index_in_dim(sums, side_index, 0, keepdims=False)
        return lax.dynamic_slice_in_dim(sums[:2], core_index * mid_local, mid_local, 1)

    grads_one = own_sums(got_back_one)
    grads_two = own_sums(got_back_two)
    grads_three = got_back

    def whole(array):
        return array.reshape(2, pixel_count, seg_count, chan_local).transpose(0, 2, 1, 3)

    return (
        whole(output),
        logits,
        whole(grad_frames),
        grad_w_reduce,
        grads_one[1],
        grads_one[0],
        grad_spatial,
        grads_two[1],
        grads_two[0],
        grad_near,
        grad_far,
        grad_w_expand,
        grads_three[1],
        grads_three[0],
        grad_w_classes,
        grad_bias,
    )


def solution(mesh):
    in_specs = (
        P("clip", None, None, "chan"),
        P(),
        P(None, "chan"),
        P("chan"),
        P("chan"),
        P(None, None, "chan"),
        P("chan"),
        P("chan"),
        P(None, "chan"),
        P(None, "chan"),
        P(None, "chan"),
        P("chan"),
        P("chan"),
        P("chan", None),
        P(),
        P("clip", None, None, "chan"),
        P("clip", None),
    )
    out_specs = (
        P("clip", None, None, "chan"),
        P("clip", None),
        P("clip", None, None, "chan"),
        P(None, "chan"),
        P("chan"),
        P("chan"),
        P(None, None, "chan"),
        P("chan"),
        P("chan"),
        P(None, "chan"),
        P(None, "chan"),
        P(None, "chan"),
        P("chan"),
        P("chan"),
        P("chan", None),
        P(),
    )
    body = functools.partial(per_device, mesh.shape["clip"], mesh.shape["chan"])
    return jax.shard_map(
        body, mesh=mesh, in_specs=in_specs, out_specs=out_specs, check_vma=False
    )
```

```python
import functools

import jax
import jax.numpy as jnp
from jax import lax
from jax.experimental import pallas as pl
from jax.experimental.pallas import tpu as pltpu
from jax.sharding import PartitionSpec as P

SIDE = 7
WIDE = SIDE + 1
EDGE = SIDE + 4
EPSILON = 1e-05
LANES = 128
F32 = jnp.float32
WORK = {"taps_gradient": 20, "unpack_spatial": 20, "last_norm": 1, "stage_two": 50}
BF16 = jnp.bfloat16
VMEM_BYTES = 20 * 1024 * 1024


def silu_slope(pre_act):
    logistic = jax.nn.sigmoid(pre_act)
    return logistic * (1.0 + pre_act * (1.0 - logistic))


def seg_index(row_count, seg_count):
    return lax.broadcasted_iota(jnp.int32, (row_count, 1), 0) % seg_count


def dot32(left, right, dims=((1,), (0,))):
    return lax.dot_general(left, right, (dims, ((), ())), preferred_element_type=F32)


class Pick:
    def __init__(self, array, index):
        self.array = array
        self.index = index


class Free:
    def __init__(self, array):
        self.array = array


class Late:
    def __init__(self, array):
        self.array = array


class Early:
    def __init__(self, shape, dtype, parts):
        self.shape = shape
        self.dtype = dtype
        self.parts = parts


class Leaving:
    def __init__(self, target, ref, sems):
        self.target = target
        self.ref = ref
        self.sems = sems
        self.copies = []
        self.shape = ref.shape
        self.dtype = ref.dtype

    def __getitem__(self, index):
        return self.ref[index]

    def __setitem__(self, index, value):
        self.ref[index] = value

    def leave(self, source, target):
        copy = pltpu.make_async_copy(self.ref.at[source], self.target.at[target], self.sems.at[len(self.copies)])
        copy.start()
        self.copies.append(copy)


class Near:
    def __init__(self, array):
        self.array = array


class Loose:
    def __init__(self, shape, dtype):
        self.shape = shape
        self.dtype = dtype


class Arriving:
    def __init__(self, copy, ref):
        self.copy = copy
        self.ref = ref
        self.shape = ref.shape

    def __getitem__(self, index):
        if self.copy is not None:
            self.copy.wait()
            self.copy = None
        return self.ref[index]


def near(shape, kind):
    return pltpu.VMEM(shape, kind)


def call(body, out_shape, scratch=(), deps=(), ints=None, floats=None, room=VMEM_BYTES):
    single = not isinstance(out_shape, (tuple, list))
    shapes = (out_shape,) if single else tuple(out_shape)
    early = [isinstance(out, Early) for out in shapes]
    away = [isinstance(out, (jax.ShapeDtypeStruct, Early)) for out in shapes]
    loose = [isinstance(out, Loose) for out in shapes]
    outs = tuple(
        pltpu.HBM(out.shape, out.dtype) if far else jax.ShapeDtypeStruct(out.shape, out.dtype) if free else out
        for out, far, free in zip(shapes, away, loose)
    )
    scalars = [array for array in (ints, floats) if array is not None]
    name = getattr(body, "func", body).__name__
    work = WORK.get(name, 0)

    def bare(arg):
        while isinstance(arg, (Pick, Free, Near, Late)):
            arg = arg.array
        return arg

    def placed(arg):
        inner = arg.array if isinstance(arg, (Pick, Late)) else arg
        if isinstance(inner, Free):
            return inner.array
        if isinstance(inner, Near):
            return pltpu.with_memory_space_constraint(inner.array, pltpu.VMEM)
        return pltpu.with_memory_space_constraint(inner, pltpu.HBM)

    def run(*args):
        fetched = [
            isinstance(arg, Late) or isinstance(arg, Pick) and not isinstance(arg.array, Near) for arg in args
        ]
        buffers = [
            pltpu.VMEM(arg.array.shape[1 if isinstance(arg, Pick) else 0 :], arg.array.dtype)
            for arg, own in zip(args, fetched)
            if own
        ]
        count = len(buffers)
        for out, parts in zip(shapes, early):
            if parts:
                buffers += [pltpu.VMEM(out.shape, out.dtype), pltpu.SemaphoreType.DMA((out.parts,))]
        if count:
            buffers.append(pltpu.SemaphoreType.DMA((count,)))

        def kernel(*refs):
            first = refs[: len(scalars)]
            inputs = refs[len(scalars) : len(scalars) + len(args)]
            rest = refs[len(scalars) + len(args) + len(deps) :]
            results, local = rest[: len(outs)], rest[len(outs) : len(outs) + len(buffers)]
            rest = rest[len(outs) + len(buffers) :]
            passed = []
            for arg, ref, own in zip(args, inputs, fetched):
                if isinstance(arg, Pick):
                    ref = ref.at[arg.index if isinstance(arg.index, int) else arg.index(first[0])]
                if own:
                    place = sum(isinstance(each, Arriving) for each in passed)
                    copy = pltpu.make_async_copy(ref, local[place], local[-1].at[place])
                    copy.start()
                    ref = Arriving(copy, local[place])
                passed.append(ref)
            leaving, done = [], count
            for result, parts in zip(results, early):
                if parts:
                    result = Leaving(result, local[done], local[done + 1])
                    done += 2
                leaving.append(result)
            body(*first, *passed, *leaving, *rest)
            for result in leaving:
                if isinstance(result, Leaving):
                    for copy in result.copies:
                        copy.wait()

        kernel.__name__ = name
        anywhere = pl.BlockSpec(memory_space=pl.ANY)
        results = pl.pallas_call(
            kernel,
            out_shape=outs,
            in_specs=[SMEM] * len(scalars)
            + [anywhere if own else VMEM for own in fetched]
            + [anywhere] * len(deps),
            out_specs=[anywhere if parts else VMEM for parts in early],
            scratch_shapes=buffers + list(scratch),
            compiler_params=pltpu.CompilerParams(vmem_limit_bytes=room),
            cost_estimate=pl.CostEstimate(flops=work * 1_000_000_000, bytes_accessed=0, transcendentals=0) if work else None,
        )(*scalars, *[placed(arg) for arg in args], *[placed(dep) for dep in deps])
        results = tuple(
            result if far else Free(result) if free else Near(result)
            for result, far, free in zip(results, away, loose)
        )
        return results[0] if single else results

    return run


SMEM = pl.BlockSpec(memory_space=pltpu.SMEM)
VMEM = pl.BlockSpec(memory_space=pltpu.VMEM)


def store_taps(cat_ref, line, values, line_rows, seg_count):
    depth = values.shape[1]
    for tap in range(3):
        start = ((line + 1) * WIDE + 1 - tap) * seg_count
        cat_ref[start : start + line_rows, tap * depth : (tap + 1) * depth] = values


def line_sums(values, row_of):
    return jnp.sum(values.reshape(-1, 8, values.shape[1]), axis=0) + row_of


def clear_taps(cat_ref, seg_count):
    depth = cat_ref.shape[1] // 3
    for tap in range(3):
        lanes = slice(tap * depth, (tap + 1) * depth)
        spans = [(0, WIDE + 1 - tap), (SIDE * WIDE + WIDE - tap, cat_ref.shape[0] // seg_count)]
        spans += [((line + 1) * WIDE + WIDE - tap, (line + 1) * WIDE + WIDE + 1 - tap) for line in range(SIDE - 1)]
        for first, last in spans:
            rows = (last - first) * seg_count
            cat_ref[first * seg_count : last * seg_count, lanes] = jnp.zeros((rows, depth), cat_ref.dtype)


def send_sums(sent_ref, total, cross):
    sums = jnp.concatenate([jnp.sum(total, axis=0, keepdims=True), jnp.sum(cross, axis=0, keepdims=True)], axis=0)
    if len(sent_ref.shape) == 2:
        sent_ref[0:2, :] = sums
        return
    for peer in range(sent_ref.shape[0]):
        sent_ref[peer, 0:2, :] = sums


def side_sums(got_ref, side):
    total = jnp.zeros((2, got_ref.shape[3]), F32)
    for clip in range(got_ref.shape[0]):
        for core in range(2):
            total += got_ref[clip, side * 2 + core, 0:2, :]
    return total


def norm_rows(sums, gain_vec, shift_vec, count):
    average = sums[0:1, :] / count
    inv_std = lax.rsqrt(sums[1:2, :] / count - average * average + EPSILON)
    return average, gain_vec * inv_std, shift_vec, inv_std


def line_mask(line_rows, seg_count, count):
    return (seg_index(line_rows, seg_count) < count).astype(F32)


def split_blocks(
    ints_ref, w_ref, gain_one_ref, shift_one_ref, gain_two_ref, shift_two_ref, near_ref, far_ref, *refs
):
    size = refs[0].shape[0] - 96
    small = jnp.concatenate(
        [ref[...] for ref in (gain_one_ref, shift_one_ref, gain_two_ref, shift_two_ref, near_ref, far_ref)]
        + [jnp.zeros((10, refs[0].shape[1]), F32)],
        axis=0,
    )
    pieces = []
    for _ in range(3):
        piece = small.astype(BF16)
        pieces.append(piece)
        small = small - piece.astype(F32)
    for bits, ref in enumerate(refs):
        start = (ints_ref[0] ^ bits) * size
        ref[:size, :] = w_ref[pl.ds(pl.multiple_of(start, size), size), :]
        for index, piece in enumerate(pieces):
            ref[size + 32 * index : size + 32 * (index + 1), :] = piece


def reduce_side(ints_ref, first_ref, second_ref, x_oth_ref, x_own_ref, oth_ref, own_ref, w_ref, small_ref, *kept_refs):
    core = ints_ref[3]
    rows, size = w_ref.shape[0], first_ref.shape[1]
    for index, ref in ((core, first_ref), (1 - core, second_ref)):
        w_ref[:, pl.ds(pl.multiple_of(index * size, size), size)] = ref[:rows, :]
        pieces = [ref[rows + 32 * piece : rows + 32 * (piece + 1), :].astype(F32) for piece in range(3)]
        small_ref[index] = (pieces[0] + (pieces[1] + pieces[2]))[:24]
    oth_ref[...] = dot32(x_oth_ref[...], w_ref[...]).astype(BF16)
    own_ref[...] = dot32(x_own_ref[...], w_ref[...])
    for ref, kept_ref in zip((x_oth_ref, x_own_ref), kept_refs):
        kept_ref[...] = ref[...]


def add_near(own_ref, near_ref, out_ref):
    out_ref[...] = (own_ref[...] + near_ref[...].astype(F32)).astype(BF16)


def add_low(near_ref, far_ref, out_ref):
    half = out_ref.shape[1]
    out_ref[...] = (far_ref[...] + near_ref[:, half:].astype(F32)).astype(BF16)


def small_row(small_ref, row):
    return jnp.concatenate([small_ref[core, row : row + 1, :] for core in range(2)], axis=1)


def first_sums(seg_count, ints_ref, part_ref, near_ref, far_ref, low_ref, sent_ref):
    line_rows = SIDE * seg_count
    mask = line_mask(line_rows, seg_count, ints_ref[0])
    total = cross = jnp.zeros((8, low_ref.shape[1]), F32)
    for line in range(SIDE):
        rows = slice(line * line_rows, (line + 1) * line_rows)
        act = part_ref[rows, :] + near_ref[rows, :].astype(F32) + far_ref[rows, :].astype(F32)
        low_ref[rows, :] = act.astype(BF16)
        kept = act * mask
        total = line_sums(kept, total)
        cross = line_sums(kept * act, cross)
    send_sums(sent_ref, total, cross)


def conv_forward(
    seg_count, ints_ref, floats_ref, own_ref, oth_ref, got_ref, small_own_ref, small_oth_ref, w_ref,
    low_ref, sent_ref, hid_ref, cat_ref, acc_ref,
):
    line_rows = SIDE * seg_count
    half = own_ref.shape[1]
    side = ints_ref[1]
    clear_taps(cat_ref, seg_count)
    own, oth = [
        norm_rows(side_sums(got_ref, index), small_row(small_ref, 0), small_row(small_ref, 1), floats_ref[0])
        for index, small_ref in ((side, small_own_ref), (1 - side, small_oth_ref))
    ]
    average, scale, shift, _ = [jnp.concatenate(pieces, axis=1) for pieces in zip(own, oth)]
    for line in range(SIDE):
        rows = slice(line * line_rows, (line + 1) * line_rows)
        act = jnp.concatenate([own_ref[rows, :], oth_ref[rows, :]], axis=1).astype(F32)
        pre = (act - average) * scale + shift
        hid = (pre * jax.nn.sigmoid(pre)).astype(BF16)
        hid_ref[rows, :] = hid
        store_taps(cat_ref, line, hid, line_rows, seg_count)
    span = SIDE * WIDE * seg_count
    step = WIDE * seg_count
    for row_off in range(3):
        part = dot32(cat_ref[row_off * step : row_off * step + span, :], w_ref[row_off])
        if row_off == 0:
            acc_ref[...] = part
        else:
            acc_ref[...] += part
    mask = line_mask(line_rows, seg_count, ints_ref[0])
    total = cross = jnp.zeros((8, half), F32)
    for line in range(SIDE):
        rows = slice(line * line_rows, (line + 1) * line_rows)
        act = acc_ref[line * step : line * step + line_rows, :]
        low_ref[rows, :] = act.astype(BF16)
        kept = act * mask
        total = line_sums(kept, total)
        cross = line_sums(kept * act, cross)
    send_sums(sent_ref, total, cross)


def store_frames(pad_ref, line, values, line_rows, seg_count):
    start = ((line + 2) * EDGE + 2) * seg_count
    pad_ref[start : start + line_rows, :] = values


def load_frames(pad_ref, line, row_off, col_off, line_rows, seg_count):
    start = ((line + 2 + row_off) * EDGE + 2 + col_off) * seg_count
    return pad_ref[start : start + line_rows, :]


def tap_offsets():
    for index in range(9):
        yield index, index // 3 - 1, index % 3 - 1
    for index in range(9):
        yield 9 + index, 2 * (index // 3 - 1), 2 * (index % 3 - 1)


def next_mask(line_rows, seg_count, count):
    seg = seg_index(line_rows, seg_count)
    return (seg + 1 < jnp.minimum(count, seg_count)).astype(F32)


def gate_forward(
    seg_count, other, ints_ref, floats_ref, act_ref, got_ref, small_ref, gated_ref, *rest,
):
    hid_ref, gate_ref = (None, None) if other else rest[:2]
    roll_ref, pad_ref = rest[-2:]
    line_rows = SIDE * seg_count
    pad_ref[...] = jnp.zeros_like(pad_ref)
    roll_ref[...] = jnp.zeros_like(roll_ref)
    side = 1 - ints_ref[1] if other else ints_ref[1]
    sums = side_sums(got_ref, side)
    follows = next_mask(line_rows, seg_count, ints_ref[0])
    for core in range(act_ref.shape[1] // LANES):
        lanes = slice(core * LANES, (core + 1) * LANES)
        rows_for = small_ref.at[core]
        average, scale, shift, _ = norm_rows(sums[:, lanes], rows_for[2:3, :], rows_for[3:4, :], floats_ref[0])
        for line in range(SIDE):
            rows = slice(line * line_rows, (line + 1) * line_rows)
            act = act_ref[rows, lanes].astype(F32)
            pre = (act - average) * scale + shift
            roll_ref[rows, :] = pre * jax.nn.sigmoid(pre)
        for line in range(SIDE):
            first = line * line_rows
            here = roll_ref[first : first + line_rows, :]
            after = roll_ref[first + 1 : first + 1 + line_rows, :]
            store_frames(pad_ref, line, follows * (after - here), line_rows, seg_count)
        for line in range(SIDE):
            rows = slice(line * line_rows, (line + 1) * line_rows)
            total = jnp.zeros((line_rows, LANES), F32)
            for index, row_off, col_off in tap_offsets():
                kern = rows_for[4 + index : 5 + index, :]
                total += load_frames(pad_ref, line, row_off, col_off, line_rows, seg_count) * kern
            gate = jax.nn.sigmoid(total)
            hid = roll_ref[rows, :]
            gated_ref[rows, lanes] = (hid * (1.0 + gate)).astype(BF16)
            if not other:
                hid_ref[rows, lanes] = hid
                gate_ref[rows, lanes] = gate


def expand(
    seg_count, ints_ref, own_ref, oth_ref, near_own_ref, near_oth_ref, w_ref, bias_ref, act_ref, sent_ref,
):
    half = own_ref.shape[1]
    row_count = own_ref.shape[0]
    line_rows = SIDE * seg_count
    side = ints_ref[1]
    w_own = w_ref[pl.ds(pl.multiple_of(side * half, half), half), :]
    w_oth = w_ref[pl.ds(pl.multiple_of((1 - side) * half, half), half), :]
    total = cross = jnp.zeros((8, w_ref.shape[1]), F32)
    for clip, (left, right) in enumerate(((own_ref, oth_ref), (near_own_ref, near_oth_ref))):
        act_ref[clip] = dot32(left[...], w_own) + dot32(right[...], w_oth)
        mask = line_mask(line_rows, seg_count, ints_ref[2 * clip])
        for line in range(SIDE):
            act = act_ref[clip, line * line_rows : (line + 1) * line_rows, :]
            kept = act * mask
            total = line_sums(kept, total)
            cross = line_sums(kept * act, cross)
    send_sums(sent_ref, total, cross)
    sent_ref[2:3, :] = bias_ref[...]


def finish(
    seg_count, ints_ref, floats_ref, got_ref, gain_ref, shift_ref, flat_ref, act_own_ref, x_own_ref, grad_own_ref,
    act_oth_ref, x_oth_ref, grad_oth_ref, out_ref, resid_ref, pooled_ref, sent_ref,
):
    line_rows = SIDE * seg_count
    width = act_own_ref.shape[1]
    average, _, shift, inv_std = norm_rows(got_ref, gain_ref[...], shift_ref[...], floats_ref[0])
    gain = gain_ref[...]
    total = cross = jnp.zeros((8, width), F32)
    own, oth = (act_own_ref, x_own_ref, grad_own_ref), (act_oth_ref, x_oth_ref, grad_oth_ref)
    for clip, (act_ref, x_ref, grad_ref) in enumerate((own, oth)):
        place = ints_ref[3] if clip == 0 else 1 - ints_ref[3]
        mask = line_mask(line_rows, seg_count, ints_ref[2 * clip])
        flat = flat_ref[clip : clip + 1, :]
        pool = jnp.zeros((8, width), F32)
        for line in range(SIDE):
            rows = slice(line * line_rows, (line + 1) * line_rows)
            normed = (act_ref[rows, :] - average) * inv_std
            resid = x_ref[rows, :].astype(F32) + gain * normed + shift
            logistic = jax.nn.sigmoid(resid)
            output = mask * resid * logistic
            out_ref[clip, rows, :] = output.astype(BF16)
            pool = line_sums(output, pool)
            grad = (grad_ref[rows, :].astype(F32) + flat) * mask
            grad = grad * (logistic * (1.0 + resid * (1.0 - logistic)))
            resid_ref[clip, rows, :] = grad
            total = line_sums(grad, total)
            cross = line_sums(grad * normed, cross)
        out_ref.leave(clip, place)
        pooled_ref[clip : clip + 1, :] = jnp.sum(pool, axis=0, keepdims=True) * floats_ref[1 + clip]
    send_sums(sent_ref, total, cross)


def expand_backward(
    seg_count, clip, ints_ref, floats_ref, got_ref, back_ref, gain_ref, resid_ref, act_ref, w_ref,
    low_ref, *part_refs,
):
    line_rows = SIDE * seg_count
    half = w_ref.shape[0] // 2
    side = ints_ref[1]
    average, scale, _, inv_std = norm_rows(got_ref, gain_ref[...], gain_ref[...], floats_ref[0])
    back = back_ref[0:2, :] / floats_ref[0]
    mask = line_mask(line_rows, seg_count, ints_ref[2 * clip])
    for line in range(SIDE):
        rows = slice(line * line_rows, (line + 1) * line_rows)
        normed = (act_ref[rows, :] - average) * inv_std
        grad = scale * (resid_ref[rows, :] - mask * (back[0:1, :] + normed * back[1:2, :]))
        low_ref[rows, :] = grad.astype(BF16)
    for place, index in enumerate((side, 1 - side)):
        w_side = w_ref[pl.ds(pl.multiple_of(index * half, half), half), :]
        part = dot32(low_ref[...], w_side, ((1,), (1,)))
        if clip == 0:
            part_refs[place][...] = part
        else:
            part_refs[0][:, place * half : (place + 1) * half] = part.astype(BF16)


def gate_backward(
    seg_count, ints_ref, floats_ref, grad_ref, near_ref, far_ref, hid_ref, gate_ref, act_ref, got_ref, small_ref,
    logit_ref, low_ref, sent_ref, kern_grad_ref, field_ref, pad_ref, back_ref,
):
    line_rows = SIDE * seg_count
    pad_ref[...] = jnp.zeros_like(pad_ref)
    field_ref[...] = jnp.zeros_like(field_ref)
    back_ref[...] = jnp.zeros_like(back_ref)
    kern_grad_ref[...] = jnp.zeros_like(kern_grad_ref)
    side = ints_ref[1]
    sums = side_sums(got_ref, side)
    follows = next_mask(line_rows, seg_count, ints_ref[0])
    totals_all, cross_all = [], []
    for core in range(act_ref.shape[1] // LANES):
        lanes = slice(core * LANES, (core + 1) * LANES)
        rows_for = small_ref.at[core]
        average, scale, shift, inv_std = norm_rows(sums[:, lanes], rows_for[2:3, :], rows_for[3:4, :], floats_ref[0])

        def whole_grad(rows):
            return grad_ref[rows, lanes] + near_ref[rows, lanes].astype(F32) + far_ref[rows, lanes].astype(F32)

        for line in range(SIDE):
            first = line * line_rows
            rows = slice(first, first + line_rows)
            here = hid_ref[rows, lanes]
            if line < SIDE - 1:
                after = hid_ref[first + 1 : first + 1 + line_rows, lanes]
            else:
                after = jnp.concatenate([hid_ref[first + 1 : first + line_rows, lanes], here[:1, :]], axis=0)
            store_frames(pad_ref, line, follows * (after - here), line_rows, seg_count)
            gate = gate_ref[rows, lanes]
            store_frames(field_ref, line, whole_grad(rows) * here * gate * (1.0 - gate), line_rows, seg_count)
        totals = [jnp.zeros((8, LANES), F32) for _ in range(18)]
        for line in range(SIDE):
            field = load_frames(field_ref, line, 0, 0, line_rows, seg_count)
            back = jnp.zeros((line_rows, LANES), F32)
            for index, row_off, col_off in tap_offsets():
                shifted = load_frames(pad_ref, line, row_off, col_off, line_rows, seg_count)
                totals[index] = line_sums(field * shifted, totals[index])
                kern = rows_for[4 + index : 5 + index, :]
                back += load_frames(field_ref, line, -row_off, -col_off, line_rows, seg_count) * kern
            start = 8 + line * line_rows
            back_ref[start : start + line_rows, :] = follows * back
        kern_grad_ref[0:18, lanes] = jnp.concatenate(
            [jnp.sum(each, axis=0, keepdims=True) for each in totals], axis=0
        )
        total = cross = jnp.zeros((8, LANES), F32)
        for line in range(SIDE):
            first = line * line_rows
            rows = slice(first, first + line_rows)
            before = back_ref[first + 7 : first + 7 + line_rows, :]
            here = back_ref[first + 8 : first + 8 + line_rows, :]
            grad = whole_grad(rows) * (1.0 + gate_ref[rows, lanes]) + before - here
            centred = act_ref[rows, lanes].astype(F32) - average
            grad = grad * silu_slope(centred * scale + shift)
            low_ref[rows, lanes] = grad.astype(BF16)
            total = line_sums(grad, total)
            cross = line_sums(grad * (centred * inv_std), cross)
        totals_all.append(total)
        cross_all.append(cross)
    send_sums(sent_ref, jnp.concatenate(totals_all, axis=1), jnp.concatenate(cross_all, axis=1))
    for peer in range(sent_ref.shape[0]):
        sent_ref[peer, 2:4, :] = logit_ref[...]


def back_rows(got_ref, back_ref, small_ref, row, side, count):
    average, scale, shift, inv_std = norm_rows(
        side_sums(got_ref, side), small_row(small_ref, row), small_row(small_ref, row + 1), count
    )
    back = side_sums(back_ref, side) / count
    return average, inv_std, scale, back[0:1, :], back[1:2, :], shift


def conv_backward(
    seg_count, ints_ref, floats_ref, grad_ref, more_ref, act_ref, oth_ref, got_ref, back_ref, first_ref, got_one_ref,
    small_own_ref, small_oth_ref, w_ref, kern_grad_ref, low_ref, sent_ref, keep_ref, *rest,
):
    send_refs, (field_ref, cat_ref, acc_ref) = rest[:-3], rest[-3:]
    line_rows = SIDE * seg_count
    half = grad_ref.shape[1]
    step = WIDE * seg_count
    span = SIDE * step
    side = ints_ref[1]
    count = floats_ref[0]
    mask = line_mask(line_rows, seg_count, ints_ref[0])
    clear_taps(cat_ref, seg_count)
    field_ref[...] = jnp.zeros_like(field_ref)
    own = back_rows(got_ref, back_ref, small_own_ref, 2, side, count)
    oth = back_rows(got_ref, back_ref, small_oth_ref, 2, 1 - side, count)
    average, inv_std, scale, mean, mix, _ = [jnp.concatenate(pieces, axis=1) for pieces in zip(own, oth)]
    for line in range(SIDE):
        rows = slice(line * line_rows, (line + 1) * line_rows)
        act = jnp.concatenate([act_ref[rows, :], oth_ref[rows, :]], axis=1).astype(F32)
        grad = jnp.concatenate([grad_ref[rows, :], more_ref[rows, :]], axis=1).astype(F32)
        normed = (act - average) * inv_std
        low = (scale * (grad - mask * (mean + normed * mix))).astype(BF16)
        store_taps(cat_ref, line, low, line_rows, seg_count)
        field_ref[line * step : line * step + line_rows, :] = low[:, :half]
    size = half // 2
    core = ints_ref[3]
    keep_lanes, send_lanes = [pl.ds(pl.multiple_of(index * size, size), size) for index in (core, 1 - core)]
    keep_ref[:span, :] = field_ref[:, keep_lanes]
    keep_ref[span:, :] = kern_grad_ref[:, keep_lanes].astype(BF16)
    start = 0
    for ref in send_refs:
        rows = ref.shape[0]
        if start + rows <= span:
            ref[...] = field_ref[start : start + rows, send_lanes]
        else:
            ref[: span - start, :] = field_ref[start:, send_lanes]
            ref[span - start :, :] = kern_grad_ref[:, send_lanes].astype(BF16)
        start += rows
    for row_off in range(3):
        part = dot32(cat_ref[row_off * step : row_off * step + span, :], w_ref[row_off])
        if row_off == 0:
            acc_ref[...] = part
        else:
            acc_ref[...] += part
    average, scale, shift, inv_std = norm_rows(
        side_sums(got_one_ref, side), small_row(small_own_ref, 0), small_row(small_own_ref, 1), count
    )
    total = cross = jnp.zeros((8, half), F32)
    for line in range(SIDE):
        rows = slice(line * line_rows, (line + 1) * line_rows)
        centred = first_ref[rows, :].astype(F32) - average
        grad = acc_ref[line * step : line * step + line_rows, :]
        grad = grad * silu_slope(centred * scale + shift)
        low_ref[rows, :] = grad.astype(BF16)
        total = line_sums(grad, total)
        cross = line_sums(grad * (centred * inv_std), cross)
    send_sums(sent_ref, total, cross)


def split_rows(rows_ref, index, keep_ref, send_ref):
    size = keep_ref.shape[0]
    keep_ref[...] = rows_ref[pl.ds(pl.multiple_of(index * size, 16), size), :]
    send_ref[...] = rows_ref[pl.ds(pl.multiple_of((1 - index) * size, 16), size), :]


def taps_gradient(
    seg_count, ints_ref, hid_ref, field_ref, near_hid_ref, *rest,
):
    near_field_refs, (keep_ref, send_ref, taps_ref, own_ref, near_ref, sum_ref) = rest[:-6], rest[-6:]
    line_rows = SIDE * seg_count
    step = WIDE * seg_count
    span = SIDE * step
    clear_taps(taps_ref, seg_count)
    for source, turned in ((hid_ref, own_ref), (near_hid_ref, near_ref)):
        for line in range(SIDE):
            rows = slice(line * line_rows, (line + 1) * line_rows)
            store_taps(taps_ref, line, source[rows, :], line_rows, seg_count)
        for start in range(0, taps_ref.shape[1], LANES):
            turned[start : start + LANES, :] = taps_ref[:, start : start + LANES].T
    depth = taps_ref.shape[1]
    near_field = jnp.concatenate([ref[...] for ref in near_field_refs], axis=0)
    own, near = field_ref[:span, :], near_field[:span, :]
    for row_off in range(3):
        rows = slice(row_off * step, row_off * step + span)
        part = dot32(own_ref[:, rows], own) + dot32(near_ref[:, rows], near)
        sum_ref[row_off * depth : (row_off + 1) * depth, :] = part.astype(BF16)
    rest = sum_ref.shape[0] - 3 * depth
    count = field_ref.shape[0] - span
    sum_ref[3 * depth :, :] = jnp.zeros((rest, LANES), BF16)
    kern_grad = field_ref[span:, :].astype(F32) + near_field[span:, :].astype(F32)
    sum_ref[3 * depth : 3 * depth + count, :] = kern_grad.astype(BF16)
    split_rows(sum_ref, ints_ref[4], keep_ref, send_ref)


def sum_into(sum_ref, *refs):
    total = refs[0][...].astype(F32)
    for ref in refs[1:]:
        total += ref[...].astype(F32)
    sum_ref[...] = total.astype(sum_ref.dtype)


def store_blocks(ints_ref, rows_ref, refs):
    size = refs[0].shape[0]
    for bits, ref in enumerate(refs):
        start = pl.multiple_of((ints_ref[5] ^ bits) * size, 8)
        ref[...] = rows_ref[pl.ds(start, size), :].astype(ref.dtype)


def join_blocks(ints_ref, refs, out_ref):
    size = refs[0].shape[0]
    for bits, ref in enumerate(refs):
        start = pl.multiple_of((ints_ref[5] ^ bits) * size, 8)
        out_ref[pl.ds(start, size), :] = ref[...]


def sum_split(ints_ref, own_ref, got_ref, keep_ref, send_ref, sum_ref):
    sum_into(sum_ref, own_ref, got_ref)
    split_rows(sum_ref, ints_ref[4], keep_ref, send_ref)


def sum_blocks(ints_ref, own_ref, got_ref, *refs):
    sum_into(refs[-1], own_ref, got_ref)
    store_blocks(ints_ref, refs[-1], refs[:-1])


def sum_parts(*refs):
    sum_into(refs[-1], *refs[:-1])


def join_pair(ints_ref, own_ref, got_ref, out_ref):
    size = own_ref.shape[0]
    for index, ref in ((ints_ref[4], own_ref), (1 - ints_ref[4], got_ref)):
        out_ref[pl.ds(pl.multiple_of(index * size, 16), size), :] = ref[...]


def stage_one(places, ints_ref, pack_ref, pack_got_ref, reduce_ref, *refs):
    blocks, (keep_ref, send_ref, sum_ref) = refs[:places], refs[places:]
    sum_into(sum_ref, pack_ref, pack_got_ref)
    store_blocks(ints_ref, sum_ref, blocks)
    split_rows(reduce_ref, ints_ref[4], keep_ref, send_ref)


def stage_two(places, ints_ref, keep_ref, got_ref, *refs):
    pack, refs = refs[:places], refs[places:]
    outs, sum_ref = refs[:places], refs[places]
    total = pack[0][...].astype(F32)
    for ref in pack[1:]:
        total += ref[...].astype(F32)
    total = total.astype(BF16)
    sum_into(sum_ref, keep_ref, got_ref)
    rows, lanes = total.shape
    size = sum_ref.shape[0] // places
    for bits, ref in enumerate(outs):
        ref[:rows, :] = total
        start = pl.multiple_of((ints_ref[5] ^ bits) * size, 8)
        block = sum_ref[pl.ds(start, size), :].astype(BF16)
        for index in range(sum_ref.shape[1] // lanes):
            ref[rows + index * size : rows + (index + 1) * size, :] = block[:, index * lanes : (index + 1) * lanes]


def stage_three(places, rows, ints_ref, *refs):
    parts, (join_ref, columns_ref) = refs[:places], refs[places:]
    size = columns_ref.shape[1]
    for bits, ref in enumerate(parts):
        start = pl.multiple_of((ints_ref[5] ^ bits) * rows, 8)
        join_ref[pl.ds(start, rows), :] = ref[:rows, :]
    total = parts[0][rows:, :].astype(F32)
    for ref in parts[1:]:
        total += ref[rows:, :].astype(F32)
    total = total.astype(BF16)
    for place, side in enumerate((ints_ref[1], 1 - ints_ref[1])):
        for core in range(2):
            start = (2 * place + core) * size
            for clip in range(columns_ref.shape[0] // 4):
                columns_ref[clip * 4 + 2 * side + core] = total[start : start + size, :]


def join_places(ints_ref, *refs):
    join_blocks(ints_ref, refs[:-1], refs[-1])


def unpack_spatial(ints_ref, own_ref, got_ref, out_ref, near_ref, far_ref, rows_ref):
    join_pair(ints_ref, own_ref, got_ref, rows_ref)
    depth = out_ref.shape[1]
    half = depth // 2
    side = ints_ref[1]
    for tap in range(9):
        for place, index in enumerate((side, 1 - side)):
            start = tap * depth + place * half
            target = pl.ds(pl.multiple_of(index * half, half), half)
            out_ref[tap, target, :] = rows_ref[start : start + half, :].astype(F32)
    rest = rows_ref[9 * depth : 9 * depth + 32, :].astype(F32)
    near_ref[...] = rest[0:9, :]
    far_ref[...] = rest[9:18, :]


def unpack_wide(ints_ref, own_ref, got_ref, out_ref, classes_ref, rows_ref):
    join_pair(ints_ref, own_ref, got_ref, rows_ref)
    half = out_ref.shape[0] // 2
    for place, index in enumerate((ints_ref[1], 1 - ints_ref[1])):
        target = pl.ds(pl.multiple_of(index * half, half), half)
        out_ref[target, :] = rows_ref[place * half : (place + 1) * half, :].astype(F32)
    classes_ref[...] = rows_ref[2 * half :, :].astype(F32)


def last_norm(
    seg_count, ints_ref, floats_ref, grad_ref, more_ref, act_ref, oth_ref, got_ref, back_ref, small_own_ref, small_oth_ref,
    low_own_ref, low_oth_ref,
):
    line_rows = SIDE * seg_count
    side = ints_ref[1]
    mask = line_mask(line_rows, seg_count, ints_ref[0])
    half = grad_ref.shape[1]
    for place, (grads, acts) in enumerate(((grad_ref, act_ref), (more_ref, oth_ref))):
        index = side if place == 0 else 1 - side
        average, inv_std, scale, mean, mix, _ = back_rows(
            got_ref, back_ref, (small_own_ref, small_oth_ref)[place], 0, index, floats_ref[0]
        )
        for line in range(SIDE):
            rows = slice(line * line_rows, (line + 1) * line_rows)
            normed = (acts[rows, :].astype(F32) - average) * inv_std
            grad = scale * (grads[rows, :].astype(F32) - mask * (mean + normed * mix))
            (low_own_ref, low_oth_ref)[place][rows, :] = grad.astype(BF16)


def pick_rows(ints_ref, w_ref, out_ref):
    size = out_ref.shape[1]
    out_ref[...] = w_ref[:, pl.ds(pl.multiple_of((1 - ints_ref[1]) * size, size), size), :]


def join_back(ints_ref, w_ref, from_ref, pair_ref, out_ref):
    half = out_ref.shape[2]
    size = half // 2
    depth = 2 * half
    for tap in range(9):
        row_off, col = (8 - tap) // 3, (8 - tap) % 3
        own = w_ref[tap // 3, (tap % 3) * depth : (tap % 3) * depth + half, :]
        out_ref[row_off, col * depth : col * depth + half, :] = own.T
        for index, ref in ((ints_ref[3], from_ref), (1 - ints_ref[3], pair_ref)):
            start = pl.multiple_of(col * depth + half + index * size, size)
            out_ref[row_off, pl.ds(start, size), :] = ref[tap].T


def expand_gradient(
    ints_ref, own_ref, oth_ref, near_own_ref, near_oth_ref, low_ref, near_low_ref, classes_ref,
    keep_ref, send_ref, out_ref,
):
    half = own_ref.shape[1]
    for place, (first, second) in enumerate(((own_ref, near_own_ref), (oth_ref, near_oth_ref))):
        part = dot32(first[...], low_ref[...], ((0,), (0,))) + dot32(second[...], near_low_ref[...], ((0,), (0,)))
        out_ref[place * half : (place + 1) * half, :] = part.astype(BF16)
    rest = out_ref.shape[0] - 2 * half
    out_ref[2 * half :, :] = jnp.zeros((rest, out_ref.shape[1]), BF16)
    count = classes_ref.shape[0]
    out_ref[2 * half : 2 * half + count, :] = classes_ref[...].astype(BF16)
    split_rows(out_ref, ints_ref[4], keep_ref, send_ref)


def reduce_gradient(
    ints_ref, x_own_ref, own_ref, oth_ref, x_oth_ref, near_own_ref, near_oth_ref, keep_ref, send_ref, out_ref
):
    half = own_ref.shape[1]
    for place, (low, near) in enumerate(((own_ref, near_own_ref), (oth_ref, near_oth_ref))):
        part = dot32(x_own_ref[...], low[...], ((0,), (0,))) + dot32(x_oth_ref[...], near[...], ((0,), (0,)))
        out_ref[:, place * half : (place + 1) * half] = part.astype(BF16)
    split_rows(out_ref, ints_ref[4], keep_ref, send_ref)


def input_gradient(
    ints_ref, own_ref, oth_ref, w_own_ref, w_oth_ref, resid_ref, near_own_ref, near_oth_ref, out_ref
):
    core = ints_ref[3]
    w_own, w_oth = w_own_ref[...], w_oth_ref[...]
    for clip, (own, oth) in enumerate(((own_ref, oth_ref), (near_own_ref, near_oth_ref))):
        grad = dot32(own[...], w_own, ((1,), (1,))) + dot32(oth[...], w_oth, ((1,), (1,)))
        out_ref[core if clip == 0 else 1 - core] = resid_ref[clip] + grad


def per_device(
    clip_size,
    chan_size,
    frames_in,
    seg_counts,
    w_reduce,
    gain_one,
    shift_one,
    w_spatial,
    gain_two,
    shift_two,
    near_kern,
    far_kern,
    w_expand,
    gain_three,
    shift_three,
    w_classes,
    class_bias,
    out_grad,
    logit_grad,
):
    clip_count, seg_count, pixel_count, chan_local = frames_in.shape
    mid_local = w_reduce.shape[1]
    mid_width = w_spatial.shape[1]
    half = mid_width // 2
    row_count = seg_count * pixel_count
    class_count = w_classes.shape[1]
    chan_index = lax.axis_index("chan")
    clip_index = lax.axis_index("clip")
    side_index = chan_index // 2
    core_index = chan_index % 2
    everyone = clip_size * chan_size
    sds = jax.ShapeDtypeStruct

    def swap(array, bits):
        array = array.array if isinstance(array, (Near, Free)) else array
        return Free(lax.ppermute(array, "chan", [(i, i ^ bits) for i in range(chan_size)]))

    def own_first(array, index, size, axis):
        own = lax.dynamic_slice_in_dim(array, index * size, size, axis)
        oth = lax.dynamic_slice_in_dim(array, (1 - index) * size, size, axis)
        return own, oth

    def pair(own, oth):
        flip = core_index == 1
        return jnp.where(flip, oth, own), jnp.where(flip, own, oth)

    def swap_clip(array, bits):
        array = array.array if isinstance(array, (Near, Free)) else array
        return lax.ppermute(array, "clip", [(i, i ^ bits) for i in range(clip_size)])

    parity, place = clip_index % 2, clip_index // 2
    places = clip_size // 2
    groups = [list(range(first, clip_size, 2)) for first in range(2)]

    def sum_places(values):
        if places > 4:
            return lax.psum(values, "clip", axis_index_groups=groups)
        return sum([values] + [swap_clip(values, 2 * bits) for bits in range(1, places)])

    def share_all(sent):
        got = lax.all_to_all(sent, ("clip", "chan"), 0, 0)
        return Free(got.reshape((clip_size, chan_size) + sent.shape[1:]))

    def share_clip(sent):
        sent = sent.array
        return sum_places(sent + swap_clip(sent, 1))

    own_counts = lax.dynamic_slice_in_dim(seg_counts, clip_index * clip_count, clip_count)
    count_pair = jnp.concatenate(own_first(own_counts, core_index, 1, 0))
    valid_total = jnp.sum(seg_counts).astype(F32) * pixel_count
    count_scale = 1.0 / (count_pair.astype(F32) * pixel_count)
    ints = jnp.stack([count_pair[0], side_index, count_pair[1], core_index, parity, place])
    floats = jnp.concatenate([valid_total[None], count_scale])

    x_all = frames_in.transpose(0, 2, 1, 3).reshape(clip_count, row_count, chan_local)
    grad_all = out_grad.transpose(0, 2, 1, 3).reshape(clip_count, row_count, chan_local)
    x_own, x_oth = Pick(x_all, lambda ints: ints[3]), Pick(x_all, lambda ints: 1 - ints[3])
    grad_own, grad_oth = Pick(grad_all, lambda ints: ints[3]), Pick(grad_all, lambda ints: 1 - ints[3])
    half_f32, near_f32 = sds((row_count, half), F32), near((row_count, half), F32)
    half_low, near_low_half = sds((row_count, half), BF16), near((row_count, half), BF16)
    sums_shape = sds((everyone, 2, half), F32)
    pad_rows = 9 * WIDE * seg_count
    span = SIDE * WIDE * seg_count
    edge_rows = EDGE * EDGE * seg_count

    block_shape = Loose((chan_local + 96, mid_local), BF16)
    chan = chan_index.astype(jnp.int32)[None]
    sent_blocks = call(split_blocks, (block_shape,) * chan_size, ints=chan)(
        w_reduce, gain_one[None], shift_one[None], gain_two[None], shift_two[None], near_kern, far_kern
    )
    got_blocks = {bits: swap(sent_blocks[bits], bits) for bits in (2, 3, 1)}

    def side_call(first, second, frames, kept=()):
        return call(
            reduce_side,
            (
                near((row_count, half), BF16),
                near((row_count, half), F32),
                sds((chan_local, half), BF16),
                sds((2, 24, mid_local), F32),
            )
            + kept,
            ints=ints,
        )(first, second, *frames)

    kept = (near((row_count, chan_local), BF16),) * 2
    oth_one, own_one, w_own_side, small_own, *frames = side_call(sent_blocks[0], got_blocks[1], (x_oth, x_own), kept)
    near_one = swap(oth_one, 1)
    oth_far, own_far, w_oth_side, small_oth = side_call(got_blocks[2], got_blocks[3], frames)
    far_one = swap(call(add_near, near((row_count, half), BF16))(own_far, swap(oth_far, 1)), 2)

    w_pair = jnp.concatenate(pair(w_spatial, swap(w_spatial, 1).array), axis=2)
    w_fwd_own, w_fwd_oth = own_first(w_pair, side_index, half, 1)
    w_fwd = jnp.concatenate([w_fwd_own, w_fwd_oth], axis=1).reshape(3, 3 * mid_width, half)

    act_one, sent_one = call(
        functools.partial(first_sums, seg_count), (half_low, sums_shape), deps=(w_fwd,), ints=ints,
    )(own_one, near_one, far_one)
    act_one_oth = swap(act_one, 2)
    got_one = share_all(sent_one)

    to_side = call(pick_rows, sds((9, half, mid_local), BF16), ints=ints)(w_spatial)

    act_two, sent_two, hid_one = call(
        functools.partial(conv_forward, seg_count),
        (half_low, sums_shape, sds((row_count, mid_width), BF16)),
        [pltpu.VMEM((pad_rows, 3 * mid_width), BF16), pltpu.VMEM((span, half), F32)],
        deps=(to_side,),
        ints=ints,
        floats=floats,
    )(act_one, act_one_oth, got_one, small_own, small_oth, w_fwd)
    act_two_oth = swap(act_two, 2)
    got_two = share_all(sent_two)

    def gate_call(act, other):
        return call(
            functools.partial(gate_forward, seg_count, other),
            (near_low_half,) if other else (near_low_half, near_f32, near_f32),
            [pltpu.VMEM((row_count + 8, LANES), F32), pltpu.VMEM((edge_rows, LANES), F32)],
            ints=ints,
            floats=floats,
        )(act, got_two, small_oth if other else small_own)

    gated_own, hid_two, gate = gate_call(act_two, False)
    near_own = swap(gated_own, 1)
    gated_oth = gate_call(act_two_oth, True)[0]
    near_oth = swap(gated_oth, 1)

    near_hid = swap(hid_one, 1)

    bias_row = jnp.sum(logit_grad.astype(F32), axis=0)
    bias_row = jnp.pad(bias_row, (0, chan_local - class_count))[None]
    act_three, sent_three = call(
        functools.partial(expand, seg_count),
        (near((2, row_count, chan_local), F32), near((3, chan_local), F32)),
        ints=ints,
    )(gated_own, gated_oth, near_own, near_oth, w_expand, bias_row)
    got_three = share_clip(sent_three)

    from_side = swap(to_side, 2)
    from_pair = swap(from_side, 1)


    logit_pair = jnp.concatenate(own_first(logit_grad, core_index, 1, 0))
    grad_pooled = dot32(logit_pair, w_classes, ((1,), (1,))) * count_scale[:, None]
    output, grad_resid, pooled, sent_back = call(
        functools.partial(finish, seg_count),
        (
            Early((2, row_count, chan_local), BF16, 2),
            near((2, row_count, chan_local), F32),
            near((2, chan_local), F32),
            near((2, chan_local), F32),
        ),
        deps=(from_side,),
        ints=ints,
        floats=floats,
    )(
        got_three, gain_three[None], shift_three[None], grad_pooled,
        Pick(act_three, 0), x_own, grad_own, Pick(act_three, 1), x_oth, grad_oth,
    )
    got_back = share_clip(sent_back)
    pooled = pooled.array.astype(BF16)

    def back_call(clip):
        outs = [near((row_count, chan_local), BF16)]
        if clip == 0:
            outs += [near((row_count, half), F32)] * 2
        else:
            outs += [near((row_count, mid_width), BF16)]
        return call(
            functools.partial(expand_backward, seg_count, clip), tuple(outs), ints=ints, floats=floats,
        )(got_three, got_back, gain_three[None], Pick(grad_resid, clip), Pick(act_three, clip), w_expand)

    low_three_oth, back_oth = back_call(1)
    near_back = swap(back_oth, 1)
    low_three_own, back_own, back_far = back_call(0)

    unit = 16 * clip_size
    def halves(rows, width):
        return (sds((rows // 2, width), BF16),) * 2

    def to_places(blocks):
        if places > 4:
            order = place ^ jnp.arange(places)
            sent = jnp.stack([block.array if isinstance(block, (Free, Near)) else block for block in blocks])[order]
            return list(lax.all_to_all(sent, "clip", 0, 0, axis_index_groups=groups)[order])
        return [blocks[0]] + [swap_clip(blocks[bits], 2 * bits) for bits in range(1, places)]

    def blocks_of(rows, width):
        return (sds((rows // places, width), BF16),) * places

    grad_classes = dot32(logit_pair, pooled, ((0,), (0,)))
    wide_rows = -(-(mid_width + class_count) // unit) * unit
    wide_keep, wide_send = call(
        expand_gradient, halves(wide_rows, chan_local), [pltpu.VMEM((wide_rows, chan_local), BF16)], ints=ints,
    )(gated_own, gated_oth, near_own, near_oth, low_three_own, low_three_oth, grad_classes)

    far_back = swap(call(add_low, near_low_half, deps=())(near_back, back_far), 2)
    grad_bias = got_three[2, :class_count]
    wide_blocks = call(
        sum_blocks,
        blocks_of(wide_rows // 2, chan_local),
        [pltpu.VMEM((wide_rows // 2, chan_local), BF16)],
        deps=(grad_bias,),
        ints=ints,
    )(wide_keep, swap_clip(wide_send, 1))
    wide_got = to_places(wide_blocks)

    w_back = call(
        join_back, sds((3, 3 * mid_width, half), BF16), deps=(wide_send,), ints=ints,
    )(w_fwd, from_side, from_pair)

    logits_part = jnp.concatenate(own_first(dot32(pooled, w_classes), core_index, 1, 0))
    logits_wide = jnp.pad(logits_part, ((0, 0), (0, half - class_count)))
    slope_two, sent_back_two, kern_grad = call(
        functools.partial(gate_backward, seg_count),
        (half_low, sds((everyone, 4, half), F32), sds((32, half), F32)),
        [
            pltpu.VMEM((edge_rows, LANES), F32),
            pltpu.VMEM((edge_rows, LANES), F32),
            pltpu.VMEM((row_count + 8, LANES), F32),
        ],
        deps=(w_back,),
        ints=ints,
        floats=floats,
    )(back_own, near_back, far_back, hid_two, gate, act_two, got_two, small_own, logits_wide)
    slope_two_oth = swap(slope_two, 2)
    got_back_two = share_all(sent_back_two)
    field_rows = ((span + 32) // 48 * 16,) * 2
    field_rows += (span + 32 - sum(field_rows),)
    slope_one_low, sent_back_one, field_keep, *field_send = call(
        functools.partial(conv_backward, seg_count),
        (half_low, sums_shape, sds((span + 32, mid_local), BF16))
        + tuple(sds((rows, mid_local), BF16) for rows in field_rows),
        [
            pltpu.VMEM((span, half), BF16),
            pltpu.VMEM((pad_rows, 3 * mid_width), BF16),
            pltpu.VMEM((span, half), F32),
        ],
        deps=(wide_blocks[0], near_hid),
        ints=ints,
        floats=floats,
    )(
        slope_two, slope_two_oth, act_two, act_two_oth.array, got_two, got_back_two, act_one, got_one,
        small_own, small_oth, w_back, kern_grad,
    )
    slope_one_oth = swap(slope_one_low, 2)
    got_back_one = share_all(sent_back_one)

    pack_rows = -(-(9 * mid_width + 32) // unit) * unit
    wide_part = call(sum_parts, sds((wide_rows // clip_size, chan_local), BF16), deps=(sent_back_one,))(*wide_got)
    pack_keep, pack_pair = call(
        functools.partial(taps_gradient, seg_count),
        halves(pack_rows, mid_local),
        [pltpu.VMEM((pad_rows, 3 * mid_width), BF16)]
        + [pltpu.VMEM((3 * mid_width, pad_rows), BF16)] * 2
        + [pltpu.VMEM((pack_rows, mid_local), BF16)],
        deps=(wide_part,),
        ints=ints,
        room=40 * 1024 * 1024,
    )(hid_one, field_keep, near_hid, *[swap(each, 1) for each in field_send])


    low_pair = call(
        functools.partial(last_norm, seg_count),
        (half_low,) * 2,
        deps=(pack_pair,),
        ints=ints,
        floats=floats,
    )(slope_one_low, slope_one_oth, act_one, act_one_oth.array, got_one, got_back_one, small_own, small_oth)
    near_pair = [swap(low, 1) for low in low_pair]
    pack_other = swap_clip(pack_pair, 1)
    reduce_keep, reduce_send = call(
        reduce_gradient,
        (sds((chan_local // 2, mid_width), BF16), Loose((chan_local // 2, mid_width), BF16)),
        [pltpu.VMEM((chan_local, mid_width), BF16)],
        ints=ints,
    )(x_own, *low_pair, x_oth, *near_pair)

    share = chan_local // clip_size
    loose_blocks = (sds((pack_rows // clip_size, mid_local), BF16),) * places
    pack_blocks = call(
        sum_blocks,
        loose_blocks,
        [pltpu.VMEM((pack_rows // 2, mid_local), BF16)],
        deps=(reduce_send,),
        ints=ints,
    )(pack_keep, Free(pack_other))
    pack_got = to_places(pack_blocks)
    wide_join = call(
        join_places, sds((wide_rows // 2, chan_local), BF16), deps=(pack_blocks[0],), ints=ints,
    )(*[Free(each) for each in to_places([wide_part] * places)])
    wide_other = swap_clip(wide_join, 1)
    reduce_got = swap_clip(reduce_send, 1)
    part_rows = pack_rows // clip_size
    parts = call(
        functools.partial(stage_two, places),
        (Loose((part_rows + chan_size * share, mid_local), BF16),) * places,
        [pltpu.VMEM((chan_local // 2, mid_width), F32)],
        deps=(wide_join,),
        ints=ints,
    )(reduce_keep, Free(reduce_got), *[Free(each) if index else each for index, each in enumerate(pack_got)])
    parts_got = to_places(parts)
    grad_frames = call(
        input_gradient, sds((2, row_count, chan_local), F32), deps=(parts[0],), ints=ints,
    )(*low_pair, w_own_side, w_oth_side, grad_resid, *near_pair)
    pack_join, columns = call(
        functools.partial(stage_three, places, part_rows),
        (Loose((pack_rows // 2, mid_local), BF16), sds((everyone, share, mid_local), BF16)),
        deps=(wide_other, grad_frames),
        ints=ints,
    )(*[Free(each) if index else each for index, each in enumerate(parts_got)])
    pack_other = swap_clip(pack_join, 1)
    reduce_got = lax.all_to_all(columns, ("clip", "chan"), 0, 0)
    reduce_got = reduce_got.reshape(places, 2, chan_size, share, mid_local).transpose(2, 1, 0, 3, 4)
    grad_w_reduce = reduce_got.reshape(chan_size * chan_local, mid_local).astype(F32)
    grad_w_expand, classes_got = call(
        unpack_wide,
        (sds((mid_width, chan_local), F32), sds((wide_rows - mid_width, chan_local), F32)),
        [pltpu.VMEM((wide_rows, chan_local), BF16)],
        deps=(pack_join,),
        ints=ints,
    )(wide_join, Free(wide_other))
    grad_w_classes = classes_got[:class_count].T
    grad_spatial, grad_near, grad_far = call(
        unpack_spatial,
        (sds((9, mid_width, mid_local), F32),) + (sds((9, mid_local), F32),) * 2,
        [pltpu.VMEM((pack_rows, mid_local), BF16)],
        ints=ints,
    )(pack_join, Free(pack_other))

    mine = lax.dynamic_index_in_dim(got_back_two.array, clip_index, 0, keepdims=False)
    logits = jnp.sum(mine, axis=0)[2:, :class_count] + class_bias

    def own_sums(got):
        got = got.array
        sums = jnp.sum(got.reshape((clip_size, 2, 2) + got.shape[2:]), axis=(0, 2))
        sums = lax.dynamic_index_in_dim(sums, side_index, 0, keepdims=False)
        return lax.dynamic_slice_in_dim(sums[:2], core_index * mid_local, mid_local, 1)

    grads_one = own_sums(got_back_one)
    grads_two = own_sums(got_back_two)
    grads_three = got_back

    def whole(array):
        return array.reshape(2, pixel_count, seg_count, chan_local).transpose(0, 2, 1, 3)

    return (
        whole(output),
        logits,
        whole(grad_frames),
        grad_w_reduce,
        grads_one[1],
        grads_one[0],
        grad_spatial,
        grads_two[1],
        grads_two[0],
        grad_near,
        grad_far,
        grad_w_expand,
        grads_three[1],
        grads_three[0],
        grad_w_classes,
        grad_bias,
    )


def solution(mesh):
    in_specs = (
        P("clip", None, None, "chan"),
        P(),
        P(None, "chan"),
        P("chan"),
        P("chan"),
        P(None, None, "chan"),
        P("chan"),
        P("chan"),
        P(None, "chan"),
        P(None, "chan"),
        P(None, "chan"),
        P("chan"),
        P("chan"),
        P("chan", None),
        P(),
        P("clip", None, None, "chan"),
        P("clip", None),
    )
    out_specs = (
        P("clip", None, None, "chan"),
        P("clip", None),
        P("clip", None, None, "chan"),
        P(None, "chan"),
        P("chan"),
        P("chan"),
        P(None, None, "chan"),
        P("chan"),
        P("chan"),
        P(None, "chan"),
        P(None, "chan"),
        P(None, "chan"),
        P("chan"),
        P("chan"),
        P("chan", None),
        P(),
    )
    body = functools.partial(per_device, mesh.shape["clip"], mesh.shape["chan"])
    return jax.shard_map(
        body, mesh=mesh, in_specs=in_specs, out_specs=out_specs, check_vma=False
    )
```
